256 devices in a mesh: tm: 64 (over z, x, core), depth: 4 (over y).
Axes of the slice: x: 4, y: 4, z: 8, core: 2. Of those that a mesh axis runs over, the one named last changes fastest.
Arguments:
- iq: bfloat16 [2, 384, 192, 512], P(None, 'tm', 'depth')
- half: int32 [192], P('depth'), may hold values from 1 to 8, as said below
- weights: int32 [6], replicated, may hold values from 1 to 4
Outputs:
- displacement: float32 [384, 192, 512], P('tm', 'depth')
The draws below stay inside these ranges and needn't reach their ends.
Inputs may be any that keep to these rules, and one draw needn't show every extreme that they name: `half`: every value is reached at some depth.
All inputs are finite; a program needn't handle non-finite values.
Results may differ from the reference program's by a relative error of at most 0.00035.
Values may be sent and summed in bfloat16 or wider, within the bound.
A program may use at most 64 MiB of HBM per device.

```python
import math
import jax
import jax.numpy as jnp
from jax import lax

LINES = 512
LAGS = 6
HMAX = 8
FRAMES = 384
DEPTH = 192


def draw_iq(key, part):
    key = jax.random.fold_in(key, 11)
    key_rate, key_noise, key_amp = jax.random.split(key, 3)
    times = jnp.arange(FRAMES, dtype=jnp.float32)[:, None, None]
    rate = jax.random.uniform(key_rate, (DEPTH, LINES), jnp.float32, -0.15, 0.15)
    noise = jax.random.uniform(key_noise, (FRAMES, DEPTH, LINES), jnp.float32, -0.3, 0.3)
    amp = jnp.exp(jax.random.uniform(key_amp, (FRAMES, DEPTH, LINES), jnp.float32, math.log(0.3), math.log(3.0)))
    angle = times * rate + noise
    return jnp.stack([amp * jnp.cos(angle), amp * jnp.sin(angle)]).astype(jnp.bfloat16)


def draw_half(key, part):
    key = jax.random.fold_in(key, 23)
    drawn = jax.random.randint(key, (DEPTH,), 1, HMAX + 1)
    spots = jnp.arange(DEPTH)
    drawn = jnp.where(spots == 0, HMAX, drawn)
    return jnp.where(spots == 1, 1, drawn).astype(jnp.int32)


def with_ends(array, key, low, high):
    longest = array.shape.index(max(array.shape))
    spots = []
    for shift in (0, 1):
        where = [jax.random.randint(jax.random.fold_in(key, axis), (), 0, length) for axis, length in enumerate(array.shape)]
        where[longest] = (where[longest] + shift) % array.shape[longest]
        spots.append(tuple(where))
    return array.at[spots[0]].set(low).at[spots[1]].set(high)


def setup_inputs(seed: int = 0) -> dict:
    streams_of = jax.random.split(jax.random.key(seed), 4)
    iq = draw_iq(jax.random.fold_in(streams_of[3], 71), 0)
    half = draw_half(jax.random.fold_in(streams_of[3], 71), 0)
    weights = with_ends(jax.random.randint(streams_of[2], (LAGS,), 1, 5), jax.random.fold_in(streams_of[2], 1), 1, 4).astype(jnp.int32)
    return dict(iq=iq, half=half, weights=weights)


def window(field, half):
    depth_count = field.shape[0]
    padded = jnp.pad(field, ((HMAX, HMAX), (0, 0)))
    total = jnp.zeros_like(field)
    for offset in range(-HMAX, HMAX + 1):
        keep = (jnp.abs(offset) <= half)[:, None]
        total = total + jnp.where(keep, padded[HMAX + offset:HMAX + offset + depth_count], jnp.float32(0.0))
    return total


def pair_phase(later, earlier, half):
    real_part = later[0] * earlier[0] + later[1] * earlier[1]
    imag_part = later[1] * earlier[0] - later[0] * earlier[1]
    return jnp.arctan2(window(imag_part, half), window(real_part, half))


def reference(iq, half, weights):
    wide = iq.astype(jnp.float32)
    frame_ids = jnp.arange(FRAMES)
    numer = jnp.zeros((FRAMES, DEPTH, LINES), jnp.float32)
    denom = jnp.zeros((FRAMES,), jnp.float32)
    for lag in range(1, LAGS + 1):
        weight = weights[lag - 1].astype(jnp.float32)

        def one_frame(start):
            later_id = jnp.minimum(start + lag, FRAMES - 1).astype(jnp.int32)
            later = lax.dynamic_index_in_dim(wide, later_id, 1, keepdims=False)
            earlier = lax.dynamic_index_in_dim(wide, start.astype(jnp.int32), 1, keepdims=False)
            return pair_phase(later, earlier, half)

        phase = lax.map(one_frame, frame_ids.astype(jnp.int32))
        valid = (frame_ids + lag < FRAMES)[:, None, None]
        numer = numer + weight * jnp.where(valid, phase, jnp.float32(0.0))
        numer = numer.at[lag:].add(weight * phase[:FRAMES - lag])
        denom = denom + weight * ((frame_ids + lag < FRAMES).astype(jnp.float32) + (frame_ids - lag >= 0).astype(jnp.float32))
    return numer / denom[:, None, None]
```

```python
import functools

import jax
import jax.numpy as jnp
import numpy as np
from jax import lax
from jax.experimental import pallas as pl
from jax.experimental.pallas import tpu as pltpu
from jax.sharding import PartitionSpec as P

LAGS = 6
HMAX = 8
HALF_PI = float(np.float32(np.pi / 2))
PI = float(np.float32(np.pi))
TINY = 1.1754944e-38
ATAN = (
    0.9999960660934448,
    -0.33301785588264465,
    0.19582265615463257,
    -0.12176322191953659,
    0.05807745084166527,
    -0.0137208616361022,
)
MESH = pl.DeviceIdType.MESH
UNITS = 6
STEPS = 12
HEAD = 4
EDGE_STEPS = 7


def at_least(value, bound):
    return (value >= bound).astype(jnp.int32)


def signed_phase(y, x, weight):
    ax = jnp.abs(x)
    ay = jnp.abs(y)
    high = jnp.maximum(jnp.maximum(ax, ay), TINY)
    t = jnp.minimum(ax, ay) * pltpu.reciprocal(high, approx=True)
    s = t * t
    poly = ATAN[-1] * s + ATAN[-2]
    for coefficient in ATAN[-3::-1]:
        poly = poly * s + coefficient
    angle = poly * t
    angle = jnp.where(ay > ax, HALF_PI - angle, angle)
    angle = jnp.where(x < 0, PI - angle, angle)
    return angle * jnp.where(y < 0, -weight, weight)


def kernel(
    iq_any, half, weights, out,
    own16, edge_out, edge_in, near16, near_edge, field, total, sums, band, back,
    load_sem, edge_send, edge_recv, near_send, near_recv, far_send, far_recv, back_send, back_recv,
):
    frames, depth, lines = own16.shape[1:]
    strip = lines // 2
    rows = depth + 2 * HMAX
    me, level = lax.axis_index("tm"), lax.axis_index("depth")
    blocks, slabs = lax.axis_size("tm"), lax.axis_size("depth")
    left, right = lax.rem(me + blocks - 1, blocks), lax.rem(me + 1, blocks)
    below, above = lax.rem(level + slabs - 1, slabs), lax.rem(level + 1, slabs)
    slow = lax.rem(me, 2)

    load = pltpu.make_async_copy(iq_any, own16, load_sem)
    load.start()
    barrier = pltpu.get_barrier_semaphore()
    for target in ((left, level), (right, level), (me, below), (me, above)):
        pl.semaphore_signal(barrier, inc=1, device_id=target, device_id_type=MESH)
    load.wait()

    def scale_frame(f, carry):
        for c in range(2):
            value = own16[c, f] * jnp.bfloat16(0.5)
            own16[c, f] = value
            wide = value.astype(jnp.float32)
            for s in range(2):
                field[2 * f + s, c, HMAX : HMAX + depth] = wide[:, s * strip : (s + 1) * strip]
        first = [own16[c, f, 0:16].astype(jnp.float32)[:HMAX] for c in range(2)]
        last = [own16[c, f, depth - 16 : depth].astype(jnp.float32)[16 - HMAX :] for c in range(2)]
        edge_out[0, f] = jnp.concatenate(first, axis=0).astype(jnp.bfloat16)
        edge_out[1, f] = jnp.concatenate(last, axis=0).astype(jnp.bfloat16)
        return carry

    lax.fori_loop(0, frames, scale_frame, 0)
    pl.semaphore_wait(barrier, 4)

    def edge_copy(way):
        return pltpu.make_async_remote_copy(
            src_ref=edge_out.at[way],
            dst_ref=edge_in.at[1 - way],
            send_sem=edge_send.at[way],
            recv_sem=edge_recv.at[1 - way],
            device_id=(me, below if way == 0 else above),
            device_id_type=MESH,
        )

    def near_copy(side, j):
        frame = j if side == 0 else frames - 1 - j
        return pltpu.make_async_remote_copy(
            src_ref=own16.at[:, frame, :, pl.ds(side * strip, strip)],
            dst_ref=near16.at[1 - side, j],
            send_sem=near_send.at[side, j],
            recv_sem=near_recv.at[1 - side, j],
            device_id=(left if side == 0 else right, level),
            device_id_type=MESH,
        )

    def far_copy(side):
        return pltpu.make_async_remote_copy(
            src_ref=edge_in.at[:, :, :, pl.ds(side * strip, strip)],
            dst_ref=near_edge.at[1 - side],
            send_sem=far_send.at[side],
            recv_sem=far_recv.at[1 - side],
            device_id=(left if side == 0 else right, level),
            device_id_type=MESH,
        )

    def back_copy(side, j):
        return pltpu.make_async_remote_copy(
            src_ref=total.at[2 * frames + frames * side + j],
            dst_ref=back.at[1 - side, j],
            send_sem=back_send.at[side, j],
            recv_sem=back_recv.at[1 - side, j],
            device_id=(lax.rem(me + blocks - 1 + 2 * side, blocks), level),
            device_id_type=MESH,
        )

    for way in range(2):
        edge_copy(way).start()
    for j in range(frames):
        for side in range(2):
            near_copy(side, j).start()

    column = lax.broadcasted_iota(jnp.int32, (1, 4 * rows), 1)
    place = lax.rem(column, rows) - HMAX
    upper = column < 2 * rows
    for z in range(depth):
        keep = jnp.abs(place - z) <= half[z]
        band[z : z + 1] = jnp.where(keep & upper, 1.0, 0.0)
        band[depth + z : depth + z + 1] = jnp.where(keep & jnp.logical_not(upper), 1.0, 0.0)
    window = band[...].astype(jnp.bfloat16)
    total[...] = jnp.zeros_like(total)
    sums[...] = jnp.zeros_like(sums)

    low_factor = jnp.where(level > 0, 1.0, 0.0)
    high_factor = jnp.where(level < slabs - 1, 1.0, 0.0)

    def put_edges(slot, low, high):
        low = low.astype(jnp.float32) * low_factor
        high = high.astype(jnp.float32) * high_factor
        for c in range(2):
            field[slot, c, 0:HMAX] = low[c * HMAX : (c + 1) * HMAX]
            field[slot, c, HMAX + depth : rows] = high[c * HMAX : (c + 1) * HMAX]

    for way in range(2):
        edge_copy(way).wait_recv()
    for side in range(2):
        far_copy(side).start()

    def own_edges(f, carry):
        for s in range(2):
            cut = pl.ds(s * strip, strip)
            put_edges(2 * f + s, edge_in[0, f, :, cut], edge_in[1, f, :, cut])
        return carry

    lax.fori_loop(0, frames, own_edges, 0)

    left_valid = jnp.where(me > 0, 1.0, 0.0)
    right_valid = jnp.where(me < blocks - 1, 1.0, 0.0)

    def wait_far(side):
        pltpu.make_async_remote_copy(
            src_ref=edge_in.at[:, :, :, pl.ds(0, strip)],
            dst_ref=near_edge.at[side],
            send_sem=far_send.at[side],
            recv_sem=far_recv.at[side],
            device_id=(left, level),
            device_id_type=MESH,
        ).wait_recv()

    def take_near(side, j):
        pltpu.make_async_remote_copy(
            src_ref=own16.at[:, 0, :, pl.ds(0, strip)],
            dst_ref=near16.at[side, j],
            send_sem=near_send.at[side, j],
            recv_sem=near_recv.at[side, j],
            device_id=(left, level),
            device_id_type=MESH,
        ).wait_recv()
        slot = 2 * frames + frames * side + j
        for c in range(2):
            field[slot, c, HMAX : HMAX + depth] = near16[side, j, c].astype(jnp.float32)
        frame = frames - 1 - j + side * (2 * j - frames + 1)
        put_edges(slot, near_edge[side, 0, frame], near_edge[side, 1, frame])

    def unit(n, q):
        inner = 1 - at_least(n, HEAD) + at_least(n, HEAD + EDGE_STEPS)
        nb = n - EDGE_STEPS * at_least(n, HEAD + EDGE_STEPS)
        row = q // 2
        if row == 0:
            first, last = 0, 1 + nb
        elif row == 1:
            fold = at_least(nb, 4)
            first, last = 1 + 3 * fold, 2 + nb - fold
        else:
            fold = at_least(nb, 3)
            first, last = 2 + fold, 3 + nb - 2 * fold
        v = (n - HEAD) * UNITS + q
        second = at_least(v, 21)
        v = v - 21 * second
        side = slow + second * (1 - 2 * slow)
        j = sum(at_least(v, bound) for bound in (6, 11, 15, 18, 20))
        e = v - (6 * j - (j * (j - 1)) // 2)
        mine = 2 * (e + side * (frames - 1 - 2 * e)) + 1 - side
        theirs = 2 * frames + frames * side + j
        early = theirs + side * (mine - theirs)
        late = mine + side * (theirs - mine)
        is_inner = inner > 0
        early = jnp.where(is_inner, 2 * first + q % 2, early)
        late = jnp.where(is_inner, 2 * last + q % 2, late)
        lag = jnp.where(is_inner, last - first, 1 + j + e)
        valid = jnp.where(is_inner, 1.0, jnp.where(side > 0, right_valid, left_valid))
        weight = weights[lag - 1].astype(jnp.float32) * valid
        return early, late, weight

    def windowed(early, late):
        ar, ai = field[early, 0], field[early, 1]
        br, bi = field[late, 0], field[late, 1]
        parts = []
        for value in (br * ar + bi * ai, bi * ar - br * ai):
            high = value.astype(jnp.bfloat16)
            low = (value - high.astype(jnp.float32)).astype(jnp.bfloat16)
            parts += [high, low]
        return jnp.dot(window, jnp.concatenate(parts, axis=0), preferred_element_type=jnp.float32)

    def finish(q, early, late, weight):
        for g in range(0, depth, 24):
            part = pl.ds(g, 24)
            phase = signed_phase(sums[q, pl.ds(depth + g, 24)], sums[q, part], weight)
            total[early, part] = total[early, part] + phase
            total[late, part] = total[late, part] + phase

    def step(n, carry):
        near = n - HEAD

        @pl.when(near == 0)
        def _():
            wait_far(slow)
            take_near(slow, 0)

        @pl.when(near == 1)
        def _():
            take_near(slow, 1)
            take_near(slow, 2)

        @pl.when(near == 2)
        def _():
            take_near(slow, 3)

        @pl.when(near == 3)
        def _():
            take_near(slow, 4)
            take_near(slow, 5)
            wait_far(1 - slow)
            take_near(1 - slow, 0)

        @pl.when(near == 4)
        def _():
            take_near(1 - slow, 1)

        @pl.when(near == 5)
        def _():
            take_near(1 - slow, 2)

        @pl.when(near == 6)
        def _():
            take_near(1 - slow, 3)
            take_near(1 - slow, 4)
            take_near(1 - slow, 5)

        before = jnp.maximum(n - 1, 0)
        started = jnp.where(n > 0, 1.0, 0.0)
        for q in range(UNITS):
            early, late, _ = unit(n, q)
            result = windowed(early, late)
            early, late, weight = unit(before, q)
            finish(q, early, late, weight * started)
            sums[q] = result

        @pl.when(near == 1)
        def _():
            back_copy(slow, 0).start()

        @pl.when(near == 2)
        def _():
            back_copy(slow, 1).start()

        @pl.when(near == 3)
        def _():
            back_copy(slow, 2).start()
            back_copy(slow, 3).start()

        @pl.when(near == 4)
        def _():
            back_copy(slow, 4).start()
            back_copy(slow, 5).start()

        @pl.when(near == 5)
        def _():
            back_copy(1 - slow, 0).start()

        @pl.when(near == 6)
        def _():
            back_copy(1 - slow, 1).start()
            back_copy(1 - slow, 2).start()

        @pl.when(near == 7)
        def _():
            back_copy(1 - slow, 3).start()
            back_copy(1 - slow, 4).start()
            back_copy(1 - slow, 5).start()

        return carry

    lax.fori_loop(0, STEPS, step, 0)
    for q in range(UNITS):
        early, late, weight = unit(jnp.int32(STEPS - 1), q)
        finish(q, early, late, weight)

    for way in range(2):
        edge_copy(way).wait_send()
    for side in range(2):
        far_copy(side).wait_send()
        for j in range(frames):
            near_copy(side, j).wait_send()
            back_copy(side, j).wait()

    frame_total = frames * blocks
    for f in range(frames):
        now = me * frames + f
        norm = jnp.float32(0.0)
        for lag in range(1, LAGS + 1):
            count = jnp.where(now + lag < frame_total, 1.0, 0.0) + jnp.where(now - lag >= 0, 1.0, 0.0)
            norm = norm + weights[lag - 1].astype(jnp.float32) * count
        inverse = 1.0 / jnp.full((8, strip), norm, jnp.float32)
        for g in range(0, depth, 8):
            part = pl.ds(g, 8)
            out[f, part, 0:strip] = (total[2 * f, part] + back[0, f, part]) * inverse
            out[f, part, strip:lines] = (total[2 * f + 1, part] + back[1, frames - 1 - f, part]) * inverse


def shards(iq, half, weights):
    _, frames, depth, lines = iq.shape
    strip = lines // 2
    rows = depth + 2 * HMAX
    slots = 4 * frames
    dma = pltpu.SemaphoreType.DMA
    return pl.pallas_call(
        kernel,
        out_shape=jax.ShapeDtypeStruct((frames, depth, lines), jnp.float32),
        in_specs=[
            pl.BlockSpec(memory_space=pl.ANY),
            pl.BlockSpec(memory_space=pltpu.SMEM),
            pl.BlockSpec(memory_space=pltpu.SMEM),
        ],
        out_specs=pl.BlockSpec(memory_space=pltpu.VMEM),
        scratch_shapes=[
            pltpu.VMEM((2, frames, depth, lines), jnp.bfloat16),
            pltpu.VMEM((2, frames, 2 * HMAX, lines), jnp.bfloat16),
            pltpu.VMEM((2, frames, 2 * HMAX, lines), jnp.bfloat16),
            pltpu.VMEM((2, frames, 2, depth, strip), jnp.bfloat16),
            pltpu.VMEM((2, 2, frames, 2 * HMAX, strip), jnp.bfloat16),
            pltpu.VMEM((slots, 2, rows, strip), jnp.float32),
            pltpu.VMEM((slots, depth, strip), jnp.float32),
            pltpu.VMEM((UNITS, 2 * depth, strip), jnp.float32),
            pltpu.VMEM((2 * depth, 4 * rows), jnp.float32),
            pltpu.VMEM((2, frames, depth, strip), jnp.float32),
            dma(()),
            dma((2,)),
            dma((2,)),
            dma((2, frames)),
            dma((2, frames)),
            dma((2,)),
            dma((2,)),
            dma((2, frames)),
            dma((2, frames)),
        ],
        compiler_params=pltpu.CompilerParams(
            collective_id=0, has_side_effects=True, vmem_limit_bytes=32 * 1024 * 1024
        ),
        name="pair_phases",
    )(iq, half, weights)


def solution(mesh):
    placed = (P(None, "tm", "depth", None), P("depth"), P())
    return jax.shard_map(
        shards, mesh=mesh, in_specs=placed, out_specs=P("tm", "depth", None), check_vma=False
    )
```

```python
import functools

import jax
import jax.numpy as jnp
import numpy as np
from jax import lax
from jax.experimental import pallas as pl
from jax.experimental.pallas import tpu as pltpu
from jax.sharding import PartitionSpec as P

LAGS = 6
HMAX = 8
HALF_PI = float(np.float32(np.pi / 2))
PI = float(np.float32(np.pi))
TINY = 1.1754944e-38
ATAN = (
    0.9999960660934448,
    -0.33301785588264465,
    0.19582265615463257,
    -0.12176322191953659,
    0.05807745084166527,
    -0.0137208616361022,
)
MESH = pl.DeviceIdType.MESH
UNITS = 6
STEPS = 12
HEAD = 1
EDGE_STEPS = 7


def at_least(value, bound):
    return (value >= bound).astype(jnp.int32)


def signed_phase(y, x, weight):
    ax = jnp.abs(x)
    ay = jnp.abs(y)
    high = jnp.maximum(jnp.maximum(ax, ay), TINY)
    t = jnp.minimum(ax, ay) * pltpu.reciprocal(high, approx=True)
    s = t * t
    poly = ATAN[-1] * s + ATAN[-2]
    for coefficient in ATAN[-3::-1]:
        poly = poly * s + coefficient
    angle = poly * t
    angle = jnp.where(ay > ax, HALF_PI - angle, angle)
    angle = jnp.where(x < 0, PI - angle, angle)
    return angle * jnp.where(y < 0, -weight, weight)


def kernel(
    iq_any, half_any, weights_any, out,
    half, weights, own16, edge_out, edge_in, near16, near_edge, field, total, sums, band, back,
    load_sem, small_sem, edge_send, edge_recv, near_send, near_recv, far_send, far_recv, back_send, back_recv,
):
    frames, depth, lines = own16.shape[1:]
    strip = lines // 2
    rows = depth + 2 * HMAX
    me, level = lax.axis_index("tm"), lax.axis_index("depth")
    blocks, slabs = lax.axis_size("tm"), lax.axis_size("depth")
    left, right = lax.rem(me + blocks - 1, blocks), lax.rem(me + 1, blocks)
    below, above = lax.rem(level + slabs - 1, slabs), lax.rem(level + 1, slabs)
    slow = lax.rem(me, 2)

    load = pltpu.make_async_copy(iq_any, own16, load_sem)
    load.start()
    small = [
        pltpu.make_async_copy(half_any, half, small_sem.at[0]),
        pltpu.make_async_copy(weights_any, weights, small_sem.at[1]),
    ]
    for copy in small:
        copy.start()
    beside = (me > 0, me < blocks - 1)
    barrier = pltpu.get_barrier_semaphore()
    for other in (below, above):
        pl.semaphore_signal(barrier, inc=1, device_id=(me, other), device_id_type=MESH)
    for side, column in enumerate((left, right)):

        @pl.when(beside[side])
        def _(column=column):
            for other in (level, below, above):
                pl.semaphore_signal(barrier, inc=1, device_id=(column, other), device_id_type=MESH)

    load.wait()

    def scale_frame(f, carry):
        for c in range(2):
            value = own16[c, f] * jnp.bfloat16(0.5)
            own16[c, f] = value
            wide = value.astype(jnp.float32)
            for s in range(2):
                field[2 * f + s, c, HMAX : HMAX + depth] = wide[:, s * strip : (s + 1) * strip]
        first = [own16[c, f, 0:16].astype(jnp.float32)[:HMAX] for c in range(2)]
        last = [own16[c, f, depth - 16 : depth].astype(jnp.float32)[16 - HMAX :] for c in range(2)]
        edge_out[0, f] = jnp.concatenate(first, axis=0).astype(jnp.bfloat16)
        edge_out[1, f] = jnp.concatenate(last, axis=0).astype(jnp.bfloat16)
        return carry

    lax.fori_loop(0, frames, scale_frame, 0)
    pl.semaphore_wait(barrier, 2 + 3 * sum(side.astype(jnp.int32) for side in beside))

    def edge_copy(way):
        return pltpu.make_async_remote_copy(
            src_ref=edge_out.at[way],
            dst_ref=edge_in.at[1 - way],
            send_sem=edge_send.at[way],
            recv_sem=edge_recv.at[1 - way],
            device_id=(me, below if way == 0 else above),
            device_id_type=MESH,
        )

    def near_copy(side, j):
        frame = j if side == 0 else frames - 1 - j
        return pltpu.make_async_remote_copy(
            src_ref=own16.at[:, frame, :, pl.ds(side * strip, strip)],
            dst_ref=near16.at[1 - side, j],
            send_sem=near_send.at[side, j],
            recv_sem=near_recv.at[1 - side, j],
            device_id=(left if side == 0 else right, level),
            device_id_type=MESH,
        )

    def far_copy(side, way):
        return pltpu.make_async_remote_copy(
            src_ref=edge_out.at[way, :, :, pl.ds(side * strip, strip)],
            dst_ref=near_edge.at[1 - side, 1 - way],
            send_sem=far_send.at[side, way],
            recv_sem=far_recv.at[1 - side, 1 - way],
            device_id=(left if side == 0 else right, below if way == 0 else above),
            device_id_type=MESH,
        )

    def back_copy(side, j):
        return pltpu.make_async_remote_copy(
            src_ref=total.at[2 * frames + frames * side + j],
            dst_ref=back.at[1 - side, j],
            send_sem=back_send.at[side, j],
            recv_sem=back_recv.at[1 - side, j],
            device_id=(lax.rem(me + blocks - 1 + 2 * side, blocks), level),
            device_id_type=MESH,
        )

    for way in range(2):
        edge_copy(way).start()
    for side in range(2):

        @pl.when(beside[side])
        def _(side=side):
            for way in range(2):
                far_copy(side, way).start()

    for j in range(frames):
        for side in range(2):

            @pl.when(beside[side])
            def _(side=side, j=j):
                near_copy(side, j).start()

    for copy in small:
        copy.wait()

    column = lax.broadcasted_iota(jnp.int32, (1, 4 * rows), 1)
    place = lax.rem(column, rows) - HMAX
    upper = column < 2 * rows
    for z in range(depth):
        keep = jnp.abs(place - z) <= half[z]
        band[z : z + 1] = jnp.where(keep & upper, 1.0, 0.0)
        band[depth + z : depth + z + 1] = jnp.where(keep & jnp.logical_not(upper), 1.0, 0.0)
    window = band[...].astype(jnp.bfloat16)
    total[...] = jnp.zeros_like(total)
    sums[...] = jnp.zeros_like(sums)
    for side in range(2):

        @pl.when(jnp.logical_not(beside[side]))
        def _(side=side):
            back[side] = jnp.zeros_like(back[side])


    low_factor = jnp.where(level > 0, 1.0, 0.0)
    high_factor = jnp.where(level < slabs - 1, 1.0, 0.0)

    def put_edges(slot, low, high):
        low = low.astype(jnp.float32) * low_factor
        high = high.astype(jnp.float32) * high_factor
        for c in range(2):
            field[slot, c, 0:HMAX] = low[c * HMAX : (c + 1) * HMAX]
            field[slot, c, HMAX + depth : rows] = high[c * HMAX : (c + 1) * HMAX]

    for way in range(2):
        edge_copy(way).wait_recv()
    def own_edges(f, carry):
        for s in range(2):
            cut = pl.ds(s * strip, strip)
            put_edges(2 * f + s, edge_in[0, f, :, cut], edge_in[1, f, :, cut])
        return carry

    lax.fori_loop(0, frames, own_edges, 0)

    left_valid = jnp.where(me > 0, 1.0, 0.0)
    right_valid = jnp.where(me < blocks - 1, 1.0, 0.0)

    def at_side(side):
        target = me - 1 + 2 * side
        return (target >= 0) & (target < blocks)

    def wait_far(side):
        @pl.when(at_side(side))
        def _():
            for way in range(2):
                pltpu.make_async_remote_copy(
                    src_ref=edge_out.at[way, :, :, pl.ds(0, strip)],
                    dst_ref=near_edge.at[side, way],
                    send_sem=far_send.at[side, way],
                    recv_sem=far_recv.at[side, way],
                    device_id=(left, level),
                    device_id_type=MESH,
                ).wait_recv()

    def take_near(side, j):
        slot = 2 * frames + frames * side + j

        @pl.when(at_side(side))
        def _():
            pltpu.make_async_remote_copy(
                src_ref=own16.at[:, 0, :, pl.ds(0, strip)],
                dst_ref=near16.at[side, j],
                send_sem=near_send.at[side, j],
                recv_sem=near_recv.at[side, j],
                device_id=(left, level),
                device_id_type=MESH,
            ).wait_recv()
            for c in range(2):
                field[slot, c, HMAX : HMAX + depth] = near16[side, j, c].astype(jnp.float32)
            frame = frames - 1 - j + side * (2 * j - frames + 1)
            put_edges(slot, near_edge[side, 0, frame], near_edge[side, 1, frame])

        @pl.when(jnp.logical_not(at_side(side)))
        def _():
            field[slot] = jnp.zeros_like(field[slot])

    def send_back(side, j):
        @pl.when(at_side(side))
        def _():
            back_copy(side, j).start()

    def unit(n, q):
        inner = 1 - at_least(n, HEAD) + at_least(n, HEAD + EDGE_STEPS)
        nb = n - EDGE_STEPS * at_least(n, HEAD + EDGE_STEPS)
        row = q // 2
        if row == 0:
            first, last = 0, 1 + nb
        elif row == 1:
            fold = at_least(nb, 4)
            first, last = 1 + 3 * fold, 2 + nb - fold
        else:
            fold = at_least(nb, 3)
            first, last = 2 + fold, 3 + nb - 2 * fold
        v = (n - HEAD) * UNITS + q
        second = at_least(v, 21)
        v = v - 21 * second
        side = slow + second * (1 - 2 * slow)
        j = sum(at_least(v, bound) for bound in (6, 11, 15, 18, 20))
        e = v - (6 * j - (j * (j - 1)) // 2)
        mine = 2 * (e + side * (frames - 1 - 2 * e)) + 1 - side
        theirs = 2 * frames + frames * side + j
        early = theirs + side * (mine - theirs)
        late = mine + side * (theirs - mine)
        is_inner = inner > 0
        early = jnp.where(is_inner, 2 * first + q % 2, early)
        late = jnp.where(is_inner, 2 * last + q % 2, late)
        lag = jnp.where(is_inner, last - first, 1 + j + e)
        valid = jnp.where(is_inner, 1.0, jnp.where(side > 0, right_valid, left_valid))
        weight = weights[lag - 1].astype(jnp.float32) * valid
        return early, late, weight

    def windowed(early, late):
        ar, ai = field[early, 0], field[early, 1]
        br, bi = field[late, 0], field[late, 1]
        parts = []
        for value in (br * ar + bi * ai, bi * ar - br * ai):
            high = value.astype(jnp.bfloat16)
            low = (value - high.astype(jnp.float32)).astype(jnp.bfloat16)
            parts += [high, low]
        return jnp.dot(window, jnp.concatenate(parts, axis=0), preferred_element_type=jnp.float32)

    def finish(q, early, late, weight):
        for g in range(0, depth, 24):
            part = pl.ds(g, 24)
            phase = signed_phase(sums[q, pl.ds(depth + g, 24)], sums[q, part], weight)
            total[early, part] = total[early, part] + phase
            total[late, part] = total[late, part] + phase

    def step(n, carry):
        near = n - HEAD

        @pl.when(near == 0)
        def _():
            wait_far(slow)
            take_near(slow, 0)

        @pl.when(near == 1)
        def _():
            take_near(slow, 1)
            take_near(slow, 2)

        @pl.when(near == 2)
        def _():
            take_near(slow, 3)

        @pl.when(near == 3)
        def _():
            take_near(slow, 4)
            take_near(slow, 5)
            wait_far(1 - slow)
            take_near(1 - slow, 0)

        @pl.when(near == 4)
        def _():
            take_near(1 - slow, 1)

        @pl.when(near == 5)
        def _():
            take_near(1 - slow, 2)

        @pl.when(near == 6)
        def _():
            take_near(1 - slow, 3)
            take_near(1 - slow, 4)
            take_near(1 - slow, 5)

        before = jnp.maximum(n - 1, 0)
        started = jnp.where(n > 0, 1.0, 0.0)
        for q in range(UNITS):
            early, late, _ = unit(n, q)
            result = windowed(early, late)
            early, late, weight = unit(before, q)
            finish(q, early, late, weight * started)
            sums[q] = result

        @pl.when(near == 1)
        def _():
            send_back(slow, 0)

        @pl.when(near == 2)
        def _():
            send_back(slow, 1)

        @pl.when(near == 3)
        def _():
            send_back(slow, 2)
            send_back(slow, 3)

        @pl.when(near == 4)
        def _():
            send_back(slow, 4)
            send_back(slow, 5)

        @pl.when(near == 5)
        def _():
            send_back(1 - slow, 0)

        @pl.when(near == 6)
        def _():
            send_back(1 - slow, 1)
            send_back(1 - slow, 2)

        @pl.when(near == 7)
        def _():
            send_back(1 - slow, 3)
            send_back(1 - slow, 4)
            send_back(1 - slow, 5)

        return carry

    lax.fori_loop(0, STEPS, step, 0)
    for q in range(UNITS):
        early, late, weight = unit(jnp.int32(STEPS - 1), q)
        finish(q, early, late, weight)

    for way in range(2):
        edge_copy(way).wait_send()
    for side in range(2):

        @pl.when(beside[side])
        def _(side=side):
            for way in range(2):
                far_copy(side, way).wait_send()
            for j in range(frames):
                near_copy(side, j).wait_send()
                back_copy(side, j).wait_send()
                back_copy(1 - side, j).wait_recv()


    frame_total = frames * blocks
    for f in range(frames):
        now = me * frames + f
        norm = jnp.float32(0.0)
        for lag in range(1, LAGS + 1):
            count = jnp.where(now + lag < frame_total, 1.0, 0.0) + jnp.where(now - lag >= 0, 1.0, 0.0)
            norm = norm + weights[lag - 1].astype(jnp.float32) * count
        inverse = 1.0 / jnp.full((8, strip), norm, jnp.float32)
        for g in range(0, depth, 8):
            part = pl.ds(g, 8)
            out[f, part, 0:strip] = (total[2 * f, part] + back[0, f, part]) * inverse
            out[f, part, strip:lines] = (total[2 * f + 1, part] + back[1, frames - 1 - f, part]) * inverse


def shards(iq, half, weights):
    _, frames, depth, lines = iq.shape
    strip = lines // 2
    rows = depth + 2 * HMAX
    slots = 4 * frames
    dma = pltpu.SemaphoreType.DMA
    return pl.pallas_call(
        kernel,
        out_shape=pltpu.VMEM((frames, depth, lines), jnp.float32),
        in_specs=[
            pl.BlockSpec(memory_space=pltpu.HBM),
            pl.BlockSpec(memory_space=pltpu.HBM),
            pl.BlockSpec(memory_space=pltpu.HBM),
        ],
        out_specs=pl.BlockSpec(memory_space=pltpu.VMEM),
        scratch_shapes=[
            pltpu.SMEM(half.shape, jnp.int32),
            pltpu.SMEM(weights.shape, jnp.int32),
            pltpu.VMEM((2, frames, depth, lines), jnp.bfloat16),
            pltpu.VMEM((2, frames, 2 * HMAX, lines), jnp.bfloat16),
            pltpu.VMEM((2, frames, 2 * HMAX, lines), jnp.bfloat16),
            pltpu.VMEM((2, frames, 2, depth, strip), jnp.bfloat16),
            pltpu.VMEM((2, 2, frames, 2 * HMAX, strip), jnp.bfloat16),
            pltpu.VMEM((slots, 2, rows, strip), jnp.float32),
            pltpu.VMEM((slots, depth, strip), jnp.float32),
            pltpu.VMEM((UNITS, 2 * depth, strip), jnp.float32),
            pltpu.VMEM((2 * depth, 4 * rows), jnp.float32),
            pltpu.VMEM((2, frames, depth, strip), jnp.float32),
            dma(()),
            dma((2,)),
            dma((2,)),
            dma((2,)),
            dma((2, frames)),
            dma((2, frames)),
            dma((2, 2)),
            dma((2, 2)),
            dma((2, frames)),
            dma((2, frames)),
        ],
        compiler_params=pltpu.CompilerParams(
            collective_id=0, has_side_effects=True, vmem_limit_bytes=48 * 1024 * 1024
        ),
        name="pair_phases",
    )(*(pltpu.with_memory_space_constraint(x, pltpu.HBM) for x in (iq, half, weights)))


def solution(mesh):
    placed = (P(None, "tm", "depth", None), P("depth"), P())
    return jax.shard_map(
        shards, mesh=mesh, in_specs=placed, out_specs=P("tm", "depth", None), check_vma=False
    )
```

```python
import functools

import jax
import jax.numpy as jnp
import numpy as np
from jax import lax
from jax.experimental import pallas as pl
from jax.experimental.pallas import tpu as pltpu
from jax.sharding import PartitionSpec as P

LAGS = 6
HMAX = 8
HALF_PI = float(np.float32(np.pi / 2))
PI = float(np.float32(np.pi))
TINY = 1.1754944e-38
ATAN = (
    0.9999960660934448,
    -0.33301785588264465,
    0.19582265615463257,
    -0.12176322191953659,
    0.05807745084166527,
    -0.0137208616361022,
)
MESH = pl.DeviceIdType.MESH
UNITS = 6
INNER = 5
OUTER = 7
STEPS = INNER + OUTER
EDGE = 2 * HMAX
NEAR_GROUPS = ((0, 2), (2, 2), (4, 2))
FAR_GROUPS = ((0, 1), (1, 2), (3, 3))


def at_least(value, bound):
    return (value >= bound).astype(jnp.int32)


def signed_phase(y, x, weight):
    ax = jnp.abs(x)
    ay = jnp.abs(y)
    high = jnp.maximum(jnp.maximum(ax, ay), TINY)
    t = jnp.minimum(ax, ay) * pltpu.reciprocal(high, approx=True)
    s = t * t
    poly = ATAN[-1] * s + ATAN[-2]
    for coefficient in ATAN[-3::-1]:
        poly = poly * s + coefficient
    angle = poly * t
    angle = jnp.where(ay > ax, HALF_PI - angle, angle)
    angle = jnp.where(x < 0, PI - angle, angle)
    return angle * jnp.where(y < 0, -weight, weight)


def split_products(early, late):
    parts = []
    (ar, ai), (br, bi) = early, late
    for value in (br * ar + bi * ai, bi * ar - br * ai):
        high = value.astype(jnp.bfloat16)
        low = (value - high.astype(jnp.float32)).astype(jnp.bfloat16)
        parts += [high, low]
    return parts


def kernel(
    iq_any, half_any, weights_any, out,
    half, weights, scaled, own16, edge_out, edge_in, near16, near_edge, field, edges,
    mid_total, edge_total, mid_sums, edge_sums, held, band, edge_band, mid_back, edge_back,
    load_sem, small_sem, edge_send, edge_recv, near_send, near_recv, far_send, far_recv,
    mid_send, mid_recv, rim_send, rim_recv,
):
    frames, depth, lines = own16.shape[1:]
    strip = lines // 2
    mid = depth - EDGE
    me, level = lax.axis_index("tm"), lax.axis_index("depth")
    blocks, slabs = lax.axis_size("tm"), lax.axis_size("depth")
    left, right = lax.rem(me + blocks - 1, blocks), lax.rem(me + 1, blocks)
    below, above = lax.rem(level + slabs - 1, slabs), lax.rem(level + 1, slabs)
    slow = lax.rem(me, 2)
    quick = 1 - slow
    beside = (me > 0, me < blocks - 1)
    target = me - 1 + 2 * slow
    slow_here = (target >= 0) & (target < blocks)

    load = pltpu.make_async_copy(iq_any, own16, load_sem)
    load.start()
    small = [
        pltpu.make_async_copy(half_any, half, small_sem.at[0]),
        pltpu.make_async_copy(weights_any, weights, small_sem.at[1]),
    ]
    for copy in small:
        copy.start()
    barrier = pltpu.get_barrier_semaphore()
    for other in (below, above):
        pl.semaphore_signal(barrier, inc=1, device_id=(me, other), device_id_type=MESH)
    for side, column in enumerate((left, right)):

        @pl.when(beside[side])
        def _(column=column):
            for other in (level, below, above):
                pl.semaphore_signal(barrier, inc=1, device_id=(column, other), device_id_type=MESH)

    load.wait()

    def scale_frame(f, carry):
        first, last = [], []
        for c in range(2):
            value = own16[c, f] * jnp.bfloat16(0.5)
            own16[c, f] = value
            wide = value.astype(jnp.float32)
            for s in range(2):
                field[2 * f + s, c] = wide[:, s * strip : (s + 1) * strip]
            first.append(wide[:HMAX])
            last.append(wide[depth - HMAX :])
        edge_out[0, f] = jnp.concatenate(first, axis=0).astype(jnp.bfloat16)
        edge_out[1, f] = jnp.concatenate(last, axis=0).astype(jnp.bfloat16)
        return carry

    lax.fori_loop(0, frames, scale_frame, 0)
    pl.semaphore_wait(barrier, 2 + 3 * sum(side.astype(jnp.int32) for side in beside))

    def edge_copy(way):
        return pltpu.make_async_remote_copy(
            src_ref=edge_out.at[way],
            dst_ref=edge_in.at[1 - way],
            send_sem=edge_send.at[way],
            recv_sem=edge_recv.at[1 - way],
            device_id=(me, below if way == 0 else above),
            device_id_type=MESH,
        )

    def near_copy(side, j):
        frame = j if side == 0 else frames - 1 - j
        return pltpu.make_async_remote_copy(
            src_ref=own16.at[:, frame, :, pl.ds(side * strip, strip)],
            dst_ref=near16.at[1 - side, j],
            send_sem=near_send.at[side, j],
            recv_sem=near_recv.at[1 - side, j],
            device_id=(left if side == 0 else right, level),
            device_id_type=MESH,
        )

    def far_copy(side, way):
        return pltpu.make_async_remote_copy(
            src_ref=edge_out.at[way, :, :, pl.ds(side * strip, strip)],
            dst_ref=near_edge.at[1 - side, 1 - way],
            send_sem=far_send.at[side, way],
            recv_sem=far_recv.at[1 - side, 1 - way],
            device_id=(left if side == 0 else right, below if way == 0 else above),
            device_id_type=MESH,
        )

    def back_copy(side, group, groups, source, target, send, recv):
        first, count = groups[group]
        return pltpu.make_async_remote_copy(
            src_ref=source.at[pl.ds(2 * frames + frames * side + first, count)],
            dst_ref=target.at[1 - side, pl.ds(first, count)],
            send_sem=send.at[side, group],
            recv_sem=recv.at[1 - side, group],
            device_id=(lax.rem(me + blocks - 1 + 2 * side, blocks), level),
            device_id_type=MESH,
        )

    middle = (mid_total, mid_back, mid_send, mid_recv)
    rim = (edge_total, edge_back, rim_send, rim_recv)

    def send_quick(group, what):
        back_copy(quick, group, NEAR_GROUPS, *what).start()

    def send_slow(group, what):
        @pl.when(slow_here)
        def _():
            back_copy(slow, group, FAR_GROUPS, *what).start()

    for way in range(2):
        edge_copy(way).start()
    for j in range(frames):
        for side in range(2):

            @pl.when(beside[side])
            def _(side=side, j=j):
                near_copy(side, j).start()

    for side in range(2):

        @pl.when(beside[side])
        def _(side=side):
            for way in range(2):
                far_copy(side, way).start()

    for copy in small:
        copy.wait()
    for lag in range(LAGS):
        value = weights[lag].astype(jnp.float32)
        scaled[lag] = value
        scaled[LAGS + lag] = value * jnp.where(slow_here, 1.0, 0.0)

    column = lax.broadcasted_iota(jnp.int32, (1, 4 * depth), 1)
    place = lax.rem(column, depth)
    upper = column < 2 * depth
    for z in range(depth):
        keep = jnp.abs(place - z) <= half[z]
        band[z : z + 1] = jnp.where(keep & upper, 1.0, 0.0)
        band[depth + z : depth + z + 1] = jnp.where(keep & jnp.logical_not(upper), 1.0, 0.0)
    column = lax.broadcasted_iota(jnp.int32, (1, 12 * EDGE), 1)
    which = column // (2 * EDGE)
    place = lax.rem(column, EDGE)
    low_place = jnp.where(place < HMAX, place - HMAX, 4 * depth)
    high_place = jnp.where(place < HMAX, 4 * depth, place - HMAX + depth)
    for row in range(EDGE):
        z = row if row < HMAX else row + mid
        keep = jnp.abs((low_place if row < HMAX else high_place) - z) <= half[z]
        for block in range(6):
            at = block * EDGE + row
            edge_band[at : at + 1] = jnp.where(keep & (which == block), 1.0, 0.0)
    window = band[...].astype(jnp.bfloat16)
    mid_total[...] = jnp.zeros_like(mid_total)
    edge_total[...] = jnp.zeros_like(edge_total)
    mid_sums[...] = jnp.zeros_like(mid_sums)
    edge_sums[...] = jnp.zeros_like(edge_sums)

    @pl.when(jnp.logical_not(slow_here))
    def _():
        mid_back[slow] = jnp.zeros(mid_back.shape[1:], jnp.float32)
        edge_back[slow] = jnp.zeros(edge_back.shape[1:], jnp.float32)

    low_factor = jnp.where(level > 0, 1.0, 0.0)
    high_factor = jnp.where(level < slabs - 1, 1.0, 0.0)

    def put_edges(slot, low, high):
        low = low.astype(jnp.float32) * low_factor
        high = high.astype(jnp.float32) * high_factor
        for c in range(2):
            edges[slot, c, 0:HMAX] = low[c * HMAX : (c + 1) * HMAX]
            edges[slot, c, HMAX:EDGE] = high[c * HMAX : (c + 1) * HMAX]

    def take_near(side, j):
        pltpu.make_async_remote_copy(
            src_ref=own16.at[:, 0, :, pl.ds(0, strip)],
            dst_ref=near16.at[side, j],
            send_sem=near_send.at[side, j],
            recv_sem=near_recv.at[side, j],
            device_id=(left, level),
            device_id_type=MESH,
        ).wait_recv()
        for c in range(2):
            field[2 * frames + frames * side + j, c] = near16[side, j, c].astype(jnp.float32)

    def take_slow(*js):
        @pl.when(slow_here)
        def _():
            for j in js:
                take_near(slow, j)

        @pl.when(jnp.logical_not(slow_here))
        def _():
            for j in js:
                field[2 * frames + frames * slow + j] = jnp.zeros(field.shape[1:], jnp.float32)

    def take_far(side):
        for way in range(2):
            pltpu.make_async_remote_copy(
                src_ref=edge_out.at[way, :, :, pl.ds(0, strip)],
                dst_ref=near_edge.at[side, way],
                send_sem=far_send.at[side, way],
                recv_sem=far_recv.at[side, way],
                device_id=(left, level),
                device_id_type=MESH,
            ).wait_recv()

        def put(j, carry):
            frame = frames - 1 - j + side * (2 * j - frames + 1)
            slot = 2 * frames + frames * side + j
            put_edges(slot, near_edge[side, 0, frame], near_edge[side, 1, frame])
            return carry

        lax.fori_loop(0, frames, put, 0)

    def unit(n, q):
        inner = n < INNER
        row = q // 2
        if row == 0:
            first, last = 0, 1 + n
        elif row == 1:
            fold = at_least(n, 4)
            first, last = 1 + 3 * fold, 2 + n - fold
        else:
            fold = at_least(n, 3)
            first, last = 2 + fold, 3 + n - 2 * fold
        v = (n - INNER) * UNITS + q
        second = at_least(v, 21)
        v = v - 21 * second
        side = quick + second * (slow - quick)
        j = sum(at_least(v, bound) for bound in (6, 11, 15, 18, 20))
        e = v - (6 * j - (j * (j - 1)) // 2)
        mine = 2 * (e + side * (frames - 1 - 2 * e)) + 1 - side
        theirs = 2 * frames + frames * side + j
        early = theirs + side * (mine - theirs)
        late = mine + side * (theirs - mine)
        early = jnp.where(inner, 2 * first + q % 2, early)
        late = jnp.where(inner, 2 * last + q % 2, late)
        lag = jnp.where(inner, last - first - 1, j + e + LAGS * second)
        return early, late, scaled[lag]

    def finish(total, y, x, place, part, weight):
        phase = signed_phase(y, x, weight)
        early, late = place
        total[early, part] = total[early, part] + phase
        total[late, part] = total[late, part] + phase

    def finish_middle(q, early, late, weight):
        for g in range(0, mid, 16):
            part = pl.ds(g, 16)
            finish(
                mid_total, mid_sums[q, 1, part], mid_sums[q, 0, part], (early, late), part, weight
            )

    def finish_edges(q, at, early, late, weight):
        real = edge_sums[q, 0:EDGE] + held[at, 0]
        imag = edge_sums[q, EDGE : 2 * EDGE] + held[at, 1]
        finish(edge_total, imag, real, (early, late), pl.ds(0, EDGE), weight)

    nothing = tuple((jnp.int32(0), jnp.int32(1), jnp.float32(0)) for _ in range(UNITS))

    def middle_step(n, before):
        b = n - INNER

        @pl.when(b == 0)
        def _():
            take_near(quick, 0)

        @pl.when(b == 1)
        def _():
            take_near(quick, 1)
            take_near(quick, 2)

        @pl.when(b == 2)
        def _():
            take_near(quick, 3)

        @pl.when(b == 3)
        def _():
            take_near(quick, 4)
            take_near(quick, 5)
            take_slow(0)

        @pl.when(b == 4)
        def _():
            take_slow(1)

        @pl.when(b == 5)
        def _():
            take_slow(2)

        @pl.when(b == 6)
        def _():
            take_slow(3, 4, 5)

        now = tuple(unit(n, q) for q in range(UNITS))
        for q in range(UNITS):
            early, late, _ = now[q]
            parts = split_products(
                (field[early, 0], field[early, 1]), (field[late, 0], field[late, 1])
            )
            result = jnp.dot(
                window, jnp.concatenate(parts, axis=0), preferred_element_type=jnp.float32
            )
            finish_middle(q, *before[q])
            for c in range(2):
                value = result[c * depth : (c + 1) * depth]
                mid_sums[q, c] = value[HMAX : depth - HMAX]
                held[n * UNITS + q, c, 0:HMAX] = value[:HMAX]
                held[n * UNITS + q, c, HMAX:EDGE] = value[depth - HMAX :]

        for group in range(3):

            @pl.when(b == 2 + group)
            def _(group=group):
                send_quick(group, middle)

        for group in range(2):

            @pl.when(b == 5 + group)
            def _(group=group):
                send_slow(group, middle)

        return now

    before = lax.fori_loop(0, STEPS, middle_step, nothing)
    for q in range(UNITS):
        finish_middle(q, *before[q])
    send_slow(2, middle)

    for way in range(2):
        edge_copy(way).wait_recv()

    def own_edges(f, carry):
        for s in range(2):
            cut = pl.ds(s * strip, strip)
            put_edges(2 * f + s, edge_in[0, f, :, cut], edge_in[1, f, :, cut])
        return carry

    lax.fori_loop(0, frames, own_edges, 0)
    take_far(quick)
    edge_window = edge_band[...].astype(jnp.bfloat16)

    def edge_step(m, before):
        n = lax.rem(m + INNER, STEPS)
        last = lax.rem(m + INNER + STEPS - 1, STEPS)

        @pl.when(m == 3)
        def _():
            @pl.when(slow_here)
            def _():
                take_far(slow)

            @pl.when(jnp.logical_not(slow_here))
            def _():
                def clear(j, carry):
                    edges[2 * frames + frames * slow + j] = jnp.zeros(edges.shape[1:], jnp.float32)
                    return carry

                lax.fori_loop(0, frames, clear, 0)

        now = tuple(unit(n, q) for q in range(UNITS))
        for start in range(0, UNITS, 3):
            parts = []
            for q in range(start, start + 3):
                early, late, _ = now[q]
                parts += split_products(
                    (edges[early, 0], edges[early, 1]), (edges[late, 0], edges[late, 1])
                )
            result = jnp.dot(
                edge_window, jnp.concatenate(parts, axis=0), preferred_element_type=jnp.float32
            )
            for q in range(start, start + 3):
                finish_edges(q, last * UNITS + q, *before[q])
                edge_sums[q] = result[(q - start) * 2 * EDGE : (q - start + 1) * 2 * EDGE]

        for group in range(3):

            @pl.when(m == 2 + group)
            def _(group=group):
                send_quick(group, rim)

            @pl.when(m == 5 + group)
            def _(group=group):
                send_slow(group, rim)

        return now

    before = lax.fori_loop(0, STEPS, edge_step, nothing)
    for q in range(UNITS):
        finish_edges(q, (INNER - 1) * UNITS + q, *before[q])

    frame_total = frames * blocks

    def write(side):
        cut = pl.ds(pl.multiple_of(side * strip, strip), strip)

        def write_frame(f, carry):
            now = me * frames + f
            norm = jnp.float32(0.0)
            for lag in range(1, LAGS + 1):
                count = at_least(frame_total - 1, now + lag) + at_least(now, lag)
                norm = norm + scaled[lag - 1] * count.astype(jnp.float32)
            inverse = 1.0 / jnp.full((8, strip), norm, jnp.float32)
            j = f + side * (frames - 1 - 2 * f)
            slot = 2 * f + side
            for g in range(0, mid, 8):
                part = pl.ds(g, 8)
                value = mid_total[slot, part] + mid_back[side, j, part]
                out[f, pl.ds(HMAX + g, 8), cut] = value * inverse
            for g, row in ((0, 0), (HMAX, depth - HMAX)):
                part = pl.ds(g, HMAX)
                value = edge_total[slot, part] + edge_back[side, j, part]
                out[f, pl.ds(row, HMAX), cut] = value * inverse
            return carry

        lax.fori_loop(0, frames, write_frame, 0)

    def wait_back(side, groups):
        for what in (middle, rim):
            for group in range(3):
                back_copy(side, group, groups, *what).wait_send()
                back_copy(1 - side, group, groups, *what).wait_recv()

    wait_back(quick, NEAR_GROUPS)
    write(quick)

    @pl.when(slow_here)
    def _():
        wait_back(slow, FAR_GROUPS)

    write(slow)

    for way in range(2):
        edge_copy(way).wait_send()
    for side in range(2):

        @pl.when(beside[side])
        def _(side=side):
            for way in range(2):
                far_copy(side, way).wait_send()
            for j in range(frames):
                near_copy(side, j).wait_send()


def shards(iq, half, weights):
    _, frames, depth, lines = iq.shape
    strip = lines // 2
    mid = depth - EDGE
    slots = 4 * frames
    wide, thin = jnp.float32, jnp.bfloat16
    dma = pltpu.SemaphoreType.DMA
    return pl.pallas_call(
        kernel,
        out_shape=pltpu.VMEM((frames, depth, lines), wide),
        in_specs=[pl.BlockSpec(memory_space=pltpu.HBM)] * 3,
        out_specs=pl.BlockSpec(memory_space=pltpu.VMEM),
        scratch_shapes=[
            pltpu.SMEM(half.shape, jnp.int32),
            pltpu.SMEM(weights.shape, jnp.int32),
            pltpu.SMEM((2 * LAGS,), wide),
            pltpu.VMEM((2, frames, depth, lines), thin),
            pltpu.VMEM((2, frames, EDGE, lines), thin),
            pltpu.VMEM((2, frames, EDGE, lines), thin),
            pltpu.VMEM((2, frames, 2, depth, strip), thin),
            pltpu.VMEM((2, 2, frames, EDGE, strip), thin),
            pltpu.VMEM((slots, 2, depth, strip), wide),
            pltpu.VMEM((slots, 2, EDGE, strip), wide),
            pltpu.VMEM((slots, mid, strip), wide),
            pltpu.VMEM((slots, EDGE, strip), wide),
            pltpu.VMEM((UNITS, 2, mid, strip), wide),
            pltpu.VMEM((UNITS, 2 * EDGE, strip), wide),
            pltpu.VMEM((STEPS * UNITS, 2, EDGE, strip), wide),
            pltpu.VMEM((2 * depth, 4 * depth), wide),
            pltpu.VMEM((6 * EDGE, 12 * EDGE), wide),
            pltpu.VMEM((2, frames, mid, strip), wide),
            pltpu.VMEM((2, frames, EDGE, strip), wide),
            dma(()),
            dma((2,)),
            dma((2,)),
            dma((2,)),
            dma((2, frames)),
            dma((2, frames)),
            dma((2, 2)),
            dma((2, 2)),
            dma((2, 3)),
            dma((2, 3)),
            dma((2, 3)),
            dma((2, 3)),
        ],
        compiler_params=pltpu.CompilerParams(
            collective_id=0, has_side_effects=True, vmem_limit_bytes=48 * 1024 * 1024
        ),
        name="pair_phases",
    )(*(pltpu.with_memory_space_constraint(x, pltpu.HBM) for x in (iq, half, weights)))


def solution(mesh):
    placed = (P(None, "tm", "depth", None), P("depth"), P())
    return jax.shard_map(
        shards, mesh=mesh, in_specs=placed, out_specs=P("tm", "depth", None), check_vma=False
    )
```

```python
import functools

import jax
import jax.numpy as jnp
import numpy as np
from jax import lax
from jax.experimental import pallas as pl
from jax.experimental.pallas import tpu as pltpu
from jax.sharding import PartitionSpec as P

LAGS = 6
HMAX = 8
HALF_PI = float(np.float32(np.pi / 2))
PI = float(np.float32(np.pi))
TINY = 1.1754944e-38
ATAN = (
    0.9999960660934448,
    -0.33301785588264465,
    0.19582265615463257,
    -0.12176322191953659,
    0.05807745084166527,
    -0.0137208616361022,
)
MESH = pl.DeviceIdType.MESH
UNITS = 3
STEPS = 7
INNER = 10
QUICK = 7
EDGE = 2 * HMAX
SLOW_GROUPS = ((0, 1), (1, 1), (2, 1), (3, 1), (4, 2))


def at_least(value, bound):
    return (value >= bound).astype(jnp.int32)


def signed_phase(y, x, weight):
    ax = jnp.abs(x)
    ay = jnp.abs(y)
    high = jnp.maximum(jnp.maximum(ax, ay), TINY)
    t = jnp.minimum(ax, ay) * pltpu.reciprocal(high, approx=True)
    s = t * t
    poly = ATAN[-1] * s + ATAN[-2]
    for coefficient in ATAN[-3::-1]:
        poly = poly * s + coefficient
    angle = poly * t
    angle = jnp.where(ay > ax, HALF_PI - angle, angle)
    angle = jnp.where(x < 0, PI - angle, angle)
    return angle * jnp.where(y < 0, -weight, weight)


def split_products(early, late):
    parts = []
    (ar, ai), (br, bi) = early, late
    for value in (br * ar + bi * ai, bi * ar - br * ai):
        high = value.astype(jnp.bfloat16)
        low = (value - high.astype(jnp.float32)).astype(jnp.bfloat16)
        parts += [high, low]
    return parts


def kernel(
    iq_any, half_any, weights_any, out,
    half, weights, scaled, own16, edge_out, edge_in, near16, near_edge, field, edges,
    total, sums, held, band, edge_band, back,
    load_sem, small_sem, edge_send, edge_recv, near_send, near_recv, far_send, far_recv,
    back_send, back_recv,
):
    frames, depth, lines = own16.shape[1:]
    strip = lines // 2
    me, level = lax.axis_index("tm"), lax.axis_index("depth")
    blocks, slabs = lax.axis_size("tm"), lax.axis_size("depth")
    left, right = lax.rem(me + blocks - 1, blocks), lax.rem(me + 1, blocks)
    below, above = lax.rem(level + slabs - 1, slabs), lax.rem(level + 1, slabs)
    slow = lax.rem(me, 2)
    quick = 1 - slow
    beside = (me > 0, me < blocks - 1)
    target = me - 1 + 2 * slow
    slow_here = (target >= 0) & (target < blocks)

    load = pltpu.make_async_copy(iq_any, own16, load_sem)
    load.start()
    small = [
        pltpu.make_async_copy(half_any, half, small_sem.at[0]),
        pltpu.make_async_copy(weights_any, weights, small_sem.at[1]),
    ]
    for copy in small:
        copy.start()
    barrier = pltpu.get_barrier_semaphore()
    for other in (below, above):
        pl.semaphore_signal(barrier, inc=1, device_id=(me, other), device_id_type=MESH)
    for side, column in enumerate((left, right)):

        @pl.when(beside[side])
        def _(column=column):
            for other in (level, below, above):
                pl.semaphore_signal(barrier, inc=1, device_id=(column, other), device_id_type=MESH)

    def cut(side):
        return pl.ds(pl.multiple_of(side * strip, strip), strip)

    def next_to(side):
        return lax.rem(me + blocks - 1 + 2 * side, blocks)

    def frame_at(side, j):
        return j + side * (frames - 1 - 2 * j)

    def edge_copy(way):
        return pltpu.make_async_remote_copy(
            src_ref=edge_out.at[way],
            dst_ref=edge_in.at[1 - way],
            send_sem=edge_send,
            recv_sem=edge_recv,
            device_id=(me, below if way == 0 else above),
            device_id_type=MESH,
        )

    def near_copy(side, j):
        return pltpu.make_async_remote_copy(
            src_ref=own16.at[:, frame_at(side, j), :, cut(side)],
            dst_ref=near16.at[1 - side, j],
            send_sem=near_send.at[side],
            recv_sem=near_recv.at[1 - side, j],
            device_id=(next_to(side), level),
            device_id_type=MESH,
        )

    def far_copy(way):
        return pltpu.make_async_remote_copy(
            src_ref=edge_out.at[way, :, :, cut(slow)],
            dst_ref=near_edge.at[1 - slow, 1 - way],
            send_sem=far_send.at[slow],
            recv_sem=far_recv.at[1 - slow],
            device_id=(next_to(slow), below if way == 0 else above),
            device_id_type=MESH,
        )

    def halo_copy():
        return pltpu.make_async_remote_copy(
            src_ref=edge_in.at[:, :, :, cut(quick)],
            dst_ref=near_edge.at[1 - quick],
            send_sem=far_send.at[quick],
            recv_sem=far_recv.at[1 - quick],
            device_id=(next_to(quick), level),
            device_id_type=MESH,
        )

    def back_copy(side, first, count):
        return pltpu.make_async_remote_copy(
            src_ref=total.at[pl.ds(2 * frames + frames * side + first, count)],
            dst_ref=back.at[1 - side, pl.ds(first, count)],
            send_sem=back_send.at[side],
            recv_sem=back_recv.at[1 - side],
            device_id=(next_to(side), level),
            device_id_type=MESH,
        )

    def waiter(ref, send, recv):
        return pltpu.make_async_remote_copy(
            src_ref=ref, dst_ref=ref, send_sem=send, recv_sem=recv,
            device_id=(me, above), device_id_type=MESH,
        )

    def if_slow(act):
        pl.when(slow_here)(act)

    for copy in small:
        copy.wait()
    for lag in range(LAGS):
        value = weights[lag].astype(jnp.float32)
        scaled[lag] = value
        scaled[LAGS + lag] = value * jnp.where(slow_here, 1.0, 0.0)
    sub = lax.broadcasted_iota(jnp.int32, (8, 4 * (depth + EDGE)), 0)
    column = lax.broadcasted_iota(jnp.int32, (8, 4 * (depth + EDGE)), 1)
    halo = lax.rem(column, EDGE)
    halo = jnp.where(halo < HMAX, halo - HMAX, halo - HMAX + depth)
    inside = column < 4 * depth
    place = jnp.where(inside, lax.rem(column, depth), halo)
    upper = column < jnp.where(inside, 2 * depth, 4 * depth + 2 * EDGE)
    reach = []
    for g in range(0, depth, 8):
        value = jnp.full(sub.shape, half[g], jnp.int32)
        for r in range(1, 8):
            value = jnp.where(sub == r, half[g + r], value)
        reach.append(value)
        keep = jnp.abs(place - (sub + g)) <= value
        band[g : g + 8] = jnp.where(keep & upper, 1.0, 0.0)
        band[depth + g : depth + g + 8] = jnp.where(keep & jnp.logical_not(upper), 1.0, 0.0)
    which = column // (2 * EDGE)
    for block in range(16):
        g = 0 if block % 2 == 0 else depth - 8
        keep = jnp.abs(halo - (sub + g)) <= reach[g // 8]
        edge_band[block * 8 : block * 8 + 8] = jnp.where(keep & (which == block // 2), 1.0, 0.0)
    window = band[...].astype(jnp.bfloat16)

    pl.semaphore_wait(barrier, 2 + 3 * sum(side.astype(jnp.int32) for side in beside))

    load.wait()

    for f in range(frames):
        first, last = [], []
        for c in range(2):
            wide = own16[c, f].astype(jnp.float32)
            first.append(wide[:HMAX])
            last.append(wide[depth - HMAX :])
        edge_out[0, f] = jnp.concatenate(first, axis=0).astype(jnp.bfloat16)
        edge_out[1, f] = jnp.concatenate(last, axis=0).astype(jnp.bfloat16)

    for way in range(2):
        edge_copy(way).start()

    @if_slow
    def _():
        for way in range(2):
            far_copy(way).start()
        for j in range(frames):
            near_copy(slow, j).start()

    for j in range(frames):
        near_copy(quick, j).start()

    def own_field(f, carry):
        for c in range(2):
            wide = own16[c, f].astype(jnp.float32) * 0.5
            for s in range(2):
                field[2 * f + s, c] = wide[:, s * strip : (s + 1) * strip]
        return carry

    lax.fori_loop(0, frames, own_field, 0)
    total[...] = jnp.zeros_like(total)
    sums[...] = jnp.zeros_like(sums)

    @pl.when(jnp.logical_not(slow_here))
    def _():
        back[slow] = jnp.zeros(back.shape[1:], jnp.float32)

    low_factor = jnp.where(level > 0, 0.5, 0.0)
    high_factor = jnp.where(level < slabs - 1, 0.5, 0.0)

    def put_edges(slot, low, high):
        low = low.astype(jnp.float32) * low_factor
        high = high.astype(jnp.float32) * high_factor
        for c in range(2):
            edges[slot, c, 0:HMAX] = low[c * HMAX : (c + 1) * HMAX]
            edges[slot, c, HMAX:EDGE] = high[c * HMAX : (c + 1) * HMAX]

    def take_near(side, j):
        waiter(near16.at[side, j], near_send.at[side], near_recv.at[side, j]).wait_recv()
        for c in range(2):
            wide = near16[side, j, c].astype(jnp.float32) * 0.5
            field[2 * frames + frames * side + j, c] = wide

    def take_far(side):
        waiter(near_edge.at[side], far_send.at[side], far_recv.at[side]).wait_recv()
        for j in range(frames):
            frame = frame_at(1 - side, j)
            slot = 2 * frames + frames * side + j
            put_edges(slot, near_edge[side, 0, frame], near_edge[side, 1, frame])

    def finish(place, part, y, x, weight):
        phase = signed_phase(y, x, weight)
        early, late = place
        total[early, part] = total[early, part] + phase
        total[late, part] = total[late, part] + phase

    def inner_unit(n, q):
        c, s = q // 2, q % 2
        rows = ((0, 1 + c), (1, 2 + c) if c < 4 else (4, 5), (2, 3 + c) if c < 3 else (3, 1 + c))
        first, last = (
            jnp.where(n == 0, rows[0][i], jnp.where(n == 1, rows[1][i], rows[2][i])) for i in range(2)
        )
        return 2 * first + s, 2 * last + s, scaled[last - first - 1]

    def outer_unit(side, v, weight_at):
        j = sum(at_least(v, bound) for bound in (6, 11, 15, 18, 20))
        e = v - (6 * j - (j * (j - 1)) // 2)
        mine = 2 * frame_at(side, e) + 1 - side
        theirs = 2 * frames + frames * side + j
        early = theirs + side * (mine - theirs)
        late = mine + side * (theirs - mine)
        return early, late, scaled[weight_at + j + e]

    def middles(units, base):
        results = []
        for q in range(len(units) + 2):
            if q < len(units):
                early, late, _ = units[q]
                parts = split_products(
                    (field[early, 0], field[early, 1]), (field[late, 0], field[late, 1])
                )
                results.append(
                    jnp.dot(
                        window[:, : 4 * depth],
                        jnp.concatenate(parts, axis=0),
                        preferred_element_type=jnp.float32,
                    )
                )
            if q >= 2:
                early, late, weight = units[q - 2]
                real, imag = results[q - 2][:depth], results[q - 2][depth:]
                for c, value in enumerate((real, imag)):
                    held[base + q - 2, c, 0:HMAX] = value[:HMAX]
                    held[base + q - 2, c, HMAX:EDGE] = value[depth - HMAX :]
                for g in range(HMAX, depth - HMAX, 16):
                    finish(
                        (early, late), pl.ds(g, 16), imag[g : g + 16], real[g : g + 16], weight
                    )

    def rims(units, base):
        results = []
        for start in range(0, len(units), 4):
            group = units[start : start + 4]
            parts = []
            for early, late, _ in group:
                parts += split_products(
                    (edges[early, 0], edges[early, 1]), (edges[late, 0], edges[late, 1])
                )
            rows, columns = 2 * EDGE * len(group), 4 * EDGE * len(group)
            result = jnp.dot(
                edge_window[:rows, :columns],
                jnp.concatenate(parts, axis=0),
                preferred_element_type=jnp.float32,
            )
            results += [result[2 * EDGE * k : 2 * EDGE * (k + 1)] for k in range(len(group))]
        for q, (early, late, weight) in enumerate(units):
            real = results[q][:EDGE] + held[base + q, 0]
            imag = results[q][EDGE:] + held[base + q, 1]
            finish((early, late), pl.ds(0, HMAX), imag[:HMAX], real[:HMAX], weight)
            finish((early, late), pl.ds(depth - HMAX, HMAX), imag[HMAX:], real[HMAX:], weight)

    def inner_middles(n, carry):
        middles([inner_unit(n, q) for q in range(INNER)], n * INNER)
        return carry

    def inner_rims(n, carry):
        rims([inner_unit(n, q) for q in range(INNER)], n * INNER)
        return carry

    def quick_middles(n, carry):
        for at, js in ((0, (0, 1)), (1, (2,)), (2, (3, 4, 5))):

            @pl.when(n == at)
            def _(js=js):
                for j in js:
                    take_near(quick, j)

        middles([outer_unit(quick, n * QUICK + q, 0) for q in range(QUICK)], 3 * INNER + n * QUICK)
        return carry

    def quick_rims(n, carry):
        rims([outer_unit(quick, n * QUICK + q, 0) for q in range(QUICK)], 3 * INNER + n * QUICK)
        return carry

    def slow_unit(n, q):
        return outer_unit(slow, n * UNITS + q, LAGS)

    def finish_slow(q, early, late, weight):
        for g in range(0, depth, 24):
            part = pl.ds(g, 24)
            finish((early, late), part, sums[q, pl.ds(depth + g, 24)], sums[q, part], weight)

    def slow_step(n, carry):
        before, now = carry
        for at, js in ((0, (0,)), (2, (1,)), (3, (2,)), (5, (3,)), (6, (4, 5))):

            @pl.when((n == at) & slow_here)
            def _(js=js):
                for j in js:
                    take_near(slow, j)

        after = tuple(slow_unit(jnp.minimum(n + 1, STEPS - 1), q) for q in range(UNITS))
        for q in range(UNITS):
            early, late, _ = now[q]
            parts = split_products(
                (field[early, 0], field[early, 1]), (field[late, 0], field[late, 1])
            ) + split_products(
                (edges[early, 0], edges[early, 1]), (edges[late, 0], edges[late, 1])
            )
            result = jnp.dot(
                window, jnp.concatenate(parts, axis=0), preferred_element_type=jnp.float32
            )
            finish_slow(q, *before[q])
            sums[q] = result

        for at, group in zip((2, 4, 5, 6), SLOW_GROUPS):

            @pl.when((n == at) & slow_here)
            def _(group=group):
                back_copy(slow, *group).start()

        return now, after

    @pl.when(jnp.logical_not(slow_here))
    def _():
        def clear(j, carry):
            slot = 2 * frames + frames * slow + j
            field[slot] = jnp.zeros(field.shape[1:], jnp.float32)
            edges[slot] = jnp.zeros(edges.shape[1:], jnp.float32)
            return carry

        lax.fori_loop(0, frames, clear, 0)

    lax.fori_loop(0, 3, inner_middles, 0)
    lax.fori_loop(0, 3, quick_middles, 0)

    waiter(edge_in, edge_send, edge_recv).wait_recv()
    halo_copy().start()
    for f in range(frames):
        for s in range(2):
            lanes = pl.ds(s * strip, strip)
            put_edges(2 * f + s, edge_in[0, f, :, lanes], edge_in[1, f, :, lanes])

    @if_slow
    def _():
        take_far(slow)

    nothing = tuple((jnp.int32(0), jnp.int32(1), jnp.float32(0)) for _ in range(UNITS))
    start = tuple(slow_unit(jnp.int32(0), q) for q in range(UNITS))
    before, _ = lax.fori_loop(0, STEPS, slow_step, (nothing, start))
    for q in range(UNITS):
        finish_slow(q, *before[q])

    @if_slow
    def _():
        back_copy(slow, *SLOW_GROUPS[-1]).start()

    take_far(quick)
    edge_window = edge_band[...].astype(jnp.bfloat16)
    lax.fori_loop(0, 3, quick_rims, 0)
    back_copy(quick, 0, frames).start()
    lax.fori_loop(0, 3, inner_rims, 0)

    frame_total = frames * blocks

    def write(side):
        lanes = cut(side)

        def write_frame(f, carry):
            now = me * frames + f
            norm = jnp.float32(0.0)
            for lag in range(1, LAGS + 1):
                count = at_least(frame_total - 1, now + lag) + at_least(now, lag)
                norm = norm + scaled[lag - 1] * count.astype(jnp.float32)
            inverse = 1.0 / jnp.full((8, strip), norm, jnp.float32)
            j = frame_at(side, f)
            slot = 2 * f + side
            for g in range(0, depth, 8):
                part = pl.ds(g, 8)
                out[f, part, lanes] = (total[slot, part] + back[side, j, part]) * inverse
            return carry

        lax.fori_loop(0, frames, write_frame, 0)

    def wait_back(side):
        waiter(back.at[side], back_send.at[side], back_recv.at[side]).wait()

    wait_back(quick)
    write(quick)

    @if_slow
    def _():
        wait_back(slow)

    write(slow)

    waiter(edge_out, edge_send, edge_recv).wait_send()
    for side, here in ((quick, True), (slow, slow_here)):

        @pl.when(here)
        def _(side=side):
            waiter(near_edge.at[side], far_send.at[side], far_recv.at[side]).wait_send()
            waiter(near16.at[side], near_send.at[side], near_send.at[side]).wait_send()


def shards(iq, half, weights):
    _, frames, depth, lines = iq.shape
    strip = lines // 2
    slots = 4 * frames
    wide, thin = jnp.float32, jnp.bfloat16
    dma = pltpu.SemaphoreType.DMA
    return pl.pallas_call(
        kernel,
        out_shape=pltpu.VMEM((frames, depth, lines), wide),
        in_specs=[pl.BlockSpec(memory_space=pltpu.HBM)] * 3,
        out_specs=pl.BlockSpec(memory_space=pltpu.VMEM),
        scratch_shapes=[
            pltpu.SMEM(half.shape, jnp.int32),
            pltpu.SMEM(weights.shape, jnp.int32),
            pltpu.SMEM((2 * LAGS,), wide),
            pltpu.VMEM((2, frames, depth, lines), thin),
            pltpu.VMEM((2, frames, EDGE, lines), thin),
            pltpu.VMEM((2, frames, EDGE, lines), thin),
            pltpu.VMEM((2, frames, 2, depth, strip), thin),
            pltpu.VMEM((2, 2, frames, EDGE, strip), thin),
            pltpu.VMEM((slots, 2, depth, strip), wide),
            pltpu.VMEM((slots, 2, EDGE, strip), wide),
            pltpu.VMEM((slots, depth, strip), wide),
            pltpu.VMEM((UNITS, 2 * depth, strip), wide),
            pltpu.VMEM((3 * (INNER + QUICK), 2, EDGE, strip), wide),
            pltpu.VMEM((2 * depth, 4 * (depth + EDGE)), wide),
            pltpu.VMEM((8 * EDGE, 16 * EDGE), wide),
            pltpu.VMEM((2, frames, depth, strip), wide),
            dma(()),
            dma((2,)),
            dma(()),
            dma(()),
            dma((2,)),
            dma((2, frames)),
            dma((2,)),
            dma((2,)),
            dma((2,)),
            dma((2,)),
        ],
        compiler_params=pltpu.CompilerParams(
            collective_id=0, has_side_effects=True, vmem_limit_bytes=48 * 1024 * 1024
        ),
        name="pair_phases",
    )(*(pltpu.with_memory_space_constraint(x, pltpu.HBM) for x in (iq, half, weights)))


def solution(mesh):
    placed = (P(None, "tm", "depth", None), P("depth"), P())
    return jax.shard_map(
        shards, mesh=mesh, in_specs=placed, out_specs=P("tm", "depth", None), check_vma=False
    )
```

```python
import functools

import jax
import jax.numpy as jnp
import numpy as np
from jax import lax
from jax.experimental import pallas as pl
from jax.experimental.pallas import tpu as pltpu
from jax.sharding import PartitionSpec as P

LAGS = 6
HMAX = 8
HALF_PI = float(np.float32(np.pi / 2))
PI = float(np.float32(np.pi))
TINY = 1.1754944e-38
ATAN = (
    0.9999960660934448,
    -0.33301785588264465,
    0.19582265615463257,
    -0.12176322191953659,
    0.05807745084166527,
    -0.0137208616361022,
)
MESH = pl.DeviceIdType.MESH
UNITS = 3
INNER = 10
QUICK = 7
EDGE = 2 * HMAX
SHARED = 3


def at_least(value, bound):
    return (value >= bound).astype(jnp.int32)


def signed_phase(y, x, weight):
    ax = jnp.abs(x)
    ay = jnp.abs(y)
    high = jnp.maximum(jnp.maximum(ax, ay), TINY)
    t = jnp.minimum(ax, ay) * pltpu.reciprocal(high, approx=True)
    s = t * t
    poly = ATAN[-1] * s + ATAN[-2]
    for coefficient in ATAN[-3::-1]:
        poly = poly * s + coefficient
    angle = poly * t
    angle = jnp.where(ay > ax, HALF_PI - angle, angle)
    angle = jnp.where(x < 0, PI - angle, angle)
    return angle * jnp.where(y < 0, -weight, weight)


def split_products(early, late):
    parts = []
    (ar, ai), (br, bi) = early, late
    for value in (br * ar + bi * ai, bi * ar - br * ai):
        high = value.astype(jnp.bfloat16)
        low = (value - high.astype(jnp.float32)).astype(jnp.bfloat16)
        parts += [high, low]
    return parts


def kernel(
    iq_any, half_any, weights_any, out,
    half, weights, scaled, own16, edge_out, edge_in, near16, near_edge, more16, more_edge,
    field, edges, total, held, band, edge_band, back,
    load_sem, small_sem, edge_send, edge_recv, near_send, near_recv, far_send, far_recv,
    more_send, more_recv, rest_send, rest_recv, back_send, back_recv,
):
    frames, depth, lines = own16.shape[1:]
    strip = lines // 2
    me, level = lax.axis_index("tm"), lax.axis_index("depth")
    blocks, slabs = lax.axis_size("tm"), lax.axis_size("depth")
    left, right = lax.rem(me + blocks - 1, blocks), lax.rem(me + 1, blocks)
    below, above = lax.rem(level + slabs - 1, slabs), lax.rem(level + 1, slabs)
    slow = lax.rem(me, 2)
    quick = 1 - slow
    beside = (me > 0, me < blocks - 1)
    target = me - 1 + 2 * slow
    slow_here = (target >= 0) & (target < blocks)

    load = pltpu.make_async_copy(iq_any, own16, load_sem)
    load.start()
    small = [
        pltpu.make_async_copy(half_any, half, small_sem.at[0]),
        pltpu.make_async_copy(weights_any, weights, small_sem.at[1]),
    ]
    for copy in small:
        copy.start()
    barrier = pltpu.get_barrier_semaphore()
    for other in (below, above):
        pl.semaphore_signal(barrier, inc=1, device_id=(me, other), device_id_type=MESH)
    for side, column in enumerate((left, right)):

        @pl.when(beside[side])
        def _(column=column):
            for other in (level, below, above):
                pl.semaphore_signal(barrier, inc=1, device_id=(column, other), device_id_type=MESH)

    def cut(side):
        return pl.ds(pl.multiple_of(side * strip, strip), strip)

    def next_to(side):
        return lax.rem(me + blocks - 1 + 2 * side, blocks)

    def frame_at(side, j):
        return j + side * (frames - 1 - 2 * j)

    def edge_copy(way):
        return pltpu.make_async_remote_copy(
            src_ref=edge_out.at[way],
            dst_ref=edge_in.at[1 - way],
            send_sem=edge_send,
            recv_sem=edge_recv,
            device_id=(me, below if way == 0 else above),
            device_id_type=MESH,
        )

    def near_copy(side, j):
        return pltpu.make_async_remote_copy(
            src_ref=own16.at[:, frame_at(side, j), :, cut(side)],
            dst_ref=near16.at[1 - side, j],
            send_sem=near_send.at[side],
            recv_sem=near_recv.at[1 - side, j],
            device_id=(next_to(side), level),
            device_id_type=MESH,
        )

    def far_copy(way):
        return pltpu.make_async_remote_copy(
            src_ref=edge_out.at[way, :, :, cut(slow)],
            dst_ref=near_edge.at[1 - slow, 1 - way],
            send_sem=far_send.at[slow],
            recv_sem=far_recv.at[1 - slow],
            device_id=(next_to(slow), below if way == 0 else above),
            device_id_type=MESH,
        )

    def more_copy(j):
        return pltpu.make_async_remote_copy(
            src_ref=own16.at[:, frame_at(slow, j), :, cut(quick)],
            dst_ref=more16.at[j],
            send_sem=more_send,
            recv_sem=more_recv.at[j],
            device_id=(next_to(slow), level),
            device_id_type=MESH,
        )

    def rest_copy(way):
        return pltpu.make_async_remote_copy(
            src_ref=edge_out.at[way, pl.ds(slow * (frames - SHARED), SHARED), :, cut(quick)],
            dst_ref=more_edge.at[1 - way],
            send_sem=rest_send,
            recv_sem=rest_recv,
            device_id=(next_to(slow), below if way == 0 else above),
            device_id_type=MESH,
        )

    def halo_copy():
        return pltpu.make_async_remote_copy(
            src_ref=edge_in.at[:, :, :, cut(quick)],
            dst_ref=near_edge.at[1 - quick],
            send_sem=far_send.at[quick],
            recv_sem=far_recv.at[1 - quick],
            device_id=(next_to(quick), level),
            device_id_type=MESH,
        )

    def back_copy(side, first, count):
        return pltpu.make_async_remote_copy(
            src_ref=total.at[pl.ds(2 * frames + frames * side + first, count)],
            dst_ref=back.at[1 - side, pl.ds(first, count)],
            send_sem=back_send.at[side],
            recv_sem=back_recv.at[1 - side],
            device_id=(next_to(side), level),
            device_id_type=MESH,
        )

    def waiter(ref, send, recv):
        return pltpu.make_async_remote_copy(
            src_ref=ref, dst_ref=ref, send_sem=send, recv_sem=recv,
            device_id=(me, above), device_id_type=MESH,
        )

    def if_slow(act):
        pl.when(slow_here)(act)

    load.wait()

    for f in range(frames):
        first, last = [], []
        for c in range(2):
            wide = own16[c, f].astype(jnp.float32)
            first.append(wide[:HMAX])
            last.append(wide[depth - HMAX :])
        edge_out[0, f] = jnp.concatenate(first, axis=0).astype(jnp.bfloat16)
        edge_out[1, f] = jnp.concatenate(last, axis=0).astype(jnp.bfloat16)

    pl.semaphore_wait(barrier, 2 + 3 * sum(side.astype(jnp.int32) for side in beside))

    @if_slow
    def _():
        for way in range(2):
            far_copy(way).start()
        for j in range(2):
            near_copy(slow, j).start()

    for way in range(2):
        edge_copy(way).start()

    @if_slow
    def _():
        for j in range(2, frames):
            near_copy(slow, j).start()
        for way in range(2):
            rest_copy(way).start()
        for j in range(SHARED):
            more_copy(j).start()

    for j in range(frames):
        near_copy(quick, j).start()

    for copy in small:
        copy.wait()
    for lag in range(LAGS):
        value = weights[lag].astype(jnp.float32)
        scaled[lag] = value
        scaled[LAGS + lag] = value * jnp.where(slow_here, 1.0, 0.0)
    sub = lax.broadcasted_iota(jnp.int32, (8, 4 * (depth + EDGE)), 0)
    column = lax.broadcasted_iota(jnp.int32, (8, 4 * (depth + EDGE)), 1)
    halo = lax.rem(column, EDGE)
    halo = jnp.where(halo < HMAX, halo - HMAX, halo - HMAX + depth)
    inside = column < 4 * depth
    place = jnp.where(inside, lax.rem(column, depth), halo)
    upper = column < jnp.where(inside, 2 * depth, 4 * depth + 2 * EDGE)
    reach = []
    for g in range(0, depth, 8):
        value = jnp.full(sub.shape, half[g], jnp.int32)
        for r in range(1, 8):
            value = jnp.where(sub == r, half[g + r], value)
        reach.append(value)
        keep = jnp.abs(place - (sub + g)) <= value
        band[g : g + 8] = jnp.where(keep & upper, 1.0, 0.0)
        band[depth + g : depth + g + 8] = jnp.where(keep & jnp.logical_not(upper), 1.0, 0.0)
    which = column // (2 * EDGE)
    for block in range(16):
        g = 0 if block % 2 == 0 else depth - 8
        keep = jnp.abs(halo - (sub + g)) <= reach[g // 8]
        edge_band[block * 8 : block * 8 + 8] = jnp.where(keep & (which == block // 2), 1.0, 0.0)
    window = band[...].astype(jnp.bfloat16)

    def own_field(f, carry):
        for c in range(2):
            wide = own16[c, f].astype(jnp.float32) * 0.5
            for s in range(2):
                field[2 * f + s, c] = wide[:, s * strip : (s + 1) * strip]
        return carry

    lax.fori_loop(0, frames, own_field, 0)
    total[...] = jnp.zeros_like(total)
    back[slow, SHARED:] = jnp.zeros((frames - SHARED,) + back.shape[2:], jnp.float32)

    @pl.when(jnp.logical_not(slow_here))
    def _():
        back[slow, :SHARED] = jnp.zeros((SHARED,) + back.shape[2:], jnp.float32)

    low_factor = jnp.where(level > 0, 0.5, 0.0)
    high_factor = jnp.where(level < slabs - 1, 0.5, 0.0)

    def put_edges(slot, low, high):
        low = low.astype(jnp.float32) * low_factor
        high = high.astype(jnp.float32) * high_factor
        for c in range(2):
            edges[slot, c, 0:HMAX] = low[c * HMAX : (c + 1) * HMAX]
            edges[slot, c, HMAX:EDGE] = high[c * HMAX : (c + 1) * HMAX]

    def take_near(side, j):
        waiter(near16.at[side, j], near_send.at[side], near_recv.at[side, j]).wait_recv()
        for c in range(2):
            wide = near16[side, j, c].astype(jnp.float32) * 0.5
            field[2 * frames + frames * side + j, c] = wide

    def take_far(side):
        waiter(near_edge.at[side], far_send.at[side], far_recv.at[side]).wait_recv()
        for j in range(frames):
            frame = frame_at(1 - side, j)
            slot = 2 * frames + frames * side + j
            put_edges(slot, near_edge[side, 0, frame], near_edge[side, 1, frame])

    def take_more(j):
        waiter(more16.at[j], more_send, more_recv.at[j]).wait_recv()
        for c in range(2):
            field[4 * frames + j, c] = more16[j, c].astype(jnp.float32) * 0.5

    def take_rest():
        waiter(more_edge, rest_send, rest_recv).wait_recv()
        for j in range(SHARED):
            k = SHARED - 1 - j + slow * (2 * j - SHARED + 1)
            put_edges(4 * frames + j, more_edge[0, k], more_edge[1, k])

    def finish(place, part, y, x, weight):
        phase = signed_phase(y, x, weight)
        early, late = place
        total[early, part] = total[early, part] + phase
        total[late, part] = total[late, part] + phase

    def inner_unit(n, q):
        c, s = q // 2, q % 2
        rows = ((0, 1 + c), (1, 2 + c) if c < 4 else (4, 5), (2, 3 + c) if c < 3 else (3, 1 + c))
        first, last = (
            jnp.where(n == 0, rows[0][i], jnp.where(n == 1, rows[1][i], rows[2][i])) for i in range(2)
        )
        return 2 * first + s, 2 * last + s, scaled[last - first - 1]

    def outer_unit(side, v, weight_at):
        j = sum(at_least(v, bound) for bound in (6, 11, 15, 18, 20))
        e = v - (6 * j - (j * (j - 1)) // 2)
        mine = 2 * frame_at(side, e) + 1 - side
        theirs = 2 * frames + frames * side + j
        early = theirs + side * (mine - theirs)
        late = mine + side * (theirs - mine)
        return early, late, scaled[weight_at + j + e]

    def middles(units, base):
        results = []
        for q in range(len(units) + 2):
            if q < len(units):
                early, late, _ = units[q]
                parts = split_products(
                    (field[early, 0], field[early, 1]), (field[late, 0], field[late, 1])
                )
                results.append(
                    jnp.dot(
                        window[:, : 4 * depth],
                        jnp.concatenate(parts, axis=0),
                        preferred_element_type=jnp.float32,
                    )
                )
            if q >= 2:
                early, late, weight = units[q - 2]
                real, imag = results[q - 2][:depth], results[q - 2][depth:]
                for c, value in enumerate((real, imag)):
                    held[base + q - 2, c, 0:HMAX] = value[:HMAX]
                    held[base + q - 2, c, HMAX:EDGE] = value[depth - HMAX :]
                for g in range(HMAX, depth - HMAX, 16):
                    finish(
                        (early, late), pl.ds(g, 16), imag[g : g + 16], real[g : g + 16], weight
                    )

    def rims(units, base):
        results = []
        for start in range(0, len(units), 4):
            group = units[start : start + 4]
            parts = []
            for early, late, _ in group:
                parts += split_products(
                    (edges[early, 0], edges[early, 1]), (edges[late, 0], edges[late, 1])
                )
            rows, columns = 2 * EDGE * len(group), 4 * EDGE * len(group)
            result = jnp.dot(
                edge_window[:rows, :columns],
                jnp.concatenate(parts, axis=0),
                preferred_element_type=jnp.float32,
            )
            results += [result[2 * EDGE * k : 2 * EDGE * (k + 1)] for k in range(len(group))]
        for q, (early, late, weight) in enumerate(units):
            real = results[q][:EDGE] + held[base + q, 0]
            imag = results[q][EDGE:] + held[base + q, 1]
            finish((early, late), pl.ds(0, HMAX), imag[:HMAX], real[:HMAX], weight)
            finish((early, late), pl.ds(depth - HMAX, HMAX), imag[HMAX:], real[HMAX:], weight)

    def inner_middles(n, carry):
        middles([inner_unit(n, q) for q in range(INNER)], n * INNER)
        return carry

    def inner_rims(n, carry):
        rims([inner_unit(n, q) for q in range(INNER)], n * INNER)
        return carry

    def quick_middles(n, carry):
        for at, js in ((0, (0, 1)), (1, (2,)), (2, (3, 4, 5))):

            @pl.when(n == at)
            def _(js=js):
                for j in js:
                    take_near(quick, j)

        middles([outer_unit(quick, n * QUICK + q, 0) for q in range(QUICK)], 3 * INNER + n * QUICK)
        return carry

    def quick_rims(n, carry):
        rims([outer_unit(quick, n * QUICK + q, 0) for q in range(QUICK)], 3 * INNER + n * QUICK)
        return carry

    def slow_unit(j, e):
        mine = 2 * frame_at(slow, e) + 1 - slow
        theirs = 2 * frames + frames * slow + j
        early = theirs + slow * (mine - theirs)
        late = mine + slow * (theirs - mine)
        return early, late, scaled[LAGS + j + e]

    def last_unit(n, q):
        def pick(values):
            value = values[3]
            for k in (2, 1, 0):
                value = jnp.where(n == k, values[k], value)
            return value

        j = pick(((3, 4, 0, 1), (3, 4, 0, 1), (3, 5, 0, 2))[q])
        e = pick(((0, 0, 3, 3), (1, 1, 4, 4), (2, 0, 5, 3))[q])
        own = jnp.where(n < 2, 1 - slow, slow)
        mine = 2 * frame_at(slow, e) + own
        theirs = j + jnp.where(n < 2, 2 * frames + frames * slow, 4 * frames)
        early = theirs + slow * (mine - theirs)
        late = mine + slow * (theirs - mine)
        return early, late, scaled[LAGS + j + e]

    def wholes(units):
        results = []
        for q in range(len(units) + 2):
            if q < len(units):
                early, late, _ = units[q]
                parts = split_products(
                    (field[early, 0], field[early, 1]), (field[late, 0], field[late, 1])
                ) + split_products(
                    (edges[early, 0], edges[early, 1]), (edges[late, 0], edges[late, 1])
                )
                results.append(
                    jnp.dot(
                        window, jnp.concatenate(parts, axis=0), preferred_element_type=jnp.float32
                    )
                )
            if q >= 2:
                early, late, weight = units[q - 2]
                real, imag = results[q - 2][:depth], results[q - 2][depth:]
                for g in range(0, depth, 24):
                    finish(
                        (early, late), pl.ds(g, 24), imag[g : g + 24], real[g : g + 24], weight
                    )

    def last_step(n, carry):
        @pl.when((n == 0) & slow_here)
        def _():
            take_near(slow, 3)

        @pl.when((n == 1) & slow_here)
        def _():
            take_near(slow, 4)
            take_near(slow, 5)

        @pl.when((n == 2) & slow_here)
        def _():
            take_rest()
            take_more(0)

        @pl.when((n == 3) & slow_here)
        def _():
            take_more(1)
            take_more(2)

        wholes([last_unit(n, q) for q in range(UNITS)])
        return carry

    @pl.when(jnp.logical_not(slow_here))
    def _():
        def clear(j, carry):
            slot = 2 * frames + frames * slow + j
            field[slot] = jnp.zeros(field.shape[1:], jnp.float32)
            edges[slot] = jnp.zeros(edges.shape[1:], jnp.float32)
            return carry

        lax.fori_loop(0, frames, clear, 0)
        for j in range(SHARED):
            field[4 * frames + j] = jnp.zeros(field.shape[1:], jnp.float32)
            edges[4 * frames + j] = jnp.zeros(edges.shape[1:], jnp.float32)

    lax.fori_loop(0, 3, inner_middles, 0)
    lax.fori_loop(0, 3, quick_middles, 0)

    waiter(edge_in, edge_send, edge_recv).wait_recv()
    halo_copy().start()
    for f in range(frames):
        for s in range(2):
            lanes = pl.ds(s * strip, strip)
            put_edges(2 * f + s, edge_in[0, f, :, lanes], edge_in[1, f, :, lanes])

    edge_window = edge_band[...].astype(jnp.bfloat16)
    lax.fori_loop(0, 3, inner_rims, 0)

    for j in range(SHARED):

        @if_slow
        def _(j=j):
            if j == 0:
                take_far(slow)
            take_near(slow, j)

        wholes([slow_unit(j, e) for e in range(frames - j)])

        @if_slow
        def _(j=j):
            back_copy(slow, j, 1).start()

    lax.fori_loop(0, 2, last_step, 0)
    take_far(quick)
    lax.fori_loop(0, 3, quick_rims, 0)
    back_copy(quick, 0, frames).start()
    lax.fori_loop(2, 4, last_step, 0)

    frame_total = frames * blocks

    def write(side):
        lanes = cut(side)

        def write_frame(f, carry):
            now = me * frames + f
            norm = jnp.float32(0.0)
            for lag in range(1, LAGS + 1):
                count = at_least(frame_total - 1, now + lag) + at_least(now, lag)
                norm = norm + scaled[lag - 1] * count.astype(jnp.float32)
            inverse = 1.0 / jnp.full((8, strip), norm, jnp.float32)
            j = frame_at(side, f)
            slot = 2 * f + side
            for g in range(0, depth, 8):
                part = pl.ds(g, 8)
                out[f, part, lanes] = (total[slot, part] + back[side, j, part]) * inverse
            return carry

        lax.fori_loop(0, frames, write_frame, 0)

    waiter(back.at[quick], back_send.at[quick], back_recv.at[quick]).wait()
    write(quick)

    @if_slow
    def _():
        waiter(back.at[slow, pl.ds(0, SHARED)], back_send.at[slow], back_recv.at[slow]).wait()

    write(slow)

    @if_slow
    def _():
        waiter(more_edge, rest_send, rest_recv).wait_send()
        waiter(more16, more_send, more_send).wait_send()

    waiter(edge_out, edge_send, edge_recv).wait_send()
    for side, here in ((quick, True), (slow, slow_here)):

        @pl.when(here)
        def _(side=side):
            waiter(near_edge.at[side], far_send.at[side], far_recv.at[side]).wait_send()
            waiter(near16.at[side], near_send.at[side], near_send.at[side]).wait_send()


def shards(iq, half, weights):
    _, frames, depth, lines = iq.shape
    strip = lines // 2
    slots = 4 * frames + SHARED
    wide, thin = jnp.float32, jnp.bfloat16
    dma = pltpu.SemaphoreType.DMA
    return pl.pallas_call(
        kernel,
        out_shape=pltpu.VMEM((frames, depth, lines), wide),
        in_specs=[pl.BlockSpec(memory_space=pltpu.HBM)] * 3,
        out_specs=pl.BlockSpec(memory_space=pltpu.VMEM),
        scratch_shapes=[
            pltpu.SMEM(half.shape, jnp.int32),
            pltpu.SMEM(weights.shape, jnp.int32),
            pltpu.SMEM((2 * LAGS,), wide),
            pltpu.VMEM((2, frames, depth, lines), thin),
            pltpu.VMEM((2, frames, EDGE, lines), thin),
            pltpu.VMEM((2, frames, EDGE, lines), thin),
            pltpu.VMEM((2, frames, 2, depth, strip), thin),
            pltpu.VMEM((2, 2, frames, EDGE, strip), thin),
            pltpu.VMEM((SHARED, 2, depth, strip), thin),
            pltpu.VMEM((2, SHARED, EDGE, strip), thin),
            pltpu.VMEM((slots, 2, depth, strip), wide),
            pltpu.VMEM((slots, 2, EDGE, strip), wide),
            pltpu.VMEM((slots, depth, strip), wide),
            pltpu.VMEM((3 * (INNER + QUICK), 2, EDGE, strip), wide),
            pltpu.VMEM((2 * depth, 4 * (depth + EDGE)), wide),
            pltpu.VMEM((8 * EDGE, 16 * EDGE), wide),
            pltpu.VMEM((2, frames, depth, strip), wide),
            dma(()),
            dma((2,)),
            dma(()),
            dma(()),
            dma((2,)),
            dma((2, frames)),
            dma((2,)),
            dma((2,)),
            dma(()),
            dma((SHARED,)),
            dma(()),
            dma(()),
            dma((2,)),
            dma((2,)),
        ],
        compiler_params=pltpu.CompilerParams(
            collective_id=0, has_side_effects=True, vmem_limit_bytes=48 * 1024 * 1024
        ),
        name="pair_phases",
    )(*(pltpu.with_memory_space_constraint(x, pltpu.HBM) for x in (iq, half, weights)))


def solution(mesh):
    placed = (P(None, "tm", "depth", None), P("depth"), P())
    return jax.shard_map(
        shards, mesh=mesh, in_specs=placed, out_specs=P("tm", "depth", None), check_vma=False
    )
```

```python
import functools

import jax
import jax.numpy as jnp
import numpy as np
from jax import lax
from jax.experimental import pallas as pl
from jax.experimental.pallas import tpu as pltpu
from jax.sharding import PartitionSpec as P

LAGS = 6
HMAX = 8
HALF_PI = float(np.float32(np.pi / 2))
PI = float(np.float32(np.pi))
TINY = 1.1754944e-38
ATAN = (
    0.9999960660934448,
    -0.33301785588264465,
    0.19582265615463257,
    -0.12176322191953659,
    0.05807745084166527,
    -0.0137208616361022,
)
MESH = pl.DeviceIdType.MESH
UNITS = 3
INNER = 10
QUICK = 7
EDGE = 2 * HMAX
SHARED = 3
SHARED_STRIPS = 15


def at_least(value, bound):
    return (value >= bound).astype(jnp.int32)


def signed_phase(y, x, weight):
    ax = jnp.abs(x)
    ay = jnp.abs(y)
    high = jnp.maximum(jnp.maximum(ax, ay), TINY)
    t = jnp.minimum(ax, ay) * pltpu.reciprocal(high, approx=True)
    s = t * t
    poly = ATAN[-1] * s + ATAN[-2]
    for coefficient in ATAN[-3::-1]:
        poly = poly * s + coefficient
    angle = poly * t
    angle = jnp.where(ay > ax, HALF_PI - angle, angle)
    angle = jnp.where(x < 0, PI - angle, angle)
    return angle * jnp.where(y < 0, -weight, weight)


def split_products(early, late):
    parts = []
    (ar, ai), (br, bi) = early, late
    for value in (br * ar + bi * ai, bi * ar - br * ai):
        high = value.astype(jnp.bfloat16)
        low = (value - high.astype(jnp.float32)).astype(jnp.bfloat16)
        parts += [high, low]
    return parts


def kernel(
    iq_any, half_any, weights_any, out,
    half, weights, scaled, own16, edge_out, edge_in, near16, near_edge, more16, more_edge,
    field, edges, total, held, band, edge_band, back,
    load_sem, small_sem, edge_send, edge_recv, near_send, near_recv, far_send, far_recv,
    more_send, more_recv, rest_send, rest_recv, back_send, back_recv,
):
    frames, depth, lines = own16.shape[1:]
    strip = lines // 2
    me, level = lax.axis_index("tm"), lax.axis_index("depth")
    blocks, slabs = lax.axis_size("tm"), lax.axis_size("depth")
    left, right = lax.rem(me + blocks - 1, blocks), lax.rem(me + 1, blocks)
    below, above = lax.rem(level + slabs - 1, slabs), lax.rem(level + 1, slabs)
    slow = lax.rem(me, 2)
    quick = 1 - slow
    beside = (me > 0, me < blocks - 1)
    target = me - 1 + 2 * slow
    slow_here = (target >= 0) & (target < blocks)

    load = pltpu.make_async_copy(iq_any, own16, load_sem)
    load.start()
    small = [
        pltpu.make_async_copy(half_any, half, small_sem.at[0]),
        pltpu.make_async_copy(weights_any, weights, small_sem.at[1]),
    ]
    for copy in small:
        copy.start()
    barrier = pltpu.get_barrier_semaphore()
    for other in (below, above):
        pl.semaphore_signal(barrier, inc=1, device_id=(me, other), device_id_type=MESH)
    for side, column in enumerate((left, right)):

        @pl.when(beside[side])
        def _(column=column):
            for other in (level, below, above):
                pl.semaphore_signal(barrier, inc=1, device_id=(column, other), device_id_type=MESH)

    def cut(side):
        return pl.ds(pl.multiple_of(side * strip, strip), strip)

    def next_to(side):
        return lax.rem(me + blocks - 1 + 2 * side, blocks)

    def frame_at(side, j):
        return j + side * (frames - 1 - 2 * j)

    def edge_copy(way):
        return pltpu.make_async_remote_copy(
            src_ref=edge_out.at[way],
            dst_ref=edge_in.at[1 - way],
            send_sem=edge_send,
            recv_sem=edge_recv,
            device_id=(me, below if way == 0 else above),
            device_id_type=MESH,
        )

    def near_copy(side, j):
        return pltpu.make_async_remote_copy(
            src_ref=iq_any.at[:, frame_at(side, j), :, cut(side)],
            dst_ref=near16.at[1 - side, j],
            send_sem=near_send.at[side],
            recv_sem=near_recv.at[1 - side, j],
            device_id=(next_to(side), level),
            device_id_type=MESH,
        )

    def far_copy(way):
        return pltpu.make_async_remote_copy(
            src_ref=edge_out.at[way, :, :, cut(slow)],
            dst_ref=near_edge.at[1 - slow, 1 - way],
            send_sem=far_send.at[slow],
            recv_sem=far_recv.at[1 - slow],
            device_id=(next_to(slow), below if way == 0 else above),
            device_id_type=MESH,
        )

    def more_copy(j):
        return pltpu.make_async_remote_copy(
            src_ref=own16.at[:, frame_at(slow, j), :, cut(quick)],
            dst_ref=more16.at[j],
            send_sem=more_send,
            recv_sem=more_recv.at[j],
            device_id=(next_to(slow), level),
            device_id_type=MESH,
        )

    def rest_copy(way):
        return pltpu.make_async_remote_copy(
            src_ref=edge_out.at[way, pl.ds(slow * (frames - SHARED), SHARED), :, cut(quick)],
            dst_ref=more_edge.at[1 - way],
            send_sem=rest_send,
            recv_sem=rest_recv,
            device_id=(next_to(slow), below if way == 0 else above),
            device_id_type=MESH,
        )

    def halo_copy():
        return pltpu.make_async_remote_copy(
            src_ref=edge_in.at[:, :, :, cut(quick)],
            dst_ref=near_edge.at[1 - quick],
            send_sem=far_send.at[quick],
            recv_sem=far_recv.at[1 - quick],
            device_id=(next_to(quick), level),
            device_id_type=MESH,
        )

    def back_copy(side, count, part):
        first = 2 * frames + frames * side
        return pltpu.make_async_remote_copy(
            src_ref=total.at[pl.ds(first, count), part],
            dst_ref=back.at[1 - side, pl.ds(0, count), part],
            send_sem=back_send.at[side],
            recv_sem=back_recv.at[1 - side],
            device_id=(next_to(side), level),
            device_id_type=MESH,
        )

    def waiter(ref, send, recv):
        return pltpu.make_async_remote_copy(
            src_ref=ref, dst_ref=ref, send_sem=send, recv_sem=recv,
            device_id=(me, above), device_id_type=MESH,
        )

    def if_slow(act):
        pl.when(slow_here)(act)

    total[...] = jnp.zeros_like(total)
    pl.semaphore_wait(barrier, 2 + 3 * sum(side.astype(jnp.int32) for side in beside))

    @if_slow
    def _():
        for j in range(SHARED):
            near_copy(slow, j).start()

    load.wait()

    for f in range(frames):
        first, last = [], []
        for c in range(2):
            wide = own16[c, f].astype(jnp.float32)
            first.append(wide[:HMAX])
            last.append(wide[depth - HMAX :])
        edge_out[0, f] = jnp.concatenate(first, axis=0).astype(jnp.bfloat16)
        edge_out[1, f] = jnp.concatenate(last, axis=0).astype(jnp.bfloat16)


    @if_slow
    def _():
        for way in range(2):
            far_copy(way).start()

    for way in range(2):
        edge_copy(way).start()

    @if_slow
    def _():
        for j in range(SHARED, frames):
            near_copy(slow, j).start()
        for way in range(2):
            rest_copy(way).start()
        for j in range(SHARED):
            more_copy(j).start()

    for j in range(frames):
        near_copy(quick, j).start()

    for copy in small:
        copy.wait()
    for lag in range(LAGS):
        value = weights[lag].astype(jnp.float32)
        scaled[lag] = value
        scaled[LAGS + lag] = value * jnp.where(slow_here, 1.0, 0.0)
    sub = lax.broadcasted_iota(jnp.int32, (8, 4 * (depth + EDGE)), 0)
    column = lax.broadcasted_iota(jnp.int32, (8, 4 * (depth + EDGE)), 1)
    halo = lax.rem(column, EDGE)
    halo = jnp.where(halo < HMAX, halo - HMAX, halo - HMAX + depth)
    inside = column < 4 * depth
    place = jnp.where(inside, lax.rem(column, depth), halo)
    upper = column < jnp.where(inside, 2 * depth, 4 * depth + 2 * EDGE)
    reach = []
    for g in range(0, depth, 8):
        value = jnp.full(sub.shape, half[g], jnp.int32)
        for r in range(1, 8):
            value = jnp.where(sub == r, half[g + r], value)
        reach.append(value)
        keep = jnp.abs(place - (sub + g)) <= value
        band[g : g + 8] = jnp.where(keep & upper, 1.0, 0.0)
        band[depth + g : depth + g + 8] = jnp.where(keep & jnp.logical_not(upper), 1.0, 0.0)
    which = column // (2 * EDGE)
    for block in range(16):
        g = 0 if block % 2 == 0 else depth - 8
        keep = jnp.abs(halo - (sub + g)) <= reach[g // 8]
        edge_band[block * 8 : block * 8 + 8] = jnp.where(keep & (which == block // 2), 1.0, 0.0)
    window = band[...].astype(jnp.bfloat16)

    def own_field(f, carry):
        for c in range(2):
            wide = own16[c, f].astype(jnp.float32) * 0.5
            for s in range(2):
                field[2 * f + s, c] = wide[:, s * strip : (s + 1) * strip]
        return carry

    lax.fori_loop(0, frames, own_field, 0)
    back[slow, SHARED:] = jnp.zeros((frames - SHARED,) + back.shape[2:], jnp.float32)

    @pl.when(jnp.logical_not(slow_here))
    def _():
        back[slow, :SHARED] = jnp.zeros((SHARED,) + back.shape[2:], jnp.float32)

    low_factor = jnp.where(level > 0, 0.5, 0.0)
    high_factor = jnp.where(level < slabs - 1, 0.5, 0.0)

    def put_edges(slot, low, high):
        low = low.astype(jnp.float32) * low_factor
        high = high.astype(jnp.float32) * high_factor
        for c in range(2):
            edges[slot, c, 0:HMAX] = low[c * HMAX : (c + 1) * HMAX]
            edges[slot, c, HMAX:EDGE] = high[c * HMAX : (c + 1) * HMAX]

    def take_near(side, j):
        waiter(near16.at[side, j], near_send.at[side], near_recv.at[side, j]).wait_recv()
        for c in range(2):
            wide = near16[side, j, c].astype(jnp.float32) * 0.5
            field[2 * frames + frames * side + j, c] = wide

    def take_far(side):
        waiter(near_edge.at[side], far_send.at[side], far_recv.at[side]).wait_recv()
        for j in range(frames):
            frame = frame_at(1 - side, j)
            slot = 2 * frames + frames * side + j
            put_edges(slot, near_edge[side, 0, frame], near_edge[side, 1, frame])

    def take_more(j):
        waiter(more16.at[j], more_send, more_recv.at[j]).wait_recv()
        for c in range(2):
            field[4 * frames + j, c] = more16[j, c].astype(jnp.float32) * 0.5

    def take_rest():
        waiter(more_edge, rest_send, rest_recv).wait_recv()
        for j in range(SHARED):
            k = SHARED - 1 - j + slow * (2 * j - SHARED + 1)
            put_edges(4 * frames + j, more_edge[0, k], more_edge[1, k])

    def finish(place, part, y, x, weight):
        phase = signed_phase(y, x, weight)
        early, late = place
        first, second = total[early, part] + phase, total[late, part] + phase
        total[early, part] = first
        total[late, part] = second

    def inner_unit(n, q):
        c, s = q // 2, q % 2
        rows = ((0, 1 + c), (1, 2 + c) if c < 4 else (4, 5), (2, 3 + c) if c < 3 else (3, 1 + c))
        first, last = (
            jnp.where(n == 0, rows[0][i], jnp.where(n == 1, rows[1][i], rows[2][i])) for i in range(2)
        )
        return 2 * first + s, 2 * last + s, scaled[last - first - 1]

    def outer_unit(side, v, weight_at):
        j = sum(at_least(v, bound) for bound in (6, 11, 15, 18, 20))
        e = v - (6 * j - (j * (j - 1)) // 2)
        mine = 2 * frame_at(side, e) + 1 - side
        theirs = 2 * frames + frames * side + j
        early = theirs + side * (mine - theirs)
        late = mine + side * (theirs - mine)
        return early, late, scaled[weight_at + j + e]

    def middles(units, base):
        results = []
        for q in range(len(units) + 2):
            if q < len(units):
                early, late, _ = units[q]
                parts = split_products(
                    (field[early, 0], field[early, 1]), (field[late, 0], field[late, 1])
                )
                results.append(
                    jnp.dot(
                        window[:, : 4 * depth],
                        jnp.concatenate(parts, axis=0),
                        preferred_element_type=jnp.float32,
                    )
                )
            if q >= 2:
                early, late, weight = units[q - 2]
                real, imag = results[q - 2][:depth], results[q - 2][depth:]
                for c, value in enumerate((real, imag)):
                    held[base + q - 2, c, 0:HMAX] = value[:HMAX]
                    held[base + q - 2, c, HMAX:EDGE] = value[depth - HMAX :]
                for g in range(HMAX, depth - HMAX, 16):
                    finish(
                        (early, late), pl.ds(g, 16), imag[g : g + 16], real[g : g + 16], weight
                    )

    def rims(units, base):
        results = []
        for start in range(0, len(units), 4):
            group = units[start : start + 4]
            parts = []
            for early, late, _ in group:
                parts += split_products(
                    (edges[early, 0], edges[early, 1]), (edges[late, 0], edges[late, 1])
                )
            rows, columns = 2 * EDGE * len(group), 4 * EDGE * len(group)
            result = jnp.dot(
                edge_window[:rows, :columns],
                jnp.concatenate(parts, axis=0),
                preferred_element_type=jnp.float32,
            )
            results += [result[2 * EDGE * k : 2 * EDGE * (k + 1)] for k in range(len(group))]
        for q, (early, late, weight) in enumerate(units):
            real = results[q][:EDGE] + held[base + q, 0]
            imag = results[q][EDGE:] + held[base + q, 1]
            finish((early, late), pl.ds(0, HMAX), imag[:HMAX], real[:HMAX], weight)
            finish((early, late), pl.ds(depth - HMAX, HMAX), imag[HMAX:], real[HMAX:], weight)

    def inner_middles(n, carry):
        middles([inner_unit(n, q) for q in range(INNER)], n * INNER)
        return carry

    def inner_rims(n, carry):
        rims([inner_unit(n, q) for q in range(INNER)], n * INNER)
        return carry

    def quick_middles(n, carry):
        for at, js in ((0, (0, 1)), (1, (2,)), (2, (3, 4, 5))):

            @pl.when(n == at)
            def _(js=js):
                for j in js:
                    take_near(quick, j)

        middles([outer_unit(quick, n * QUICK + q, 0) for q in range(QUICK)], 3 * INNER + n * QUICK)
        return carry

    def quick_rims(n, carry):
        rims([outer_unit(quick, n * QUICK + q, 0) for q in range(QUICK)], 3 * INNER + n * QUICK)
        return carry

    def slow_unit(j, e):
        mine = 2 * frame_at(slow, e) + 1 - slow
        theirs = 2 * frames + frames * slow + j
        early = theirs + slow * (mine - theirs)
        late = mine + slow * (theirs - mine)
        return early, late, scaled[LAGS + j + e]

    def last_unit(n, q):
        def pick(values):
            value = values[3]
            for k in (2, 1, 0):
                value = jnp.where(n == k, values[k], value)
            return value

        j = pick(((3, 4, 0, 1), (3, 4, 0, 1), (3, 5, 0, 2))[q])
        e = pick(((0, 0, 3, 3), (1, 1, 4, 4), (2, 0, 5, 3))[q])
        own = jnp.where(n < 2, 1 - slow, slow)
        mine = 2 * frame_at(slow, e) + own
        theirs = j + jnp.where(n < 2, 2 * frames + frames * slow, 4 * frames)
        early = theirs + slow * (mine - theirs)
        late = mine + slow * (theirs - mine)
        return early, late, scaled[LAGS + j + e]

    def wholes(units):
        results = []
        for q in range(len(units) + 2):
            if q < len(units):
                early, late, _ = units[q]
                parts = split_products(
                    (field[early, 0], field[early, 1]), (field[late, 0], field[late, 1])
                ) + split_products(
                    (edges[early, 0], edges[early, 1]), (edges[late, 0], edges[late, 1])
                )
                results.append(
                    jnp.dot(
                        window, jnp.concatenate(parts, axis=0), preferred_element_type=jnp.float32
                    )
                )
            if q >= 2:
                early, late, weight = units[q - 2]
                real, imag = results[q - 2][:depth], results[q - 2][depth:]
                for g in range(0, depth, 24):
                    finish(
                        (early, late), pl.ds(g, 24), imag[g : g + 24], real[g : g + 24], weight
                    )

    def last_step(n, carry):
        @pl.when((n == 0) & slow_here)
        def _():
            take_near(slow, 3)

        @pl.when((n == 1) & slow_here)
        def _():
            take_near(slow, 4)
            take_near(slow, 5)

        @pl.when((n == 2) & slow_here)
        def _():
            take_rest()
            take_more(0)

        @pl.when((n == 3) & slow_here)
        def _():
            take_more(1)
            take_more(2)

        wholes([last_unit(n, q) for q in range(UNITS)])
        return carry

    @pl.when(jnp.logical_not(slow_here))
    def _():
        def clear(j, carry):
            slot = 2 * frames + frames * slow + j
            field[slot] = jnp.zeros(field.shape[1:], jnp.float32)
            edges[slot] = jnp.zeros(edges.shape[1:], jnp.float32)
            return carry

        lax.fori_loop(0, frames, clear, 0)
        for j in range(SHARED):
            field[4 * frames + j] = jnp.zeros(field.shape[1:], jnp.float32)
            edges[4 * frames + j] = jnp.zeros(edges.shape[1:], jnp.float32)

    lax.fori_loop(0, 3, inner_middles, 0)
    lax.fori_loop(0, 3, quick_middles, 0)

    shared = [[slow_unit(j, e) for e in range(frames - j)] for j in range(SHARED)]
    bases = [3 * (INNER + QUICK) + sum(map(len, shared[:j])) for j in range(SHARED)]
    for j, base in enumerate(bases):

        @if_slow
        def _(j=j):
            take_near(slow, j)

        middles(shared[j], base)

    @if_slow
    def _():
        back_copy(slow, SHARED, pl.ds(HMAX, depth - EDGE)).start()

    waiter(edge_in, edge_send, edge_recv).wait_recv()
    halo_copy().start()
    for f in range(frames):
        for s in range(2):
            lanes = pl.ds(s * strip, strip)
            put_edges(2 * f + s, edge_in[0, f, :, lanes], edge_in[1, f, :, lanes])

    edge_window = edge_band[...].astype(jnp.bfloat16)

    @if_slow
    def _():
        take_far(slow)

    for j, base in enumerate(bases):
        rims(shared[j], base)

    @if_slow
    def _():
        for at in (0, depth - HMAX):
            back_copy(slow, SHARED, pl.ds(at, HMAX)).start()

    take_far(quick)
    lax.fori_loop(0, 3, quick_rims, 0)
    back_copy(quick, frames, pl.ds(0, depth)).start()
    lax.fori_loop(0, 3, inner_rims, 0)

    frame_total = frames * blocks

    def write(side):
        lanes = cut(side)

        def write_frame(f, carry):
            now = me * frames + f
            norm = jnp.float32(0.0)
            for lag in range(1, LAGS + 1):
                count = at_least(frame_total - 1, now + lag) + at_least(now, lag)
                norm = norm + scaled[lag - 1] * count.astype(jnp.float32)
            inverse = 1.0 / jnp.full((8, strip), norm, jnp.float32)
            j = frame_at(side, f)
            slot = 2 * f + side
            for g in range(0, depth, 8):
                part = pl.ds(g, 8)
                out[f, part, lanes] = (total[slot, part] + back[side, j, part]) * inverse
            return carry

        lax.fori_loop(0, frames, write_frame, 0)

    lax.fori_loop(0, 2, last_step, 0)
    waiter(back.at[quick], back_send.at[quick], back_recv.at[quick]).wait()
    write(quick)
    lax.fori_loop(2, 4, last_step, 0)

    @if_slow
    def _():
        waiter(back.at[slow, pl.ds(0, SHARED)], back_send.at[slow], back_recv.at[slow]).wait()

    write(slow)

    @if_slow
    def _():
        waiter(more_edge, rest_send, rest_recv).wait_send()
        waiter(more16, more_send, more_send).wait_send()

    waiter(edge_out, edge_send, edge_recv).wait_send()
    for side, here in ((quick, True), (slow, slow_here)):

        @pl.when(here)
        def _(side=side):
            waiter(near_edge.at[side], far_send.at[side], far_recv.at[side]).wait_send()
            waiter(near16.at[side], near_send.at[side], near_send.at[side]).wait_send()


def shards(iq, half, weights):
    _, frames, depth, lines = iq.shape
    strip = lines // 2
    slots = 4 * frames + SHARED
    wide, thin = jnp.float32, jnp.bfloat16
    dma = pltpu.SemaphoreType.DMA
    return pl.pallas_call(
        kernel,
        out_shape=pltpu.VMEM((frames, depth, lines), wide),
        in_specs=[pl.BlockSpec(memory_space=pltpu.HBM)] * 3,
        out_specs=pl.BlockSpec(memory_space=pltpu.VMEM),
        scratch_shapes=[
            pltpu.SMEM(half.shape, jnp.int32),
            pltpu.SMEM(weights.shape, jnp.int32),
            pltpu.SMEM((2 * LAGS,), wide),
            pltpu.VMEM((2, frames, depth, lines), thin),
            pltpu.VMEM((2, frames, EDGE, lines), thin),
            pltpu.VMEM((2, frames, EDGE, lines), thin),
            pltpu.VMEM((2, frames, 2, depth, strip), thin),
            pltpu.VMEM((2, 2, frames, EDGE, strip), thin),
            pltpu.VMEM((SHARED, 2, depth, strip), thin),
            pltpu.VMEM((2, SHARED, EDGE, strip), thin),
            pltpu.VMEM((slots, 2, depth, strip), wide),
            pltpu.VMEM((slots, 2, EDGE, strip), wide),
            pltpu.VMEM((slots, depth, strip), wide),
            pltpu.VMEM((3 * (INNER + QUICK) + SHARED_STRIPS, 2, EDGE, strip), wide),
            pltpu.VMEM((2 * depth, 4 * (depth + EDGE)), wide),
            pltpu.VMEM((8 * EDGE, 16 * EDGE), wide),
            pltpu.VMEM((2, frames, depth, strip), wide),
            dma(()),
            dma((2,)),
            dma(()),
            dma(()),
            dma((2,)),
            dma((2, frames)),
            dma((2,)),
            dma((2,)),
            dma(()),
            dma((SHARED,)),
            dma(()),
            dma(()),
            dma((2,)),
            dma((2,)),
        ],
        compiler_params=pltpu.CompilerParams(
            collective_id=0, has_side_effects=True, vmem_limit_bytes=48 * 1024 * 1024
        ),
        name="pair_phases",
    )(*(pltpu.with_memory_space_constraint(x, pltpu.HBM) for x in (iq, half, weights)))


def solution(mesh):
    placed = (P(None, "tm", "depth", None), P("depth"), P())
    return jax.shard_map(
        shards, mesh=mesh, in_specs=placed, out_specs=P("tm", "depth", None), check_vma=False
    )
```

```python
import functools

import jax
import jax.numpy as jnp
import numpy as np
from jax import lax
from jax.experimental import pallas as pl
from jax.experimental.pallas import tpu as pltpu
from jax.sharding import PartitionSpec as P

LAGS = 6
HMAX = 8
HALF_PI = float(np.float32(np.pi / 2))
PI = float(np.float32(np.pi))
TINY = 1.1754944e-38
ATAN = (
    0.9999960660934448,
    -0.33301785588264465,
    0.19582265615463257,
    -0.12176322191953659,
    0.05807745084166527,
    -0.0137208616361022,
)
MESH = pl.DeviceIdType.MESH
UNITS = 3
INNER = 10
QUICK = 7
EDGE = 2 * HMAX
SHARED = 3
SHARED_STRIPS = 15


def at_least(value, bound):
    return (value >= bound).astype(jnp.int32)


def signed_phase(y, x, weight):
    ax = jnp.abs(x)
    ay = jnp.abs(y)
    high = jnp.maximum(jnp.maximum(ax, ay), TINY)
    t = jnp.minimum(ax, ay) * pltpu.reciprocal(high, approx=True)
    s = t * t
    poly = ATAN[-1] * s + ATAN[-2]
    for coefficient in ATAN[-3::-1]:
        poly = poly * s + coefficient
    angle = poly * t
    angle = jnp.where(ay > ax, HALF_PI - angle, angle)
    angle = jnp.where(x < 0, PI - angle, angle)
    return angle * jnp.where(y < 0, -weight, weight)


def split_products(early, late):
    parts = []
    (ar, ai), (br, bi) = early, late
    for value in (br * ar + bi * ai, bi * ar - br * ai):
        high = value.astype(jnp.bfloat16)
        low = (value - high.astype(jnp.float32)).astype(jnp.bfloat16)
        parts += [high, low]
    return parts


def kernel(
    iq_any, half_any, weights_any, out,
    half, weights, scaled, own16, edge_out, edge_in, near16, near_edge, more16, more_edge,
    field, edges, total, held, band, edge_band, back,
    load_sem, small_sem, edge_send, edge_recv, near_send, near_recv, far_send, far_recv, halo_send, halo_recv,
    more_send, more_recv, rest_send, rest_recv, back_send, back_recv,
):
    frames, depth, lines = own16.shape[1:]
    strip = lines // 2
    me, level = lax.axis_index("tm"), lax.axis_index("depth")
    blocks, slabs = lax.axis_size("tm"), lax.axis_size("depth")
    left, right = lax.rem(me + blocks - 1, blocks), lax.rem(me + 1, blocks)
    below, above = lax.rem(level + slabs - 1, slabs), lax.rem(level + 1, slabs)
    slow = lax.rem(me, 2)
    quick = 1 - slow
    beside = (me > 0, me < blocks - 1)
    slab_at = (level > 0, level < slabs - 1)
    target = me - 1 + 2 * slow
    slow_here = (target >= 0) & (target < blocks)

    load = pltpu.make_async_copy(iq_any, own16, load_sem)
    load.start()
    small = [
        pltpu.make_async_copy(half_any, half, small_sem.at[0]),
        pltpu.make_async_copy(weights_any, weights, small_sem.at[1]),
    ]
    for copy in small:
        copy.start()
    barrier = pltpu.get_barrier_semaphore()
    for way, other in enumerate((below, above)):

        @pl.when(slab_at[way])
        def _(other=other):
            pl.semaphore_signal(barrier, inc=1, device_id=(me, other), device_id_type=MESH)

    for side, column in enumerate((left, right)):

        @pl.when(beside[side])
        def _(column=column):
            pl.semaphore_signal(barrier, inc=1, device_id=(column, level), device_id_type=MESH)

        for way, other in enumerate((below, above)):

            @pl.when(beside[side] & slab_at[way])
            def _(column=column, other=other):
                pl.semaphore_signal(barrier, inc=1, device_id=(column, other), device_id_type=MESH)

    def cut(side):
        return pl.ds(pl.multiple_of(side * strip, strip), strip)

    def next_to(side):
        return lax.rem(me + blocks - 1 + 2 * side, blocks)

    def frame_at(side, j):
        return j + side * (frames - 1 - 2 * j)

    def edge_copy(way):
        return pltpu.make_async_remote_copy(
            src_ref=edge_out.at[way],
            dst_ref=edge_in.at[1 - way],
            send_sem=edge_send.at[way],
            recv_sem=edge_recv.at[1 - way],
            device_id=(me, below if way == 0 else above),
            device_id_type=MESH,
        )

    def near_copy(side, j):
        return pltpu.make_async_remote_copy(
            src_ref=iq_any.at[:, frame_at(side, j), :, cut(side)],
            dst_ref=near16.at[1 - side, j],
            send_sem=near_send.at[side],
            recv_sem=near_recv.at[1 - side, j],
            device_id=(next_to(side), level),
            device_id_type=MESH,
        )

    def far_copy(way):
        return pltpu.make_async_remote_copy(
            src_ref=edge_out.at[way, :, :, cut(slow)],
            dst_ref=near_edge.at[1 - slow, 1 - way],
            send_sem=far_send.at[way],
            recv_sem=far_recv.at[1 - way],
            device_id=(next_to(slow), below if way == 0 else above),
            device_id_type=MESH,
        )

    def more_copy(j):
        return pltpu.make_async_remote_copy(
            src_ref=own16.at[:, frame_at(slow, j), :, cut(quick)],
            dst_ref=more16.at[j],
            send_sem=more_send,
            recv_sem=more_recv.at[j],
            device_id=(next_to(slow), level),
            device_id_type=MESH,
        )

    def rest_copy(way):
        return pltpu.make_async_remote_copy(
            src_ref=edge_out.at[way, pl.ds(slow * (frames - SHARED), SHARED), :, cut(quick)],
            dst_ref=more_edge.at[1 - way],
            send_sem=rest_send.at[way],
            recv_sem=rest_recv.at[1 - way],
            device_id=(next_to(slow), below if way == 0 else above),
            device_id_type=MESH,
        )

    def halo_copy():
        return pltpu.make_async_remote_copy(
            src_ref=edge_in.at[:, :, :, cut(quick)],
            dst_ref=near_edge.at[1 - quick],
            send_sem=halo_send,
            recv_sem=halo_recv,
            device_id=(next_to(quick), level),
            device_id_type=MESH,
        )

    def back_copy(side, count, part):
        first = 2 * frames + frames * side
        return pltpu.make_async_remote_copy(
            src_ref=total.at[pl.ds(first, count), part],
            dst_ref=back.at[1 - side, pl.ds(0, count), part],
            send_sem=back_send.at[side],
            recv_sem=back_recv.at[1 - side],
            device_id=(next_to(side), level),
            device_id_type=MESH,
        )

    def waiter(ref, send, recv):
        return pltpu.make_async_remote_copy(
            src_ref=ref, dst_ref=ref, send_sem=send, recv_sem=recv,
            device_id=(me, above), device_id_type=MESH,
        )

    def if_slow(act):
        pl.when(slow_here)(act)

    total[...] = jnp.zeros_like(total)
    columns = sum(here.astype(jnp.int32) for here in beside)
    others = sum(here.astype(jnp.int32) for here in slab_at)
    pl.semaphore_wait(barrier, others + columns * (1 + others))

    @if_slow
    def _():
        for j in range(SHARED):
            near_copy(slow, j).start()

    load.wait()

    for f in range(frames):
        first, last = [], []
        for c in range(2):
            wide = own16[c, f].astype(jnp.float32)
            first.append(wide[:HMAX])
            last.append(wide[depth - HMAX :])
        edge_out[0, f] = jnp.concatenate(first, axis=0).astype(jnp.bfloat16)
        edge_out[1, f] = jnp.concatenate(last, axis=0).astype(jnp.bfloat16)


    for way in range(2):

        @pl.when(slow_here & slab_at[way])
        def _(way=way):
            far_copy(way).start()


    for way in range(2):

        @pl.when(slab_at[way])
        def _(way=way):
            edge_copy(way).start()

        @pl.when(jnp.logical_not(slab_at[way]))
        def _(way=way):
            edge_in[way] = jnp.zeros(edge_in.shape[1:], jnp.bfloat16)
            near_edge[slow, way] = jnp.zeros(near_edge.shape[2:], jnp.bfloat16)
            more_edge[way] = jnp.zeros(more_edge.shape[1:], jnp.bfloat16)

    @if_slow
    def _():
        for j in range(SHARED, frames):
            near_copy(slow, j).start()

    for way in range(2):

        @pl.when(slow_here & slab_at[way])
        def _(way=way):
            rest_copy(way).start()

    @if_slow
    def _():
        for j in range(SHARED):
            more_copy(j).start()

    for j in range(frames):
        near_copy(quick, j).start()

    for copy in small:
        copy.wait()
    for lag in range(LAGS):
        value = weights[lag].astype(jnp.float32)
        scaled[lag] = value
        scaled[LAGS + lag] = value * jnp.where(slow_here, 1.0, 0.0)
    sub = lax.broadcasted_iota(jnp.int32, (8, 4 * (depth + EDGE)), 0)
    column = lax.broadcasted_iota(jnp.int32, (8, 4 * (depth + EDGE)), 1)
    halo = lax.rem(column, EDGE)
    halo = jnp.where(halo < HMAX, halo - HMAX, halo - HMAX + depth)
    inside = column < 4 * depth
    place = jnp.where(inside, lax.rem(column, depth), halo)
    upper = column < jnp.where(inside, 2 * depth, 4 * depth + 2 * EDGE)
    reach = []
    for g in range(0, depth, 8):
        value = jnp.full(sub.shape, half[g], jnp.int32)
        for r in range(1, 8):
            value = jnp.where(sub == r, half[g + r], value)
        reach.append(value)
        keep = jnp.abs(place - (sub + g)) <= value
        band[g : g + 8] = jnp.where(keep & upper, 1.0, 0.0)
        band[depth + g : depth + g + 8] = jnp.where(keep & jnp.logical_not(upper), 1.0, 0.0)
    which = column // (2 * EDGE)
    for block in range(16):
        g = 0 if block % 2 == 0 else depth - 8
        keep = jnp.abs(halo - (sub + g)) <= reach[g // 8]
        edge_band[block * 8 : block * 8 + 8] = jnp.where(keep & (which == block // 2), 1.0, 0.0)
    window = band[...].astype(jnp.bfloat16)

    def own_field(f, carry):
        for c in range(2):
            wide = own16[c, f].astype(jnp.float32) * 0.5
            for s in range(2):
                field[2 * f + s, c] = wide[:, s * strip : (s + 1) * strip]
        return carry

    lax.fori_loop(0, frames, own_field, 0)
    back[slow, SHARED:] = jnp.zeros((frames - SHARED,) + back.shape[2:], jnp.float32)

    @pl.when(jnp.logical_not(slow_here))
    def _():
        back[slow, :SHARED] = jnp.zeros((SHARED,) + back.shape[2:], jnp.float32)

    low_factor = jnp.where(level > 0, 0.5, 0.0)
    high_factor = jnp.where(level < slabs - 1, 0.5, 0.0)

    def put_edges(slot, low, high):
        low = low.astype(jnp.float32) * low_factor
        high = high.astype(jnp.float32) * high_factor
        for c in range(2):
            edges[slot, c, 0:HMAX] = low[c * HMAX : (c + 1) * HMAX]
            edges[slot, c, HMAX:EDGE] = high[c * HMAX : (c + 1) * HMAX]

    def take_near(side, j):
        waiter(near16.at[side, j], near_send.at[side], near_recv.at[side, j]).wait_recv()
        for c in range(2):
            wide = near16[side, j, c].astype(jnp.float32) * 0.5
            field[2 * frames + frames * side + j, c] = wide

    def wait_ways(refs, send, recv):
        for way in range(2):

            @pl.when(slab_at[way])
            def _(way=way):
                waiter(refs.at[way], send.at[way], recv.at[way]).wait_recv()

    def sent_ways(refs, send):
        for way in range(2):

            @pl.when(slab_at[way])
            def _(way=way):
                waiter(refs.at[way], send.at[way], send.at[way]).wait_send()

    def take_far(side):
        for j in range(frames):
            frame = frame_at(1 - side, j)
            slot = 2 * frames + frames * side + j
            put_edges(slot, near_edge[side, 0, frame], near_edge[side, 1, frame])

    def take_more(j):
        waiter(more16.at[j], more_send, more_recv.at[j]).wait_recv()
        for c in range(2):
            field[4 * frames + j, c] = more16[j, c].astype(jnp.float32) * 0.5

    def take_rest():
        wait_ways(more_edge, rest_send, rest_recv)
        for j in range(SHARED):
            k = SHARED - 1 - j + slow * (2 * j - SHARED + 1)
            put_edges(4 * frames + j, more_edge[0, k], more_edge[1, k])

    def finish(place, part, y, x, weight):
        phase = signed_phase(y, x, weight)
        early, late = place
        first, second = total[early, part] + phase, total[late, part] + phase
        total[early, part] = first
        total[late, part] = second

    def inner_unit(n, q):
        c, s = q // 2, q % 2
        rows = ((0, 1 + c), (1, 2 + c) if c < 4 else (4, 5), (2, 3 + c) if c < 3 else (3, 1 + c))
        first, last = (
            jnp.where(n == 0, rows[0][i], jnp.where(n == 1, rows[1][i], rows[2][i])) for i in range(2)
        )
        return 2 * first + s, 2 * last + s, scaled[last - first - 1]

    def outer_unit(side, v, weight_at):
        j = sum(at_least(v, bound) for bound in (6, 11, 15, 18, 20))
        e = v - (6 * j - (j * (j - 1)) // 2)
        mine = 2 * frame_at(side, e) + 1 - side
        theirs = 2 * frames + frames * side + j
        early = theirs + side * (mine - theirs)
        late = mine + side * (theirs - mine)
        return early, late, scaled[weight_at + j + e]

    def middles(units, base):
        results = []
        for q in range(len(units) + 2):
            if q < len(units):
                early, late, _ = units[q]
                parts = split_products(
                    (field[early, 0], field[early, 1]), (field[late, 0], field[late, 1])
                )
                results.append(
                    jnp.dot(
                        window[:, : 4 * depth],
                        jnp.concatenate(parts, axis=0),
                        preferred_element_type=jnp.float32,
                    )
                )
            if q >= 2:
                early, late, weight = units[q - 2]
                real, imag = results[q - 2][:depth], results[q - 2][depth:]
                for c, value in enumerate((real, imag)):
                    held[base + q - 2, c, 0:HMAX] = value[:HMAX]
                    held[base + q - 2, c, HMAX:EDGE] = value[depth - HMAX :]
                for g in range(HMAX, depth - HMAX, 16):
                    finish(
                        (early, late), pl.ds(g, 16), imag[g : g + 16], real[g : g + 16], weight
                    )

    def rims(units, base):
        results = []
        for start in range(0, len(units), 4):
            group = units[start : start + 4]
            parts = []
            for early, late, _ in group:
                parts += split_products(
                    (edges[early, 0], edges[early, 1]), (edges[late, 0], edges[late, 1])
                )
            rows, columns = 2 * EDGE * len(group), 4 * EDGE * len(group)
            result = jnp.dot(
                edge_window[:rows, :columns],
                jnp.concatenate(parts, axis=0),
                preferred_element_type=jnp.float32,
            )
            results += [result[2 * EDGE * k : 2 * EDGE * (k + 1)] for k in range(len(group))]
        for q, (early, late, weight) in enumerate(units):
            real = results[q][:EDGE] + held[base + q, 0]
            imag = results[q][EDGE:] + held[base + q, 1]
            finish((early, late), pl.ds(0, HMAX), imag[:HMAX], real[:HMAX], weight)
            finish((early, late), pl.ds(depth - HMAX, HMAX), imag[HMAX:], real[HMAX:], weight)

    def inner_middles(n, carry):
        middles([inner_unit(n, q) for q in range(INNER)], n * INNER)
        return carry

    def inner_rims(n, carry):
        rims([inner_unit(n, q) for q in range(INNER)], n * INNER)
        return carry

    def quick_middles(n, carry):
        for at, js in ((0, (0, 1)), (1, (2,)), (2, (3, 4, 5))):

            @pl.when(n == at)
            def _(js=js):
                for j in js:
                    take_near(quick, j)

        middles([outer_unit(quick, n * QUICK + q, 0) for q in range(QUICK)], 3 * INNER + n * QUICK)
        return carry

    def quick_rims(n, carry):
        rims([outer_unit(quick, n * QUICK + q, 0) for q in range(QUICK)], 3 * INNER + n * QUICK)
        return carry

    def slow_unit(j, e):
        mine = 2 * frame_at(slow, e) + 1 - slow
        theirs = 2 * frames + frames * slow + j
        early = theirs + slow * (mine - theirs)
        late = mine + slow * (theirs - mine)
        return early, late, scaled[LAGS + j + e]

    def last_unit(n, q):
        def pick(values):
            value = values[3]
            for k in (2, 1, 0):
                value = jnp.where(n == k, values[k], value)
            return value

        j = pick(((3, 4, 0, 1), (3, 4, 0, 1), (3, 5, 0, 2))[q])
        e = pick(((0, 0, 3, 3), (1, 1, 4, 4), (2, 0, 5, 3))[q])
        own = jnp.where(n < 2, 1 - slow, slow)
        mine = 2 * frame_at(slow, e) + own
        theirs = j + jnp.where(n < 2, 2 * frames + frames * slow, 4 * frames)
        early = theirs + slow * (mine - theirs)
        late = mine + slow * (theirs - mine)
        return early, late, scaled[LAGS + j + e]

    def wholes(units):
        results = []
        for q in range(len(units) + 2):
            if q < len(units):
                early, late, _ = units[q]
                parts = split_products(
                    (field[early, 0], field[early, 1]), (field[late, 0], field[late, 1])
                ) + split_products(
                    (edges[early, 0], edges[early, 1]), (edges[late, 0], edges[late, 1])
                )
                results.append(
                    jnp.dot(
                        window, jnp.concatenate(parts, axis=0), preferred_element_type=jnp.float32
                    )
                )
            if q >= 2:
                early, late, weight = units[q - 2]
                real, imag = results[q - 2][:depth], results[q - 2][depth:]
                for g in range(0, depth, 24):
                    finish(
                        (early, late), pl.ds(g, 24), imag[g : g + 24], real[g : g + 24], weight
                    )

    def last_step(n, carry):
        @pl.when((n == 0) & slow_here)
        def _():
            take_near(slow, 3)

        @pl.when((n == 1) & slow_here)
        def _():
            take_near(slow, 4)
            take_near(slow, 5)

        @pl.when((n == 2) & slow_here)
        def _():
            take_rest()
            take_more(0)

        @pl.when((n == 3) & slow_here)
        def _():
            take_more(1)
            take_more(2)

        wholes([last_unit(n, q) for q in range(UNITS)])
        return carry

    @pl.when(jnp.logical_not(slow_here))
    def _():
        def clear(j, carry):
            slot = 2 * frames + frames * slow + j
            field[slot] = jnp.zeros(field.shape[1:], jnp.float32)
            edges[slot] = jnp.zeros(edges.shape[1:], jnp.float32)
            return carry

        lax.fori_loop(0, frames, clear, 0)
        for j in range(SHARED):
            field[4 * frames + j] = jnp.zeros(field.shape[1:], jnp.float32)
            edges[4 * frames + j] = jnp.zeros(edges.shape[1:], jnp.float32)

    lax.fori_loop(0, 3, inner_middles, 0)
    lax.fori_loop(0, 3, quick_middles, 0)

    shared = [[slow_unit(j, e) for e in range(frames - j)] for j in range(SHARED)]
    bases = [3 * (INNER + QUICK) + sum(map(len, shared[:j])) for j in range(SHARED)]
    for j, base in enumerate(bases):

        @if_slow
        def _(j=j):
            take_near(slow, j)

        middles(shared[j], base)

    @if_slow
    def _():
        back_copy(slow, SHARED, pl.ds(HMAX, depth - EDGE)).start()

    wait_ways(edge_in, edge_send, edge_recv)
    halo_copy().start()
    for f in range(frames):
        for s in range(2):
            lanes = pl.ds(s * strip, strip)
            put_edges(2 * f + s, edge_in[0, f, :, lanes], edge_in[1, f, :, lanes])

    edge_window = edge_band[...].astype(jnp.bfloat16)

    @if_slow
    def _():
        wait_ways(near_edge.at[slow], far_send, far_recv)
        take_far(slow)

    for j, base in enumerate(bases):
        rims(shared[j], base)

    @if_slow
    def _():
        for at in (0, depth - HMAX):
            back_copy(slow, SHARED, pl.ds(at, HMAX)).start()

    waiter(near_edge.at[quick], halo_send, halo_recv).wait_recv()
    take_far(quick)
    lax.fori_loop(0, 3, quick_rims, 0)
    back_copy(quick, frames, pl.ds(0, depth)).start()
    lax.fori_loop(0, 3, inner_rims, 0)

    frame_total = frames * blocks

    def write(side):
        lanes = cut(side)

        def write_frame(f, carry):
            now = me * frames + f
            norm = jnp.float32(0.0)
            for lag in range(1, LAGS + 1):
                count = at_least(frame_total - 1, now + lag) + at_least(now, lag)
                norm = norm + scaled[lag - 1] * count.astype(jnp.float32)
            inverse = 1.0 / jnp.full((8, strip), norm, jnp.float32)
            j = frame_at(side, f)
            slot = 2 * f + side
            for g in range(0, depth, 8):
                part = pl.ds(g, 8)
                out[f, part, lanes] = (total[slot, part] + back[side, j, part]) * inverse
            return carry

        lax.fori_loop(0, frames, write_frame, 0)

    lax.fori_loop(0, 2, last_step, 0)
    waiter(back.at[quick], back_send.at[quick], back_recv.at[quick]).wait()
    write(quick)
    lax.fori_loop(2, 4, last_step, 0)

    @if_slow
    def _():
        waiter(back.at[slow, pl.ds(0, SHARED)], back_send.at[slow], back_recv.at[slow]).wait()

    write(slow)

    @if_slow
    def _():
        sent_ways(more_edge, rest_send)
        sent_ways(near_edge.at[slow], far_send)
        waiter(more16, more_send, more_send).wait_send()
        waiter(near16.at[slow], near_send.at[slow], near_send.at[slow]).wait_send()

    sent_ways(edge_out, edge_send)
    waiter(near_edge.at[quick], halo_send, halo_send).wait_send()
    waiter(near16.at[quick], near_send.at[quick], near_send.at[quick]).wait_send()


def shards(iq, half, weights):
    _, frames, depth, lines = iq.shape
    strip = lines // 2
    slots = 4 * frames + SHARED
    wide, thin = jnp.float32, jnp.bfloat16
    dma = pltpu.SemaphoreType.DMA
    return pl.pallas_call(
        kernel,
        out_shape=pltpu.VMEM((frames, depth, lines), wide),
        in_specs=[pl.BlockSpec(memory_space=pltpu.HBM)] * 3,
        out_specs=pl.BlockSpec(memory_space=pltpu.VMEM),
        scratch_shapes=[
            pltpu.SMEM(half.shape, jnp.int32),
            pltpu.SMEM(weights.shape, jnp.int32),
            pltpu.SMEM((2 * LAGS,), wide),
            pltpu.VMEM((2, frames, depth, lines), thin),
            pltpu.VMEM((2, frames, EDGE, lines), thin),
            pltpu.VMEM((2, frames, EDGE, lines), thin),
            pltpu.VMEM((2, frames, 2, depth, strip), thin),
            pltpu.VMEM((2, 2, frames, EDGE, strip), thin),
            pltpu.VMEM((SHARED, 2, depth, strip), thin),
            pltpu.VMEM((2, SHARED, EDGE, strip), thin),
            pltpu.VMEM((slots, 2, depth, strip), wide),
            pltpu.VMEM((slots, 2, EDGE, strip), wide),
            pltpu.VMEM((slots, depth, strip), wide),
            pltpu.VMEM((3 * (INNER + QUICK) + SHARED_STRIPS, 2, EDGE, strip), wide),
            pltpu.VMEM((2 * depth, 4 * (depth + EDGE)), wide),
            pltpu.VMEM((8 * EDGE, 16 * EDGE), wide),
            pltpu.VMEM((2, frames, depth, strip), wide),
            dma(()),
            dma((2,)),
            dma((2,)),
            dma((2,)),
            dma((2,)),
            dma((2, frames)),
            dma((2,)),
            dma((2,)),
            dma(()),
            dma(()),
            dma(()),
            dma((SHARED,)),
            dma((2,)),
            dma((2,)),
            dma((2,)),
            dma((2,)),
        ],
        compiler_params=pltpu.CompilerParams(
            collective_id=0, has_side_effects=True, vmem_limit_bytes=48 * 1024 * 1024
        ),
        name="pair_phases",
    )(*(pltpu.with_memory_space_constraint(x, pltpu.HBM) for x in (iq, half, weights)))


def solution(mesh):
    placed = (P(None, "tm", "depth", None), P("depth"), P())
    return jax.shard_map(
        shards, mesh=mesh, in_specs=placed, out_specs=P("tm", "depth", None), check_vma=False
    )
```

```python
import functools

import jax
import jax.numpy as jnp
import numpy as np
from jax import lax
from jax.experimental import pallas as pl
from jax.experimental.pallas import tpu as pltpu
from jax.sharding import PartitionSpec as P

LAGS = 6
HMAX = 8
HALF_PI = float(np.float32(np.pi / 2))
PI = float(np.float32(np.pi))
TINY = 1.1754944e-38
ATAN = (
    0.9999960660934448,
    -0.33301785588264465,
    0.19582265615463257,
    -0.12176322191953659,
    0.05807745084166527,
    -0.0137208616361022,
)
MESH = pl.DeviceIdType.MESH
UNITS = 3
INNER = 10
QUICK = 7
EDGE = 2 * HMAX
SHARED = 3
SHARED_STRIPS = 15


def at_least(value, bound):
    return (value >= bound).astype(jnp.int32)


def signed_phase(y, x, weight):
    ax = jnp.abs(x)
    ay = jnp.abs(y)
    high = jnp.maximum(jnp.maximum(ax, ay), TINY)
    t = jnp.minimum(ax, ay) * pltpu.reciprocal(high, approx=True)
    s = t * t
    poly = ATAN[-1] * s + ATAN[-2]
    for coefficient in ATAN[-3::-1]:
        poly = poly * s + coefficient
    angle = poly * t
    angle = jnp.where(ay > ax, HALF_PI - angle, angle)
    angle = jnp.where(x < 0, PI - angle, angle)
    return angle * jnp.where(y < 0, -weight, weight)


def split_products(early, late):
    parts = []
    (ar, ai), (br, bi) = early, late
    for value in (br * ar + bi * ai, bi * ar - br * ai):
        high = value.astype(jnp.bfloat16)
        low = (value - high.astype(jnp.float32)).astype(jnp.bfloat16)
        parts += [high, low]
    return parts


def kernel(
    iq_any, half_any, weights_any, out,
    half, weights, scaled, own16, edge_out, edge_in, near16, near_edge, more16, more_edge,
    field, edges, total, held, band, edge_band, back,
    load_sem, small_sem, edge_send, edge_recv, near_send, near_recv, far_send, far_recv, halo_send, halo_recv,
    more_send, more_recv, rest_send, rest_recv, back_send, back_recv,
):
    frames, depth, lines = own16.shape[1:]
    strip = lines // 2
    me, level = lax.axis_index("tm"), lax.axis_index("depth")
    blocks, slabs = lax.axis_size("tm"), lax.axis_size("depth")
    left, right = lax.rem(me + blocks - 1, blocks), lax.rem(me + 1, blocks)
    below, above = lax.rem(level + slabs - 1, slabs), lax.rem(level + 1, slabs)
    slow = lax.rem(me, 2)
    quick = 1 - slow
    beside = (me > 0, me < blocks - 1)
    slab_at = (level > 0, level < slabs - 1)
    target = me - 1 + 2 * slow
    slow_here = (target >= 0) & (target < blocks)

    load = pltpu.make_async_copy(iq_any, own16, load_sem)
    load.start()
    small = [
        pltpu.make_async_copy(half_any, half, small_sem.at[0]),
        pltpu.make_async_copy(weights_any, weights, small_sem.at[1]),
    ]
    for copy in small:
        copy.start()
    barrier = pltpu.get_barrier_semaphore()
    for way, other in enumerate((below, above)):

        @pl.when(slab_at[way])
        def _(other=other):
            pl.semaphore_signal(barrier, inc=1, device_id=(me, other), device_id_type=MESH)

    for side, column in enumerate((left, right)):

        @pl.when(beside[side])
        def _(column=column):
            pl.semaphore_signal(barrier, inc=1, device_id=(column, level), device_id_type=MESH)

        for way, other in enumerate((below, above)):

            @pl.when(beside[side] & slab_at[way])
            def _(column=column, other=other):
                pl.semaphore_signal(barrier, inc=1, device_id=(column, other), device_id_type=MESH)

    def cut(side):
        return pl.ds(pl.multiple_of(side * strip, strip), strip)

    def next_to(side):
        return lax.rem(me + blocks - 1 + 2 * side, blocks)

    def frame_at(side, j):
        return j + side * (frames - 1 - 2 * j)

    def edge_copy(way):
        return pltpu.make_async_remote_copy(
            src_ref=edge_out.at[way],
            dst_ref=edge_in.at[1 - way],
            send_sem=edge_send.at[way],
            recv_sem=edge_recv.at[1 - way],
            device_id=(me, below if way == 0 else above),
            device_id_type=MESH,
        )

    def near_copy(side, j):
        return pltpu.make_async_remote_copy(
            src_ref=iq_any.at[:, frame_at(side, j), :, cut(side)],
            dst_ref=near16.at[1 - side, j],
            send_sem=near_send.at[side],
            recv_sem=near_recv.at[1 - side, j],
            device_id=(next_to(side), level),
            device_id_type=MESH,
        )

    def part_of(side, part):
        return pl.ds((side + part - 2 * side * part) * SHARED, SHARED)

    def far_copy(way, part):
        return pltpu.make_async_remote_copy(
            src_ref=edge_out.at[way, part_of(slow, part), :, cut(slow)],
            dst_ref=near_edge.at[1 - slow, 1 - way, part_of(slow, part)],
            send_sem=far_send.at[part, way],
            recv_sem=far_recv.at[part, 1 - way],
            device_id=(next_to(slow), below if way == 0 else above),
            device_id_type=MESH,
        )

    def more_copy(j):
        return pltpu.make_async_remote_copy(
            src_ref=own16.at[:, frame_at(slow, j), :, cut(quick)],
            dst_ref=more16.at[j],
            send_sem=more_send,
            recv_sem=more_recv.at[j],
            device_id=(next_to(slow), level),
            device_id_type=MESH,
        )

    def rest_copy(way):
        return pltpu.make_async_remote_copy(
            src_ref=edge_out.at[way, pl.ds(slow * (frames - SHARED), SHARED), :, cut(quick)],
            dst_ref=more_edge.at[1 - way],
            send_sem=rest_send.at[way],
            recv_sem=rest_recv.at[1 - way],
            device_id=(next_to(slow), below if way == 0 else above),
            device_id_type=MESH,
        )

    def halo_copy():
        return pltpu.make_async_remote_copy(
            src_ref=edge_in.at[:, :, :, cut(quick)],
            dst_ref=near_edge.at[1 - quick],
            send_sem=halo_send,
            recv_sem=halo_recv,
            device_id=(next_to(quick), level),
            device_id_type=MESH,
        )

    def back_copy(side, count, part):
        first = 2 * frames + frames * side
        return pltpu.make_async_remote_copy(
            src_ref=total.at[pl.ds(first, count), part],
            dst_ref=back.at[1 - side, pl.ds(0, count), part],
            send_sem=back_send.at[side],
            recv_sem=back_recv.at[1 - side],
            device_id=(next_to(side), level),
            device_id_type=MESH,
        )

    def waiter(ref, send, recv):
        return pltpu.make_async_remote_copy(
            src_ref=ref, dst_ref=ref, send_sem=send, recv_sem=recv,
            device_id=(me, above), device_id_type=MESH,
        )

    def if_slow(act):
        pl.when(slow_here)(act)

    total[...] = jnp.zeros_like(total)
    columns = sum(here.astype(jnp.int32) for here in beside)
    others = sum(here.astype(jnp.int32) for here in slab_at)
    pl.semaphore_wait(barrier, others + columns * (1 + others))

    @if_slow
    def _():
        for j in range(SHARED):
            near_copy(slow, j).start()

    load.wait()

    for f in range(frames):
        first, last = [], []
        for c in range(2):
            wide = own16[c, f].astype(jnp.float32)
            first.append(wide[:HMAX])
            last.append(wide[depth - HMAX :])
        edge_out[0, f] = jnp.concatenate(first, axis=0).astype(jnp.bfloat16)
        edge_out[1, f] = jnp.concatenate(last, axis=0).astype(jnp.bfloat16)


    for way in range(2):

        @pl.when(slow_here & slab_at[way])
        def _(way=way):
            far_copy(way, 0).start()


    for way in range(2):

        @pl.when(slab_at[way])
        def _(way=way):
            edge_copy(way).start()

        @pl.when(jnp.logical_not(slab_at[way]))
        def _(way=way):
            edge_in[way] = jnp.zeros(edge_in.shape[1:], jnp.bfloat16)
            near_edge[slow, way] = jnp.zeros(near_edge.shape[2:], jnp.bfloat16)
            more_edge[way] = jnp.zeros(more_edge.shape[1:], jnp.bfloat16)

    @if_slow
    def _():
        for j in range(SHARED, frames):
            near_copy(slow, j).start()

    for way in range(2):

        @pl.when(slow_here & slab_at[way])
        def _(way=way):
            far_copy(way, 1).start()
            rest_copy(way).start()

    @if_slow
    def _():
        for j in range(SHARED):
            more_copy(j).start()

    for j in range(frames):
        near_copy(quick, j).start()

    for copy in small:
        copy.wait()
    for lag in range(LAGS):
        value = weights[lag].astype(jnp.float32)
        scaled[lag] = value
        scaled[LAGS + lag] = value * jnp.where(slow_here, 1.0, 0.0)
    sub = lax.broadcasted_iota(jnp.int32, (8, 4 * (depth + EDGE)), 0)
    column = lax.broadcasted_iota(jnp.int32, (8, 4 * (depth + EDGE)), 1)
    halo = lax.rem(column, EDGE)
    halo = jnp.where(halo < HMAX, halo - HMAX, halo - HMAX + depth)
    inside = column < 4 * depth
    place = jnp.where(inside, lax.rem(column, depth), halo)
    upper = column < jnp.where(inside, 2 * depth, 4 * depth + 2 * EDGE)
    reach = []
    for g in range(0, depth, 8):
        value = jnp.full(sub.shape, half[g], jnp.int32)
        for r in range(1, 8):
            value = jnp.where(sub == r, half[g + r], value)
        reach.append(value)
        keep = jnp.abs(place - (sub + g)) <= value
        band[g : g + 8] = jnp.where(keep & upper, 1.0, 0.0)
        band[depth + g : depth + g + 8] = jnp.where(keep & jnp.logical_not(upper), 1.0, 0.0)
    which = column // (2 * EDGE)
    for block in range(16):
        g = 0 if block % 2 == 0 else depth - 8
        keep = jnp.abs(halo - (sub + g)) <= reach[g // 8]
        edge_band[block * 8 : block * 8 + 8] = jnp.where(keep & (which == block // 2), 1.0, 0.0)
    window = band[...].astype(jnp.bfloat16)

    def own_field(f, carry):
        for c in range(2):
            wide = own16[c, f].astype(jnp.float32) * 0.5
            for s in range(2):
                field[2 * f + s, c] = wide[:, s * strip : (s + 1) * strip]
        return carry

    lax.fori_loop(0, frames, own_field, 0)
    back[slow, SHARED:] = jnp.zeros((frames - SHARED,) + back.shape[2:], jnp.float32)

    @pl.when(jnp.logical_not(slow_here))
    def _():
        back[slow, :SHARED] = jnp.zeros((SHARED,) + back.shape[2:], jnp.float32)

    low_factor = jnp.where(level > 0, 0.5, 0.0)
    high_factor = jnp.where(level < slabs - 1, 0.5, 0.0)

    def put_edges(slot, low, high):
        low = low.astype(jnp.float32) * low_factor
        high = high.astype(jnp.float32) * high_factor
        for c in range(2):
            edges[slot, c, 0:HMAX] = low[c * HMAX : (c + 1) * HMAX]
            edges[slot, c, HMAX:EDGE] = high[c * HMAX : (c + 1) * HMAX]

    def take_near(side, j):
        waiter(near16.at[side, j], near_send.at[side], near_recv.at[side, j]).wait_recv()
        for c in range(2):
            wide = near16[side, j, c].astype(jnp.float32) * 0.5
            field[2 * frames + frames * side + j, c] = wide

    def wait_ways(refs, send, recv):
        for way in range(2):

            @pl.when(slab_at[way])
            def _(way=way):
                waiter(refs.at[way], send.at[way], recv.at[way]).wait_recv()

    def sent_ways(refs, send):
        for way in range(2):

            @pl.when(slab_at[way])
            def _(way=way):
                waiter(refs.at[way], send.at[way], send.at[way]).wait_send()

    def wait_far(part):
        for way in range(2):

            @pl.when(slab_at[way])
            def _(way=way):
                ref = near_edge.at[slow, way, part_of(quick, part)]
                waiter(ref, far_send.at[part, way], far_recv.at[part, way]).wait_recv()

    def take_far(side, first, count):
        for j in range(first, first + count):
            frame = frame_at(1 - side, j)
            slot = 2 * frames + frames * side + j
            put_edges(slot, near_edge[side, 0, frame], near_edge[side, 1, frame])

    def take_more(j):
        waiter(more16.at[j], more_send, more_recv.at[j]).wait_recv()
        for c in range(2):
            field[4 * frames + j, c] = more16[j, c].astype(jnp.float32) * 0.5

    def take_rest():
        wait_ways(more_edge, rest_send, rest_recv)
        for j in range(SHARED):
            k = SHARED - 1 - j + slow * (2 * j - SHARED + 1)
            put_edges(4 * frames + j, more_edge[0, k], more_edge[1, k])

    def finish(place, part, y, x, weight):
        phase = signed_phase(y, x, weight)
        early, late = place
        first, second = total[early, part] + phase, total[late, part] + phase
        total[early, part] = first
        total[late, part] = second

    def inner_unit(n, q):
        c, s = q // 2, q % 2
        rows = ((0, 1 + c), (1, 2 + c) if c < 4 else (4, 5), (2, 3 + c) if c < 3 else (3, 1 + c))
        first, last = (
            jnp.where(n == 0, rows[0][i], jnp.where(n == 1, rows[1][i], rows[2][i])) for i in range(2)
        )
        return 2 * first + s, 2 * last + s, scaled[last - first - 1]

    def outer_unit(side, v, weight_at):
        j = sum(at_least(v, bound) for bound in (6, 11, 15, 18, 20))
        e = v - (6 * j - (j * (j - 1)) // 2)
        mine = 2 * frame_at(side, e) + 1 - side
        theirs = 2 * frames + frames * side + j
        early = theirs + side * (mine - theirs)
        late = mine + side * (theirs - mine)
        return early, late, scaled[weight_at + j + e]

    def middles(units, base):
        results = []
        for q in range(len(units) + 2):
            if q < len(units):
                early, late, _ = units[q]
                parts = split_products(
                    (field[early, 0], field[early, 1]), (field[late, 0], field[late, 1])
                )
                results.append(
                    jnp.dot(
                        window[:, : 4 * depth],
                        jnp.concatenate(parts, axis=0),
                        preferred_element_type=jnp.float32,
                    )
                )
            if q >= 2:
                early, late, weight = units[q - 2]
                real, imag = results[q - 2][:depth], results[q - 2][depth:]
                for c, value in enumerate((real, imag)):
                    held[base + q - 2, c, 0:HMAX] = value[:HMAX]
                    held[base + q - 2, c, HMAX:EDGE] = value[depth - HMAX :]
                for g in range(HMAX, depth - HMAX, 16):
                    finish(
                        (early, late), pl.ds(g, 16), imag[g : g + 16], real[g : g + 16], weight
                    )

    def rims(units, base):
        results = []
        for start in range(0, len(units), 4):
            group = units[start : start + 4]
            parts = []
            for early, late, _ in group:
                parts += split_products(
                    (edges[early, 0], edges[early, 1]), (edges[late, 0], edges[late, 1])
                )
            rows, columns = 2 * EDGE * len(group), 4 * EDGE * len(group)
            result = jnp.dot(
                edge_window[:rows, :columns],
                jnp.concatenate(parts, axis=0),
                preferred_element_type=jnp.float32,
            )
            results += [result[2 * EDGE * k : 2 * EDGE * (k + 1)] for k in range(len(group))]
        for q, (early, late, weight) in enumerate(units):
            real = results[q][:EDGE] + held[base + q, 0]
            imag = results[q][EDGE:] + held[base + q, 1]
            finish((early, late), pl.ds(0, HMAX), imag[:HMAX], real[:HMAX], weight)
            finish((early, late), pl.ds(depth - HMAX, HMAX), imag[HMAX:], real[HMAX:], weight)

    def inner_middles(n, carry):
        middles([inner_unit(n, q) for q in range(INNER)], n * INNER)
        return carry

    def inner_rims(n, carry):
        rims([inner_unit(n, q) for q in range(INNER)], n * INNER)
        return carry

    def quick_middles(n, carry):
        for at, js in ((0, (0, 1)), (1, (2,)), (2, (3, 4, 5))):

            @pl.when(n == at)
            def _(js=js):
                for j in js:
                    take_near(quick, j)

        middles([outer_unit(quick, n * QUICK + q, 0) for q in range(QUICK)], 3 * INNER + n * QUICK)
        return carry

    def quick_rims(n, carry):
        rims([outer_unit(quick, n * QUICK + q, 0) for q in range(QUICK)], 3 * INNER + n * QUICK)
        return carry

    def slow_unit(j, e):
        mine = 2 * frame_at(slow, e) + 1 - slow
        theirs = 2 * frames + frames * slow + j
        early = theirs + slow * (mine - theirs)
        late = mine + slow * (theirs - mine)
        return early, late, scaled[LAGS + j + e]

    def last_unit(n, q):
        def pick(values):
            value = values[3]
            for k in (2, 1, 0):
                value = jnp.where(n == k, values[k], value)
            return value

        j = pick(((3, 4, 0, 1), (3, 4, 0, 1), (3, 5, 0, 2))[q])
        e = pick(((0, 0, 3, 3), (1, 1, 4, 4), (2, 0, 5, 3))[q])
        own = jnp.where(n < 2, 1 - slow, slow)
        mine = 2 * frame_at(slow, e) + own
        theirs = j + jnp.where(n < 2, 2 * frames + frames * slow, 4 * frames)
        early = theirs + slow * (mine - theirs)
        late = mine + slow * (theirs - mine)
        return early, late, scaled[LAGS + j + e]

    def wholes(units):
        results = []
        for q in range(len(units) + 2):
            if q < len(units):
                early, late, _ = units[q]
                parts = split_products(
                    (field[early, 0], field[early, 1]), (field[late, 0], field[late, 1])
                ) + split_products(
                    (edges[early, 0], edges[early, 1]), (edges[late, 0], edges[late, 1])
                )
                results.append(
                    jnp.dot(
                        window, jnp.concatenate(parts, axis=0), preferred_element_type=jnp.float32
                    )
                )
            if q >= 2:
                early, late, weight = units[q - 2]
                real, imag = results[q - 2][:depth], results[q - 2][depth:]
                for g in range(0, depth, 24):
                    finish(
                        (early, late), pl.ds(g, 24), imag[g : g + 24], real[g : g + 24], weight
                    )

    def last_step(n, carry):
        @pl.when((n == 0) & slow_here)
        def _():
            wait_far(1)
            take_far(slow, SHARED, SHARED)
            take_near(slow, 3)

        @pl.when((n == 1) & slow_here)
        def _():
            take_near(slow, 4)
            take_near(slow, 5)

        @pl.when((n == 2) & slow_here)
        def _():
            take_rest()
            take_more(0)

        @pl.when((n == 3) & slow_here)
        def _():
            take_more(1)
            take_more(2)

        wholes([last_unit(n, q) for q in range(UNITS)])
        return carry

    @pl.when(jnp.logical_not(slow_here))
    def _():
        def clear(j, carry):
            slot = 2 * frames + frames * slow + j
            field[slot] = jnp.zeros(field.shape[1:], jnp.float32)
            edges[slot] = jnp.zeros(edges.shape[1:], jnp.float32)
            return carry

        lax.fori_loop(0, frames, clear, 0)
        for j in range(SHARED):
            field[4 * frames + j] = jnp.zeros(field.shape[1:], jnp.float32)
            edges[4 * frames + j] = jnp.zeros(edges.shape[1:], jnp.float32)

    lax.fori_loop(0, 3, inner_middles, 0)
    lax.fori_loop(0, 3, quick_middles, 0)

    shared = [[slow_unit(j, e) for e in range(frames - j)] for j in range(SHARED)]
    bases = [3 * (INNER + QUICK) + sum(map(len, shared[:j])) for j in range(SHARED)]
    for j, base in enumerate(bases):

        @if_slow
        def _(j=j):
            take_near(slow, j)

        middles(shared[j], base)

    @if_slow
    def _():
        back_copy(slow, SHARED, pl.ds(HMAX, depth - EDGE)).start()

    wait_ways(edge_in, edge_send, edge_recv)
    halo_copy().start()
    for f in range(frames):
        for s in range(2):
            lanes = pl.ds(s * strip, strip)
            put_edges(2 * f + s, edge_in[0, f, :, lanes], edge_in[1, f, :, lanes])

    edge_window = edge_band[...].astype(jnp.bfloat16)

    @if_slow
    def _():
        wait_far(0)
        take_far(slow, 0, SHARED)

    for j, base in enumerate(bases):
        rims(shared[j], base)

    @if_slow
    def _():
        for at in (0, depth - HMAX):
            back_copy(slow, SHARED, pl.ds(at, HMAX)).start()

    waiter(near_edge.at[quick], halo_send, halo_recv).wait_recv()
    take_far(quick, 0, frames)
    lax.fori_loop(0, 3, quick_rims, 0)
    back_copy(quick, frames, pl.ds(0, depth)).start()
    lax.fori_loop(0, 3, inner_rims, 0)

    frame_total = frames * blocks

    def write(side):
        lanes = cut(side)

        def write_frame(f, carry):
            now = me * frames + f
            norm = jnp.float32(0.0)
            for lag in range(1, LAGS + 1):
                count = at_least(frame_total - 1, now + lag) + at_least(now, lag)
                norm = norm + scaled[lag - 1] * count.astype(jnp.float32)
            inverse = 1.0 / jnp.full((8, strip), norm, jnp.float32)
            j = frame_at(side, f)
            slot = 2 * f + side
            for g in range(0, depth, 8):
                part = pl.ds(g, 8)
                out[f, part, lanes] = (total[slot, part] + back[side, j, part]) * inverse
            return carry

        lax.fori_loop(0, frames, write_frame, 0)

    lax.fori_loop(0, 2, last_step, 0)
    waiter(back.at[quick], back_send.at[quick], back_recv.at[quick]).wait()
    write(quick)
    lax.fori_loop(2, 4, last_step, 0)

    @if_slow
    def _():
        waiter(back.at[slow, pl.ds(0, SHARED)], back_send.at[slow], back_recv.at[slow]).wait()

    write(slow)

    @if_slow
    def _():
        sent_ways(more_edge, rest_send)
        for part in range(2):
            sent_ways(near_edge.at[slow, :, part_of(slow, part)], far_send.at[part])
        waiter(more16, more_send, more_send).wait_send()
        waiter(near16.at[slow], near_send.at[slow], near_send.at[slow]).wait_send()

    sent_ways(edge_out, edge_send)
    waiter(near_edge.at[quick], halo_send, halo_send).wait_send()
    waiter(near16.at[quick], near_send.at[quick], near_send.at[quick]).wait_send()


def shards(iq, half, weights):
    _, frames, depth, lines = iq.shape
    strip = lines // 2
    slots = 4 * frames + SHARED
    wide, thin = jnp.float32, jnp.bfloat16
    dma = pltpu.SemaphoreType.DMA
    return pl.pallas_call(
        kernel,
        out_shape=pltpu.VMEM((frames, depth, lines), wide),
        in_specs=[pl.BlockSpec(memory_space=pltpu.HBM)] * 3,
        out_specs=pl.BlockSpec(memory_space=pltpu.VMEM),
        scratch_shapes=[
            pltpu.SMEM(half.shape, jnp.int32),
            pltpu.SMEM(weights.shape, jnp.int32),
            pltpu.SMEM((2 * LAGS,), wide),
            pltpu.VMEM((2, frames, depth, lines), thin),
            pltpu.VMEM((2, frames, EDGE, lines), thin),
            pltpu.VMEM((2, frames, EDGE, lines), thin),
            pltpu.VMEM((2, frames, 2, depth, strip), thin),
            pltpu.VMEM((2, 2, frames, EDGE, strip), thin),
            pltpu.VMEM((SHARED, 2, depth, strip), thin),
            pltpu.VMEM((2, SHARED, EDGE, strip), thin),
            pltpu.VMEM((slots, 2, depth, strip), wide),
            pltpu.VMEM((slots, 2, EDGE, strip), wide),
            pltpu.VMEM((slots, depth, strip), wide),
            pltpu.VMEM((3 * (INNER + QUICK) + SHARED_STRIPS, 2, EDGE, strip), wide),
            pltpu.VMEM((2 * depth, 4 * (depth + EDGE)), wide),
            pltpu.VMEM((8 * EDGE, 16 * EDGE), wide),
            pltpu.VMEM((2, frames, depth, strip), wide),
            dma(()),
            dma((2,)),
            dma((2,)),
            dma((2,)),
            dma((2,)),
            dma((2, frames)),
            dma((2, 2)),
            dma((2, 2)),
            dma(()),
            dma(()),
            dma(()),
            dma((SHARED,)),
            dma((2,)),
            dma((2,)),
            dma((2,)),
            dma((2,)),
        ],
        compiler_params=pltpu.CompilerParams(
            collective_id=0, has_side_effects=True, vmem_limit_bytes=48 * 1024 * 1024
        ),
        name="pair_phases",
    )(*(pltpu.with_memory_space_constraint(x, pltpu.HBM) for x in (iq, half, weights)))


def solution(mesh):
    placed = (P(None, "tm", "depth", None), P("depth"), P())
    return jax.shard_map(
        shards, mesh=mesh, in_specs=placed, out_specs=P("tm", "depth", None), check_vma=False
    )
```

```python
import functools

import jax
import jax.numpy as jnp
import numpy as np
from jax import lax
from jax.experimental import pallas as pl
from jax.experimental.pallas import tpu as pltpu
from jax.sharding import PartitionSpec as P

LAGS = 6
HMAX = 8
HALF_PI = float(np.float32(np.pi / 2))
PI = float(np.float32(np.pi))
TINY = 1.1754944e-38
ATAN = (
    0.9999960660934448,
    -0.33301785588264465,
    0.19582265615463257,
    -0.12176322191953659,
    0.05807745084166527,
    -0.0137208616361022,
)
MESH = pl.DeviceIdType.MESH
UNITS = 3
INNER = 10
QUICK = 7
EDGE = 2 * HMAX
SHARED = 3
SHARED_STRIPS = 15


def at_least(value, bound):
    return (value >= bound).astype(jnp.int32)


def signed_phase(y, x, weight):
    ax = jnp.abs(x)
    ay = jnp.abs(y)
    high = jnp.maximum(jnp.maximum(ax, ay), TINY)
    t = jnp.minimum(ax, ay) * pltpu.reciprocal(high, approx=True)
    s = t * t
    poly = ATAN[-1] * s + ATAN[-2]
    for coefficient in ATAN[-3::-1]:
        poly = poly * s + coefficient
    angle = poly * t
    angle = jnp.where(ay > ax, HALF_PI - angle, angle)
    angle = jnp.where(x < 0, PI - angle, angle)
    return angle * jnp.where(y < 0, -weight, weight)


def split_products(early, late):
    parts = []
    (ar, ai), (br, bi) = early, late
    for value in (br * ar + bi * ai, bi * ar - br * ai):
        high = value.astype(jnp.bfloat16)
        low = (value - high.astype(jnp.float32)).astype(jnp.bfloat16)
        parts += [high, low]
    return parts


def kernel(
    iq_any, half_any, weights_any, out,
    half, weights, scaled, own16, edge_out, edge_in, near16, near_edge, more16, more_edge,
    field, edges, total, held, band, edge_band, back,
    load_sem, small_sem, edge_send, edge_recv, near_send, near_recv, far_send, far_recv, halo_send, halo_recv,
    more_send, more_recv, rest_send, rest_recv, back_send, back_recv,
):
    frames, depth, lines = own16.shape[1:]
    strip = lines // 2
    me, level = lax.axis_index("tm"), lax.axis_index("depth")
    blocks, slabs = lax.axis_size("tm"), lax.axis_size("depth")
    left, right = lax.rem(me + blocks - 1, blocks), lax.rem(me + 1, blocks)
    below, above = lax.rem(level + slabs - 1, slabs), lax.rem(level + 1, slabs)
    slow = lax.rem(me, 2)
    quick = 1 - slow
    beside = (me > 0, me < blocks - 1)
    slab_at = (level > 0, level < slabs - 1)
    target = me - 1 + 2 * slow
    slow_here = (target >= 0) & (target < blocks)

    load = pltpu.make_async_copy(iq_any, own16, load_sem)
    load.start()
    small = [
        pltpu.make_async_copy(half_any, half, small_sem.at[0]),
        pltpu.make_async_copy(weights_any, weights, small_sem.at[1]),
    ]
    for copy in small:
        copy.start()
    barrier = pltpu.get_barrier_semaphore()
    for way, other in enumerate((below, above)):

        @pl.when(slab_at[way])
        def _(other=other):
            pl.semaphore_signal(barrier, inc=1, device_id=(me, other), device_id_type=MESH)

    for side, column in enumerate((left, right)):

        @pl.when(beside[side])
        def _(column=column):
            pl.semaphore_signal(barrier, inc=1, device_id=(column, level), device_id_type=MESH)

        for way, other in enumerate((below, above)):

            @pl.when(beside[side] & slab_at[way])
            def _(column=column, other=other):
                pl.semaphore_signal(barrier, inc=1, device_id=(column, other), device_id_type=MESH)

    def cut(side):
        return pl.ds(pl.multiple_of(side * strip, strip), strip)

    def next_to(side):
        return lax.rem(me + blocks - 1 + 2 * side, blocks)

    def frame_at(side, j):
        return j + side * (frames - 1 - 2 * j)

    def edge_copy(way):
        return pltpu.make_async_remote_copy(
            src_ref=edge_out.at[way],
            dst_ref=edge_in.at[1 - way],
            send_sem=edge_send.at[way],
            recv_sem=edge_recv.at[1 - way],
            device_id=(me, below if way == 0 else above),
            device_id_type=MESH,
        )

    def near_copy(side, j):
        return pltpu.make_async_remote_copy(
            src_ref=iq_any.at[:, frame_at(side, j), :, cut(side)],
            dst_ref=near16.at[1 - side, j],
            send_sem=near_send.at[side],
            recv_sem=near_recv.at[1 - side, j],
            device_id=(next_to(side), level),
            device_id_type=MESH,
        )

    def part_of(side, part):
        return pl.ds((side + part - 2 * side * part) * SHARED, SHARED)

    def far_copy(way, part):
        return pltpu.make_async_remote_copy(
            src_ref=edge_out.at[way, part_of(slow, part), :, cut(slow)],
            dst_ref=near_edge.at[1 - slow, 1 - way, part_of(slow, part)],
            send_sem=far_send.at[part, way],
            recv_sem=far_recv.at[part, 1 - way],
            device_id=(next_to(slow), below if way == 0 else above),
            device_id_type=MESH,
        )

    def more_copy(j):
        return pltpu.make_async_remote_copy(
            src_ref=own16.at[:, frame_at(slow, j), :, cut(quick)],
            dst_ref=more16.at[j],
            send_sem=more_send,
            recv_sem=more_recv.at[j],
            device_id=(next_to(slow), level),
            device_id_type=MESH,
        )

    def rest_copy(way):
        return pltpu.make_async_remote_copy(
            src_ref=edge_out.at[way, pl.ds(slow * (frames - SHARED), SHARED), :, cut(quick)],
            dst_ref=more_edge.at[1 - way],
            send_sem=rest_send.at[way],
            recv_sem=rest_recv.at[1 - way],
            device_id=(next_to(slow), below if way == 0 else above),
            device_id_type=MESH,
        )

    def halo_copy():
        return pltpu.make_async_remote_copy(
            src_ref=edge_in.at[:, :, :, cut(quick)],
            dst_ref=near_edge.at[1 - quick],
            send_sem=halo_send,
            recv_sem=halo_recv,
            device_id=(next_to(quick), level),
            device_id_type=MESH,
        )

    def back_copy(side, count, part):
        first = 2 * frames + frames * side
        return pltpu.make_async_remote_copy(
            src_ref=total.at[pl.ds(first, count), part],
            dst_ref=back.at[1 - side, pl.ds(0, count), part],
            send_sem=back_send.at[side],
            recv_sem=back_recv.at[1 - side],
            device_id=(next_to(side), level),
            device_id_type=MESH,
        )

    def waiter(ref, send, recv):
        return pltpu.make_async_remote_copy(
            src_ref=ref, dst_ref=ref, send_sem=send, recv_sem=recv,
            device_id=(me, above), device_id_type=MESH,
        )

    def if_slow(act):
        pl.when(slow_here)(act)

    total[...] = jnp.zeros_like(total)
    columns = sum(here.astype(jnp.int32) for here in beside)
    others = sum(here.astype(jnp.int32) for here in slab_at)
    pl.semaphore_wait(barrier, others + columns * (1 + others))

    @if_slow
    def _():
        for j in range(2):
            near_copy(slow, j).start()

    load.wait()

    for f in range(frames):
        first, last = [], []
        for c in range(2):
            wide = own16[c, f].astype(jnp.float32)
            first.append(wide[:HMAX])
            last.append(wide[depth - HMAX :])
        edge_out[0, f] = jnp.concatenate(first, axis=0).astype(jnp.bfloat16)
        edge_out[1, f] = jnp.concatenate(last, axis=0).astype(jnp.bfloat16)


    for way in range(2):

        @pl.when(slow_here & slab_at[way])
        def _(way=way):
            far_copy(way, 0).start()


    for way in range(2):

        @pl.when(slab_at[way])
        def _(way=way):
            edge_copy(way).start()

        @pl.when(jnp.logical_not(slab_at[way]))
        def _(way=way):
            edge_in[way] = jnp.zeros(edge_in.shape[1:], jnp.bfloat16)
            near_edge[slow, way] = jnp.zeros(near_edge.shape[2:], jnp.bfloat16)
            more_edge[way] = jnp.zeros(more_edge.shape[1:], jnp.bfloat16)

    @if_slow
    def _():
        for j in range(2, frames):
            near_copy(slow, j).start()

    for way in range(2):

        @pl.when(slow_here & slab_at[way])
        def _(way=way):
            far_copy(way, 1).start()
            rest_copy(way).start()

    @if_slow
    def _():
        for j in range(SHARED):
            more_copy(j).start()

    for j in range(frames):
        near_copy(quick, j).start()

    for copy in small:
        copy.wait()
    for lag in range(LAGS):
        value = weights[lag].astype(jnp.float32)
        scaled[lag] = value
        scaled[LAGS + lag] = value * jnp.where(slow_here, 1.0, 0.0)
    sub = lax.broadcasted_iota(jnp.int32, (8, 4 * (depth + EDGE)), 0)
    column = lax.broadcasted_iota(jnp.int32, (8, 4 * (depth + EDGE)), 1)
    halo = lax.rem(column, EDGE)
    halo = jnp.where(halo < HMAX, halo - HMAX, halo - HMAX + depth)
    inside = column < 4 * depth
    place = jnp.where(inside, lax.rem(column, depth), halo)
    upper = column < jnp.where(inside, 2 * depth, 4 * depth + 2 * EDGE)
    reach = []
    for g in range(0, depth, 8):
        value = jnp.full(sub.shape, half[g], jnp.int32)
        for r in range(1, 8):
            value = jnp.where(sub == r, half[g + r], value)
        reach.append(value)
        keep = jnp.abs(place - (sub + g)) <= value
        band[g : g + 8] = jnp.where(keep & upper, 1.0, 0.0)
        band[depth + g : depth + g + 8] = jnp.where(keep & jnp.logical_not(upper), 1.0, 0.0)
    which = column // (2 * EDGE)
    for block in range(16):
        g = 0 if block % 2 == 0 else depth - 8
        keep = jnp.abs(halo - (sub + g)) <= reach[g // 8]
        edge_band[block * 8 : block * 8 + 8] = jnp.where(keep & (which == block // 2), 1.0, 0.0)
    window = band[...].astype(jnp.bfloat16)

    def own_field(f, carry):
        for c in range(2):
            wide = own16[c, f].astype(jnp.float32) * 0.5
            for s in range(2):
                field[2 * f + s, c] = wide[:, s * strip : (s + 1) * strip]
        return carry

    lax.fori_loop(0, frames, own_field, 0)
    back[slow, SHARED:] = jnp.zeros((frames - SHARED,) + back.shape[2:], jnp.float32)

    @pl.when(jnp.logical_not(slow_here))
    def _():
        back[slow, :SHARED] = jnp.zeros((SHARED,) + back.shape[2:], jnp.float32)

    low_factor = jnp.where(level > 0, 0.5, 0.0)
    high_factor = jnp.where(level < slabs - 1, 0.5, 0.0)

    def put_edges(slot, low, high):
        low = low.astype(jnp.float32) * low_factor
        high = high.astype(jnp.float32) * high_factor
        for c in range(2):
            edges[slot, c, 0:HMAX] = low[c * HMAX : (c + 1) * HMAX]
            edges[slot, c, HMAX:EDGE] = high[c * HMAX : (c + 1) * HMAX]

    def take_near(side, j):
        waiter(near16.at[side, j], near_send.at[side], near_recv.at[side, j]).wait_recv()
        for c in range(2):
            wide = near16[side, j, c].astype(jnp.float32) * 0.5
            field[2 * frames + frames * side + j, c] = wide

    def wait_ways(refs, send, recv):
        for way in range(2):

            @pl.when(slab_at[way])
            def _(way=way):
                waiter(refs.at[way], send.at[way], recv.at[way]).wait_recv()

    def sent_ways(refs, send):
        for way in range(2):

            @pl.when(slab_at[way])
            def _(way=way):
                waiter(refs.at[way], send.at[way], send.at[way]).wait_send()

    def wait_far(part):
        for way in range(2):

            @pl.when(slab_at[way])
            def _(way=way):
                ref = near_edge.at[slow, way, part_of(quick, part)]
                waiter(ref, far_send.at[part, way], far_recv.at[part, way]).wait_recv()

    def take_far(side, first, count):
        for j in range(first, first + count):
            frame = frame_at(1 - side, j)
            slot = 2 * frames + frames * side + j
            put_edges(slot, near_edge[side, 0, frame], near_edge[side, 1, frame])

    def take_more(j):
        waiter(more16.at[j], more_send, more_recv.at[j]).wait_recv()
        for c in range(2):
            field[4 * frames + j, c] = more16[j, c].astype(jnp.float32) * 0.5

    def take_rest():
        wait_ways(more_edge, rest_send, rest_recv)
        for j in range(SHARED):
            k = SHARED - 1 - j + slow * (2 * j - SHARED + 1)
            put_edges(4 * frames + j, more_edge[0, k], more_edge[1, k])

    def finish(place, part, y, x, weight):
        phase = signed_phase(y, x, weight)
        early, late = place
        first, second = total[early, part] + phase, total[late, part] + phase
        total[early, part] = first
        total[late, part] = second

    def inner_unit(n, q):
        c, s = q // 2, q % 2
        rows = ((0, 1 + c), (1, 2 + c) if c < 4 else (4, 5), (2, 3 + c) if c < 3 else (3, 1 + c))
        first, last = (
            jnp.where(n == 0, rows[0][i], jnp.where(n == 1, rows[1][i], rows[2][i])) for i in range(2)
        )
        return 2 * first + s, 2 * last + s, scaled[last - first - 1]

    def outer_unit(side, v, weight_at):
        j = sum(at_least(v, bound) for bound in (6, 11, 15, 18, 20))
        e = v - (6 * j - (j * (j - 1)) // 2)
        mine = 2 * frame_at(side, e) + 1 - side
        theirs = 2 * frames + frames * side + j
        early = theirs + side * (mine - theirs)
        late = mine + side * (theirs - mine)
        return early, late, scaled[weight_at + j + e]

    def middles(units, base):
        results = []
        for q in range(len(units) + 2):
            if q < len(units):
                early, late, _ = units[q]
                parts = split_products(
                    (field[early, 0], field[early, 1]), (field[late, 0], field[late, 1])
                )
                results.append(
                    jnp.dot(
                        window[:, : 4 * depth],
                        jnp.concatenate(parts, axis=0),
                        preferred_element_type=jnp.float32,
                    )
                )
            if q >= 2:
                early, late, weight = units[q - 2]
                real, imag = results[q - 2][:depth], results[q - 2][depth:]
                for c, value in enumerate((real, imag)):
                    held[base + q - 2, c, 0:HMAX] = value[:HMAX]
                    held[base + q - 2, c, HMAX:EDGE] = value[depth - HMAX :]
                for g in range(HMAX, depth - HMAX, 16):
                    finish(
                        (early, late), pl.ds(g, 16), imag[g : g + 16], real[g : g + 16], weight
                    )

    def rims(units, base):
        results = []
        for start in range(0, len(units), 4):
            group = units[start : start + 4]
            parts = []
            for early, late, _ in group:
                parts += split_products(
                    (edges[early, 0], edges[early, 1]), (edges[late, 0], edges[late, 1])
                )
            rows, columns = 2 * EDGE * len(group), 4 * EDGE * len(group)
            result = jnp.dot(
                edge_window[:rows, :columns],
                jnp.concatenate(parts, axis=0),
                preferred_element_type=jnp.float32,
            )
            results += [result[2 * EDGE * k : 2 * EDGE * (k + 1)] for k in range(len(group))]
        for q, (early, late, weight) in enumerate(units):
            real = results[q][:EDGE] + held[base + q, 0]
            imag = results[q][EDGE:] + held[base + q, 1]
            finish((early, late), pl.ds(0, HMAX), imag[:HMAX], real[:HMAX], weight)
            finish((early, late), pl.ds(depth - HMAX, HMAX), imag[HMAX:], real[HMAX:], weight)

    def inner_middles(n, carry):
        middles([inner_unit(n, q) for q in range(INNER)], n * INNER)
        return carry

    def inner_rims(n, carry):
        rims([inner_unit(n, q) for q in range(INNER)], n * INNER)
        return carry

    def quick_middles(n, carry):
        for at, js in ((0, (0, 1)), (1, (2,)), (2, (3, 4, 5))):

            @pl.when(n == at)
            def _(js=js):
                for j in js:
                    take_near(quick, j)

        middles([outer_unit(quick, n * QUICK + q, 0) for q in range(QUICK)], 3 * INNER + n * QUICK)
        return carry

    def quick_rims(n, carry):
        rims([outer_unit(quick, n * QUICK + q, 0) for q in range(QUICK)], 3 * INNER + n * QUICK)
        return carry

    def slow_unit(j, e):
        mine = 2 * frame_at(slow, e) + 1 - slow
        theirs = 2 * frames + frames * slow + j
        early = theirs + slow * (mine - theirs)
        late = mine + slow * (theirs - mine)
        return early, late, scaled[LAGS + j + e]

    def last_unit(n, q):
        def pick(values):
            value = values[3]
            for k in (2, 1, 0):
                value = jnp.where(n == k, values[k], value)
            return value

        j = pick(((3, 4, 0, 1), (3, 4, 0, 1), (3, 5, 0, 2))[q])
        e = pick(((0, 0, 3, 3), (1, 1, 4, 4), (2, 0, 5, 3))[q])
        own = jnp.where(n < 2, 1 - slow, slow)
        mine = 2 * frame_at(slow, e) + own
        theirs = j + jnp.where(n < 2, 2 * frames + frames * slow, 4 * frames)
        early = theirs + slow * (mine - theirs)
        late = mine + slow * (theirs - mine)
        return early, late, scaled[LAGS + j + e]

    def wholes(units):
        results = []
        for q in range(len(units) + 2):
            if q < len(units):
                early, late, _ = units[q]
                parts = split_products(
                    (field[early, 0], field[early, 1]), (field[late, 0], field[late, 1])
                ) + split_products(
                    (edges[early, 0], edges[early, 1]), (edges[late, 0], edges[late, 1])
                )
                results.append(
                    jnp.dot(
                        window, jnp.concatenate(parts, axis=0), preferred_element_type=jnp.float32
                    )
                )
            if q >= 2:
                early, late, weight = units[q - 2]
                real, imag = results[q - 2][:depth], results[q - 2][depth:]
                for g in range(0, depth, 24):
                    finish(
                        (early, late), pl.ds(g, 24), imag[g : g + 24], real[g : g + 24], weight
                    )

    def last_step(n, carry):
        @pl.when((n == 0) & slow_here)
        def _():
            wait_far(1)
            take_far(slow, SHARED, SHARED)
            take_near(slow, 3)

        @pl.when((n == 1) & slow_here)
        def _():
            take_near(slow, 4)
            take_near(slow, 5)

        @pl.when((n == 2) & slow_here)
        def _():
            take_rest()
            take_more(0)

        @pl.when((n == 3) & slow_here)
        def _():
            take_more(1)
            take_more(2)

        wholes([last_unit(n, q) for q in range(UNITS)])
        return carry

    @pl.when(jnp.logical_not(slow_here))
    def _():
        def clear(j, carry):
            slot = 2 * frames + frames * slow + j
            field[slot] = jnp.zeros(field.shape[1:], jnp.float32)
            edges[slot] = jnp.zeros(edges.shape[1:], jnp.float32)
            return carry

        lax.fori_loop(0, frames, clear, 0)
        for j in range(SHARED):
            field[4 * frames + j] = jnp.zeros(field.shape[1:], jnp.float32)
            edges[4 * frames + j] = jnp.zeros(edges.shape[1:], jnp.float32)

    lax.fori_loop(0, 3, inner_middles, 0)
    lax.fori_loop(0, 3, quick_middles, 0)

    shared = [[slow_unit(j, e) for e in range(frames - j)] for j in range(SHARED)]
    bases = [3 * (INNER + QUICK) + sum(map(len, shared[:j])) for j in range(SHARED)]
    for j, base in enumerate(bases):

        @if_slow
        def _(j=j):
            take_near(slow, j)

        middles(shared[j], base)

    @if_slow
    def _():
        back_copy(slow, SHARED, pl.ds(HMAX, depth - EDGE)).start()

    wait_ways(edge_in, edge_send, edge_recv)
    halo_copy().start()
    for f in range(frames):
        for s in range(2):
            lanes = pl.ds(s * strip, strip)
            put_edges(2 * f + s, edge_in[0, f, :, lanes], edge_in[1, f, :, lanes])

    edge_window = edge_band[...].astype(jnp.bfloat16)

    @if_slow
    def _():
        wait_far(0)
        take_far(slow, 0, SHARED)

    rims(sum(shared, []), bases[0])

    @if_slow
    def _():
        for at in (0, depth - HMAX):
            back_copy(slow, SHARED, pl.ds(at, HMAX)).start()

    waiter(near_edge.at[quick], halo_send, halo_recv).wait_recv()
    take_far(quick, 0, frames)
    lax.fori_loop(0, 3, quick_rims, 0)
    back_copy(quick, frames, pl.ds(0, depth)).start()
    lax.fori_loop(0, 3, inner_rims, 0)

    frame_total = frames * blocks

    def write(side):
        lanes = cut(side)

        def write_frame(f, carry):
            now = me * frames + f
            norm = jnp.float32(0.0)
            for lag in range(1, LAGS + 1):
                count = at_least(frame_total - 1, now + lag) + at_least(now, lag)
                norm = norm + scaled[lag - 1] * count.astype(jnp.float32)
            inverse = 1.0 / jnp.full((8, strip), norm, jnp.float32)
            j = frame_at(side, f)
            slot = 2 * f + side
            for g in range(0, depth, 8):
                part = pl.ds(g, 8)
                out[f, part, lanes] = (total[slot, part] + back[side, j, part]) * inverse
            return carry

        lax.fori_loop(0, frames, write_frame, 0)

    lax.fori_loop(0, 2, last_step, 0)
    waiter(back.at[quick], back_send.at[quick], back_recv.at[quick]).wait()
    write(quick)
    lax.fori_loop(2, 4, last_step, 0)

    @if_slow
    def _():
        waiter(back.at[slow, pl.ds(0, SHARED)], back_send.at[slow], back_recv.at[slow]).wait()

    write(slow)

    @if_slow
    def _():
        sent_ways(more_edge, rest_send)
        for part in range(2):
            sent_ways(near_edge.at[slow, :, part_of(slow, part)], far_send.at[part])
        waiter(more16, more_send, more_send).wait_send()
        waiter(near16.at[slow], near_send.at[slow], near_send.at[slow]).wait_send()

    sent_ways(edge_out, edge_send)
    waiter(near_edge.at[quick], halo_send, halo_send).wait_send()
    waiter(near16.at[quick], near_send.at[quick], near_send.at[quick]).wait_send()


def shards(iq, half, weights):
    _, frames, depth, lines = iq.shape
    strip = lines // 2
    slots = 4 * frames + SHARED
    wide, thin = jnp.float32, jnp.bfloat16
    dma = pltpu.SemaphoreType.DMA
    return pl.pallas_call(
        kernel,
        out_shape=pltpu.VMEM((frames, depth, lines), wide),
        in_specs=[pl.BlockSpec(memory_space=pltpu.HBM)] * 3,
        out_specs=pl.BlockSpec(memory_space=pltpu.VMEM),
        scratch_shapes=[
            pltpu.SMEM(half.shape, jnp.int32),
            pltpu.SMEM(weights.shape, jnp.int32),
            pltpu.SMEM((2 * LAGS,), wide),
            pltpu.VMEM((2, frames, depth, lines), thin),
            pltpu.VMEM((2, frames, EDGE, lines), thin),
            pltpu.VMEM((2, frames, EDGE, lines), thin),
            pltpu.VMEM((2, frames, 2, depth, strip), thin),
            pltpu.VMEM((2, 2, frames, EDGE, strip), thin),
            pltpu.VMEM((SHARED, 2, depth, strip), thin),
            pltpu.VMEM((2, SHARED, EDGE, strip), thin),
            pltpu.VMEM((slots, 2, depth, strip), wide),
            pltpu.VMEM((slots, 2, EDGE, strip), wide),
            pltpu.VMEM((slots, depth, strip), wide),
            pltpu.VMEM((3 * (INNER + QUICK) + SHARED_STRIPS, 2, EDGE, strip), wide),
            pltpu.VMEM((2 * depth, 4 * (depth + EDGE)), wide),
            pltpu.VMEM((8 * EDGE, 16 * EDGE), wide),
            pltpu.VMEM((2, frames, depth, strip), wide),
            dma(()),
            dma((2,)),
            dma((2,)),
            dma((2,)),
            dma((2,)),
            dma((2, frames)),
            dma((2, 2)),
            dma((2, 2)),
            dma(()),
            dma(()),
            dma(()),
            dma((SHARED,)),
            dma((2,)),
            dma((2,)),
            dma((2,)),
            dma((2,)),
        ],
        compiler_params=pltpu.CompilerParams(
            collective_id=0, has_side_effects=True, vmem_limit_bytes=48 * 1024 * 1024
        ),
        name="pair_phases",
    )(*(pltpu.with_memory_space_constraint(x, pltpu.HBM) for x in (iq, half, weights)))


def solution(mesh):
    placed = (P(None, "tm", "depth", None), P("depth"), P())
    return jax.shard_map(
        shards, mesh=mesh, in_specs=placed, out_specs=P("tm", "depth", None), check_vma=False
    )
```

```python
import functools

import jax
import jax.numpy as jnp
import numpy as np
from jax import lax
from jax.experimental import pallas as pl
from jax.experimental.pallas import tpu as pltpu
from jax.sharding import PartitionSpec as P

LAGS = 6
HMAX = 8
HALF_PI = float(np.float32(np.pi / 2))
PI = float(np.float32(np.pi))
TINY = 1.1754944e-38
ATAN = (
    0.9999960660934448,
    -0.33301785588264465,
    0.19582265615463257,
    -0.12176322191953659,
    0.05807745084166527,
    -0.0137208616361022,
)
MESH = pl.DeviceIdType.MESH
UNITS = 3
INNER = 10
QUICK = 7
EDGE = 2 * HMAX
SHARED = 3
SHARED_STRIPS = 15


def at_least(value, bound):
    return (value >= bound).astype(jnp.int32)


def signed_phase(y, x, weight):
    ax = jnp.abs(x)
    ay = jnp.abs(y)
    high = jnp.maximum(jnp.maximum(ax, ay), TINY)
    t = jnp.minimum(ax, ay) * pltpu.reciprocal(high, approx=True)
    s = t * t
    poly = ATAN[-1] * s + ATAN[-2]
    for coefficient in ATAN[-3::-1]:
        poly = poly * s + coefficient
    angle = poly * t
    angle = jnp.where(ay > ax, HALF_PI - angle, angle)
    angle = jnp.where(x < 0, PI - angle, angle)
    return angle * jnp.where(y < 0, -weight, weight)


def split_products(early, late):
    parts = []
    (ar, ai), (br, bi) = early, late
    for value in (br * ar + bi * ai, bi * ar - br * ai):
        high = value.astype(jnp.bfloat16)
        low = (value - high.astype(jnp.float32)).astype(jnp.bfloat16)
        parts += [high, low]
    return parts


def kernel(
    iq_any, half_any, weights_any, out,
    half, weights, scaled, own16, edge_out, edge_in, near16, near_edge, more16, more_edge,
    field, edges, total, held, band, edge_band, back,
    load_sem, small_sem, edge_send, edge_recv, near_send, near_recv, far_send, far_recv, halo_send, halo_recv,
    more_send, more_recv, rest_send, rest_recv, back_send, back_recv,
):
    frames, depth, lines = own16.shape[1:]
    strip = lines // 2
    me, level = lax.axis_index("tm"), lax.axis_index("depth")
    blocks, slabs = lax.axis_size("tm"), lax.axis_size("depth")
    left, right = lax.rem(me + blocks - 1, blocks), lax.rem(me + 1, blocks)
    below, above = lax.rem(level + slabs - 1, slabs), lax.rem(level + 1, slabs)
    slow = lax.rem(me, 2)
    quick = 1 - slow
    beside = (me > 0, me < blocks - 1)
    slab_at = (level > 0, level < slabs - 1)
    target = me - 1 + 2 * slow
    slow_here = (target >= 0) & (target < blocks)

    load = pltpu.make_async_copy(iq_any, own16, load_sem)
    load.start()
    small = [
        pltpu.make_async_copy(half_any, half, small_sem.at[0]),
        pltpu.make_async_copy(weights_any, weights, small_sem.at[1]),
    ]
    for copy in small:
        copy.start()
    barrier = pltpu.get_barrier_semaphore()
    for way, other in enumerate((below, above)):

        @pl.when(slab_at[way])
        def _(other=other):
            pl.semaphore_signal(barrier, inc=1, device_id=(me, other), device_id_type=MESH)

    for side, column in enumerate((left, right)):

        @pl.when(beside[side])
        def _(column=column):
            pl.semaphore_signal(barrier, inc=1, device_id=(column, level), device_id_type=MESH)

        for way, other in enumerate((below, above)):

            @pl.when(beside[side] & slab_at[way])
            def _(column=column, other=other):
                pl.semaphore_signal(barrier, inc=1, device_id=(column, other), device_id_type=MESH)

    def cut(side):
        return pl.ds(pl.multiple_of(side * strip, strip), strip)

    def next_to(side):
        return lax.rem(me + blocks - 1 + 2 * side, blocks)

    def frame_at(side, j):
        return j + side * (frames - 1 - 2 * j)

    def edge_copy(way):
        return pltpu.make_async_remote_copy(
            src_ref=edge_out.at[way],
            dst_ref=edge_in.at[1 - way],
            send_sem=edge_send.at[way],
            recv_sem=edge_recv.at[1 - way],
            device_id=(me, below if way == 0 else above),
            device_id_type=MESH,
        )

    def near_copy(side, j):
        return pltpu.make_async_remote_copy(
            src_ref=iq_any.at[:, frame_at(side, j), :, cut(side)],
            dst_ref=near16.at[1 - side, j],
            send_sem=near_send.at[side],
            recv_sem=near_recv.at[1 - side, j],
            device_id=(next_to(side), level),
            device_id_type=MESH,
        )

    def part_of(side, part):
        return pl.ds((side + part - 2 * side * part) * SHARED, SHARED)

    def far_copy(way, part):
        return pltpu.make_async_remote_copy(
            src_ref=edge_out.at[way, part_of(slow, part), :, cut(slow)],
            dst_ref=near_edge.at[1 - slow, 1 - way, part_of(slow, part)],
            send_sem=far_send.at[part, way],
            recv_sem=far_recv.at[part, 1 - way],
            device_id=(next_to(slow), below if way == 0 else above),
            device_id_type=MESH,
        )

    def more_copy(j):
        return pltpu.make_async_remote_copy(
            src_ref=own16.at[:, frame_at(slow, j), :, cut(quick)],
            dst_ref=more16.at[j],
            send_sem=more_send,
            recv_sem=more_recv.at[j],
            device_id=(next_to(slow), level),
            device_id_type=MESH,
        )

    def rest_copy(way):
        return pltpu.make_async_remote_copy(
            src_ref=edge_out.at[way, pl.ds(slow * (frames - SHARED), SHARED), :, cut(quick)],
            dst_ref=more_edge.at[1 - way],
            send_sem=rest_send.at[way],
            recv_sem=rest_recv.at[1 - way],
            device_id=(next_to(slow), below if way == 0 else above),
            device_id_type=MESH,
        )

    def halo_copy():
        return pltpu.make_async_remote_copy(
            src_ref=edge_in.at[:, :, :, cut(quick)],
            dst_ref=near_edge.at[1 - quick],
            send_sem=halo_send,
            recv_sem=halo_recv,
            device_id=(next_to(quick), level),
            device_id_type=MESH,
        )

    def back_copy(side, count, part):
        first = 2 * frames + frames * side
        return pltpu.make_async_remote_copy(
            src_ref=total.at[pl.ds(first, count), part],
            dst_ref=back.at[1 - side, pl.ds(0, count), part],
            send_sem=back_send.at[side],
            recv_sem=back_recv.at[1 - side],
            device_id=(next_to(side), level),
            device_id_type=MESH,
        )

    def waiter(ref, send, recv):
        return pltpu.make_async_remote_copy(
            src_ref=ref, dst_ref=ref, send_sem=send, recv_sem=recv,
            device_id=(me, above), device_id_type=MESH,
        )

    def if_slow(act):
        pl.when(slow_here)(act)

    total[...] = jnp.zeros_like(total)
    columns = sum(here.astype(jnp.int32) for here in beside)
    others = sum(here.astype(jnp.int32) for here in slab_at)
    pl.semaphore_wait(barrier, others + columns * (1 + others))

    @if_slow
    def _():
        for j in range(SHARED):
            near_copy(slow, j).start()

    load.wait()

    for f in range(frames):
        first, last = [], []
        for c in range(2):
            wide = own16[c, f].astype(jnp.float32)
            first.append(wide[:HMAX])
            last.append(wide[depth - HMAX :])
        edge_out[0, f] = jnp.concatenate(first, axis=0).astype(jnp.bfloat16)
        edge_out[1, f] = jnp.concatenate(last, axis=0).astype(jnp.bfloat16)


    for way in range(2):

        @pl.when(slow_here & slab_at[way])
        def _(way=way):
            far_copy(way, 0).start()


    for way in range(2):

        @pl.when(slab_at[way])
        def _(way=way):
            edge_copy(way).start()

        @pl.when(jnp.logical_not(slab_at[way]))
        def _(way=way):
            edge_in[way] = jnp.zeros(edge_in.shape[1:], jnp.bfloat16)
            near_edge[slow, way] = jnp.zeros(near_edge.shape[2:], jnp.bfloat16)
            more_edge[way] = jnp.zeros(more_edge.shape[1:], jnp.bfloat16)

    @if_slow
    def _():
        for j in range(SHARED, frames):
            near_copy(slow, j).start()

    for way in range(2):

        @pl.when(slow_here & slab_at[way])
        def _(way=way):
            far_copy(way, 1).start()
            rest_copy(way).start()

    @if_slow
    def _():
        for j in range(SHARED):
            more_copy(j).start()

    for j in range(frames):
        near_copy(quick, j).start()

    for copy in small:
        copy.wait()
    for lag in range(LAGS):
        value = weights[lag].astype(jnp.float32)
        scaled[lag] = value
        scaled[LAGS + lag] = value * jnp.where(slow_here, 1.0, 0.0)
    sub = lax.broadcasted_iota(jnp.int32, (8, 4 * (depth + EDGE)), 0)
    column = lax.broadcasted_iota(jnp.int32, (8, 4 * (depth + EDGE)), 1)
    halo = lax.rem(column, EDGE)
    halo = jnp.where(halo < HMAX, halo - HMAX, halo - HMAX + depth)
    inside = column < 4 * depth
    place = jnp.where(inside, lax.rem(column, depth), halo)
    upper = column < jnp.where(inside, 2 * depth, 4 * depth + 2 * EDGE)
    reach = []
    for g in range(0, depth, 8):
        value = jnp.full(sub.shape, half[g], jnp.int32)
        for r in range(1, 8):
            value = jnp.where(sub == r, half[g + r], value)
        reach.append(value)
        keep = jnp.abs(place - (sub + g)) <= value
        band[g : g + 8] = jnp.where(keep & upper, 1.0, 0.0)
        band[depth + g : depth + g + 8] = jnp.where(keep & jnp.logical_not(upper), 1.0, 0.0)
    which = column // (2 * EDGE)
    for block in range(16):
        g = 0 if block % 2 == 0 else depth - 8
        keep = jnp.abs(halo - (sub + g)) <= reach[g // 8]
        edge_band[block * 8 : block * 8 + 8] = jnp.where(keep & (which == block // 2), 1.0, 0.0)
    window = band[...].astype(jnp.bfloat16)

    def own_field(f, carry):
        for c in range(2):
            wide = own16[c, f].astype(jnp.float32) * 0.5
            for s in range(2):
                field[2 * f + s, c] = wide[:, s * strip : (s + 1) * strip]
        return carry

    lax.fori_loop(0, frames, own_field, 0)
    back[slow, SHARED:] = jnp.zeros((frames - SHARED,) + back.shape[2:], jnp.float32)

    @pl.when(jnp.logical_not(slow_here))
    def _():
        back[slow, :SHARED] = jnp.zeros((SHARED,) + back.shape[2:], jnp.float32)

    low_factor = jnp.where(level > 0, 0.5, 0.0)
    high_factor = jnp.where(level < slabs - 1, 0.5, 0.0)

    def put_edges(slot, low, high):
        low = low.astype(jnp.float32) * low_factor
        high = high.astype(jnp.float32) * high_factor
        for c in range(2):
            edges[slot, c, 0:HMAX] = low[c * HMAX : (c + 1) * HMAX]
            edges[slot, c, HMAX:EDGE] = high[c * HMAX : (c + 1) * HMAX]

    def take_near(side, j):
        waiter(near16.at[side, j], near_send.at[side], near_recv.at[side, j]).wait_recv()
        for c in range(2):
            wide = near16[side, j, c].astype(jnp.float32) * 0.5
            field[2 * frames + frames * side + j, c] = wide

    def wait_ways(refs, send, recv):
        for way in range(2):

            @pl.when(slab_at[way])
            def _(way=way):
                waiter(refs.at[way], send.at[way], recv.at[way]).wait_recv()

    def sent_ways(refs, send):
        for way in range(2):

            @pl.when(slab_at[way])
            def _(way=way):
                waiter(refs.at[way], send.at[way], send.at[way]).wait_send()

    def wait_far(part):
        for way in range(2):

            @pl.when(slab_at[way])
            def _(way=way):
                ref = near_edge.at[slow, way, part_of(quick, part)]
                waiter(ref, far_send.at[part, way], far_recv.at[part, way]).wait_recv()

    def take_far(side, first, count):
        for j in range(first, first + count):
            frame = frame_at(1 - side, j)
            slot = 2 * frames + frames * side + j
            put_edges(slot, near_edge[side, 0, frame], near_edge[side, 1, frame])

    def take_more(j):
        waiter(more16.at[j], more_send, more_recv.at[j]).wait_recv()
        for c in range(2):
            field[4 * frames + j, c] = more16[j, c].astype(jnp.float32) * 0.5

    def take_rest():
        wait_ways(more_edge, rest_send, rest_recv)
        for j in range(SHARED):
            k = SHARED - 1 - j + slow * (2 * j - SHARED + 1)
            put_edges(4 * frames + j, more_edge[0, k], more_edge[1, k])

    def finish(place, part, y, x, weight):
        phase = signed_phase(y, x, weight)
        early, late = place
        first, second = total[early, part] + phase, total[late, part] + phase
        total[early, part] = first
        total[late, part] = second

    def inner_unit(n, q):
        c, s = q // 2, q % 2
        rows = ((0, 1 + c), (1, 2 + c) if c < 4 else (4, 5), (2, 3 + c) if c < 3 else (3, 1 + c))
        first, last = (
            jnp.where(n == 0, rows[0][i], jnp.where(n == 1, rows[1][i], rows[2][i])) for i in range(2)
        )
        return 2 * first + s, 2 * last + s, scaled[last - first - 1]

    def outer_unit(side, v, weight_at):
        j = sum(at_least(v, bound) for bound in (6, 11, 15, 18, 20))
        e = v - (6 * j - (j * (j - 1)) // 2)
        mine = 2 * frame_at(side, e) + 1 - side
        theirs = 2 * frames + frames * side + j
        early = theirs + side * (mine - theirs)
        late = mine + side * (theirs - mine)
        return early, late, scaled[weight_at + j + e]

    def middles(units, base):
        results = []
        for q in range(len(units) + 2):
            if q < len(units):
                early, late, _ = units[q]
                parts = split_products(
                    (field[early, 0], field[early, 1]), (field[late, 0], field[late, 1])
                )
                results.append(
                    jnp.dot(
                        window[:, : 4 * depth],
                        jnp.concatenate(parts, axis=0),
                        preferred_element_type=jnp.float32,
                    )
                )
            if q >= 2:
                early, late, weight = units[q - 2]
                real, imag = results[q - 2][:depth], results[q - 2][depth:]
                for c, value in enumerate((real, imag)):
                    held[base + q - 2, c, 0:HMAX] = value[:HMAX]
                    held[base + q - 2, c, HMAX:EDGE] = value[depth - HMAX :]
                for g in range(HMAX, depth - HMAX, 16):
                    finish(
                        (early, late), pl.ds(g, 16), imag[g : g + 16], real[g : g + 16], weight
                    )

    def rims(units, base):
        results = []
        for start in range(0, len(units), 4):
            group = units[start : start + 4]
            parts = []
            for early, late, _ in group:
                parts += split_products(
                    (edges[early, 0], edges[early, 1]), (edges[late, 0], edges[late, 1])
                )
            rows, columns = 2 * EDGE * len(group), 4 * EDGE * len(group)
            result = jnp.dot(
                edge_window[:rows, :columns],
                jnp.concatenate(parts, axis=0),
                preferred_element_type=jnp.float32,
            )
            results += [result[2 * EDGE * k : 2 * EDGE * (k + 1)] for k in range(len(group))]
        for q, (early, late, weight) in enumerate(units):
            real = results[q][:EDGE] + held[base + q, 0]
            imag = results[q][EDGE:] + held[base + q, 1]
            finish((early, late), pl.ds(0, HMAX), imag[:HMAX], real[:HMAX], weight)
            finish((early, late), pl.ds(depth - HMAX, HMAX), imag[HMAX:], real[HMAX:], weight)

    def inner_middles(n, carry):
        middles([inner_unit(n, q) for q in range(INNER)], n * INNER)
        return carry

    def inner_rims(n, carry):
        rims([inner_unit(n, q) for q in range(INNER)], n * INNER)
        return carry

    def quick_middles(n, carry):
        for at, js in ((0, (0, 1)), (1, (2,)), (2, (3, 4, 5))):

            @pl.when(n == at)
            def _(js=js):
                for j in js:
                    take_near(quick, j)

        middles([outer_unit(quick, n * QUICK + q, 0) for q in range(QUICK)], 3 * INNER + n * QUICK)
        return carry

    def quick_rims(n, carry):
        rims([outer_unit(quick, n * QUICK + q, 0) for q in range(QUICK)], 3 * INNER + n * QUICK)
        return carry

    def slow_unit(j, e):
        mine = 2 * frame_at(slow, e) + 1 - slow
        theirs = 2 * frames + frames * slow + j
        early = theirs + slow * (mine - theirs)
        late = mine + slow * (theirs - mine)
        return early, late, scaled[LAGS + j + e]

    def last_unit(n, q):
        def pick(values):
            value = values[3]
            for k in (2, 1, 0):
                value = jnp.where(n == k, values[k], value)
            return value

        j = pick(((3, 4, 0, 1), (3, 4, 0, 1), (3, 5, 0, 2))[q])
        e = pick(((0, 0, 3, 3), (1, 1, 4, 4), (2, 0, 5, 3))[q])
        own = jnp.where(n < 2, 1 - slow, slow)
        mine = 2 * frame_at(slow, e) + own
        theirs = j + jnp.where(n < 2, 2 * frames + frames * slow, 4 * frames)
        early = theirs + slow * (mine - theirs)
        late = mine + slow * (theirs - mine)
        return early, late, scaled[LAGS + j + e]

    def wholes(units):
        results = []
        for q in range(len(units) + 2):
            if q < len(units):
                early, late, _ = units[q]
                parts = split_products(
                    (field[early, 0], field[early, 1]), (field[late, 0], field[late, 1])
                ) + split_products(
                    (edges[early, 0], edges[early, 1]), (edges[late, 0], edges[late, 1])
                )
                results.append(
                    jnp.dot(
                        window, jnp.concatenate(parts, axis=0), preferred_element_type=jnp.float32
                    )
                )
            if q >= 2:
                early, late, weight = units[q - 2]
                real, imag = results[q - 2][:depth], results[q - 2][depth:]
                for g in range(0, depth, 24):
                    finish(
                        (early, late), pl.ds(g, 24), imag[g : g + 24], real[g : g + 24], weight
                    )

    def last_step(n, carry):
        @pl.when((n == 0) & slow_here)
        def _():
            wait_far(1)
            take_far(slow, SHARED, SHARED)
            take_near(slow, 3)

        @pl.when((n == 1) & slow_here)
        def _():
            take_near(slow, 4)
            take_near(slow, 5)

        @pl.when((n == 2) & slow_here)
        def _():
            take_rest()
            take_more(0)

        @pl.when((n == 3) & slow_here)
        def _():
            take_more(1)
            take_more(2)

        wholes([last_unit(n, q) for q in range(UNITS)])
        return carry

    @pl.when(jnp.logical_not(slow_here))
    def _():
        def clear(j, carry):
            slot = 2 * frames + frames * slow + j
            field[slot] = jnp.zeros(field.shape[1:], jnp.float32)
            edges[slot] = jnp.zeros(edges.shape[1:], jnp.float32)
            return carry

        lax.fori_loop(0, frames, clear, 0)
        for j in range(SHARED):
            field[4 * frames + j] = jnp.zeros(field.shape[1:], jnp.float32)
            edges[4 * frames + j] = jnp.zeros(edges.shape[1:], jnp.float32)

    lax.fori_loop(0, 3, inner_middles, 0)
    lax.fori_loop(0, 3, quick_middles, 0)

    shared = [[slow_unit(j, e) for e in range(frames - j)] for j in range(SHARED)]
    bases = [3 * (INNER + QUICK) + sum(map(len, shared[:j])) for j in range(SHARED)]
    for j, base in enumerate(bases):

        @if_slow
        def _(j=j):
            take_near(slow, j)

        middles(shared[j], base)

    @if_slow
    def _():
        back_copy(slow, SHARED, pl.ds(HMAX, depth - EDGE)).start()

    wait_ways(edge_in, edge_send, edge_recv)
    halo_copy().start()
    for f in range(frames):
        for s in range(2):
            lanes = pl.ds(s * strip, strip)
            put_edges(2 * f + s, edge_in[0, f, :, lanes], edge_in[1, f, :, lanes])

    edge_window = edge_band[...].astype(jnp.bfloat16)

    @if_slow
    def _():
        wait_far(0)
        take_far(slow, 0, SHARED)

    rims(sum(shared, []), bases[0])

    @if_slow
    def _():
        for at in (0, depth - HMAX):
            back_copy(slow, SHARED, pl.ds(at, HMAX)).start()

    waiter(near_edge.at[quick], halo_send, halo_recv).wait_recv()
    take_far(quick, 0, frames)
    lax.fori_loop(0, 3, quick_rims, 0)
    back_copy(quick, frames, pl.ds(0, depth)).start()
    lax.fori_loop(0, 3, inner_rims, 0)

    frame_total = frames * blocks

    def write(side):
        lanes = cut(side)

        def write_frame(f, carry):
            now = me * frames + f
            norm = jnp.float32(0.0)
            for lag in range(1, LAGS + 1):
                count = at_least(frame_total - 1, now + lag) + at_least(now, lag)
                norm = norm + scaled[lag - 1] * count.astype(jnp.float32)
            inverse = 1.0 / jnp.full((8, strip), norm, jnp.float32)
            j = frame_at(side, f)
            slot = 2 * f + side
            for g in range(0, depth, 8):
                part = pl.ds(g, 8)
                out[f, part, lanes] = (total[slot, part] + back[side, j, part]) * inverse
            return carry

        lax.fori_loop(0, frames, write_frame, 0)

    lax.fori_loop(0, 2, last_step, 0)
    waiter(back.at[quick], back_send.at[quick], back_recv.at[quick]).wait()
    write(quick)
    lax.fori_loop(2, 4, last_step, 0)

    @if_slow
    def _():
        waiter(back.at[slow, pl.ds(0, SHARED)], back_send.at[slow], back_recv.at[slow]).wait()

    write(slow)

    @if_slow
    def _():
        sent_ways(more_edge, rest_send)
        for part in range(2):
            sent_ways(near_edge.at[slow, :, part_of(slow, part)], far_send.at[part])
        waiter(more16, more_send, more_send).wait_send()
        waiter(near16.at[slow], near_send.at[slow], near_send.at[slow]).wait_send()

    sent_ways(edge_out, edge_send)
    waiter(near_edge.at[quick], halo_send, halo_send).wait_send()
    waiter(near16.at[quick], near_send.at[quick], near_send.at[quick]).wait_send()


def shards(iq, half, weights):
    _, frames, depth, lines = iq.shape
    strip = lines // 2
    slots = 4 * frames + SHARED
    wide, thin = jnp.float32, jnp.bfloat16
    dma = pltpu.SemaphoreType.DMA
    return pl.pallas_call(
        kernel,
        out_shape=pltpu.VMEM((frames, depth, lines), wide),
        in_specs=[pl.BlockSpec(memory_space=pltpu.HBM)] * 3,
        out_specs=pl.BlockSpec(memory_space=pltpu.VMEM),
        scratch_shapes=[
            pltpu.SMEM(half.shape, jnp.int32),
            pltpu.SMEM(weights.shape, jnp.int32),
            pltpu.SMEM((2 * LAGS,), wide),
            pltpu.VMEM((2, frames, depth, lines), thin),
            pltpu.VMEM((2, frames, EDGE, lines), thin),
            pltpu.VMEM((2, frames, EDGE, lines), thin),
            pltpu.VMEM((2, frames, 2, depth, strip), thin),
            pltpu.VMEM((2, 2, frames, EDGE, strip), thin),
            pltpu.VMEM((SHARED, 2, depth, strip), thin),
            pltpu.VMEM((2, SHARED, EDGE, strip), thin),
            pltpu.VMEM((slots, 2, depth, strip), wide),
            pltpu.VMEM((slots, 2, EDGE, strip), wide),
            pltpu.VMEM((slots, depth, strip), wide),
            pltpu.VMEM((3 * (INNER + QUICK) + SHARED_STRIPS, 2, EDGE, strip), wide),
            pltpu.VMEM((2 * depth, 4 * (depth + EDGE)), wide),
            pltpu.VMEM((8 * EDGE, 16 * EDGE), wide),
            pltpu.VMEM((2, frames, depth, strip), wide),
            dma(()),
            dma((2,)),
            dma((2,)),
            dma((2,)),
            dma((2,)),
            dma((2, frames)),
            dma((2, 2)),
            dma((2, 2)),
            dma(()),
            dma(()),
            dma(()),
            dma((SHARED,)),
            dma((2,)),
            dma((2,)),
            dma((2,)),
            dma((2,)),
        ],
        compiler_params=pltpu.CompilerParams(
            collective_id=0, has_side_effects=True, vmem_limit_bytes=48 * 1024 * 1024
        ),
        name="pair_phases",
    )(*(pltpu.with_memory_space_constraint(x, pltpu.HBM) for x in (iq, half, weights)))


def solution(mesh):
    placed = (P(None, "tm", "depth", None), P("depth"), P())
    return jax.shard_map(
        shards, mesh=mesh, in_specs=placed, out_specs=P("tm", "depth", None), check_vma=False
    )
```

```python
import functools

import jax
import jax.numpy as jnp
import numpy as np
from jax import lax
from jax.experimental import pallas as pl
from jax.experimental.pallas import tpu as pltpu
from jax.sharding import PartitionSpec as P

LAGS = 6
HMAX = 8
HALF_PI = float(np.float32(np.pi / 2))
PI = float(np.float32(np.pi))
TINY = 1.1754944e-38
ATAN = (
    0.9999960660934448,
    -0.33301785588264465,
    0.19582265615463257,
    -0.12176322191953659,
    0.05807745084166527,
    -0.0137208616361022,
)
MESH = pl.DeviceIdType.MESH
UNITS = 3
INNER = 10
QUICK = 7
EDGE = 2 * HMAX
SHARED = 3
SHARED_STRIPS = 15


def at_least(value, bound):
    return (value >= bound).astype(jnp.int32)


def signed_phase(y, x, weight):
    ax = jnp.abs(x)
    ay = jnp.abs(y)
    high = jnp.maximum(jnp.maximum(ax, ay), TINY)
    t = jnp.minimum(ax, ay) * pltpu.reciprocal(high, approx=True)
    s = t * t
    poly = ATAN[-1] * s + ATAN[-2]
    for coefficient in ATAN[-3::-1]:
        poly = poly * s + coefficient
    angle = poly * t
    angle = jnp.where(ay > ax, HALF_PI - angle, angle)
    angle = jnp.where(x < 0, PI - angle, angle)
    return angle * jnp.where(y < 0, -weight, weight)


def split_products(early, late):
    parts = []
    (ar, ai), (br, bi) = early, late
    for value in (br * ar + bi * ai, bi * ar - br * ai):
        high = value.astype(jnp.bfloat16)
        low = (value - high.astype(jnp.float32)).astype(jnp.bfloat16)
        parts += [high, low]
    return parts


def kernel(
    iq_any, half_any, weights_any, out,
    half, weights, scaled, own16, edge_out, edge_in, near16, near_edge, more16, more_edge,
    field, edges, total, held, band, edge_band, back,
    load_sem, small_sem, edge_send, edge_recv, near_send, near_recv, far_send, far_recv, halo_send, halo_recv,
    more_send, more_recv, rest_send, rest_recv, back_send, back_recv,
):
    frames, depth, lines = own16.shape[1:]
    strip = lines // 2
    me, level = lax.axis_index("tm"), lax.axis_index("depth")
    blocks, slabs = lax.axis_size("tm"), lax.axis_size("depth")
    left, right = lax.rem(me + blocks - 1, blocks), lax.rem(me + 1, blocks)
    below, above = lax.rem(level + slabs - 1, slabs), lax.rem(level + 1, slabs)
    slow = lax.rem(me, 2)
    quick = 1 - slow
    beside = (me > 0, me < blocks - 1)
    slab_at = (level > 0, level < slabs - 1)
    target = me - 1 + 2 * slow
    slow_here = (target >= 0) & (target < blocks)

    load = pltpu.make_async_copy(iq_any, own16, load_sem)
    load.start()
    small = [
        pltpu.make_async_copy(half_any, half, small_sem.at[0]),
        pltpu.make_async_copy(weights_any, weights, small_sem.at[1]),
    ]
    for copy in small:
        copy.start()
    barrier = pltpu.get_barrier_semaphore()
    for way, other in enumerate((below, above)):

        @pl.when(slab_at[way])
        def _(other=other):
            pl.semaphore_signal(barrier, inc=1, device_id=(me, other), device_id_type=MESH)

    for side, column in enumerate((left, right)):

        @pl.when(beside[side])
        def _(column=column):
            pl.semaphore_signal(barrier, inc=1, device_id=(column, level), device_id_type=MESH)

        for way, other in enumerate((below, above)):

            @pl.when(beside[side] & slab_at[way])
            def _(column=column, other=other):
                pl.semaphore_signal(barrier, inc=1, device_id=(column, other), device_id_type=MESH)

    def cut(side):
        return pl.ds(pl.multiple_of(side * strip, strip), strip)

    def next_to(side):
        return lax.rem(me + blocks - 1 + 2 * side, blocks)

    def frame_at(side, j):
        return j + side * (frames - 1 - 2 * j)

    def edge_copy(way):
        return pltpu.make_async_remote_copy(
            src_ref=edge_out.at[way],
            dst_ref=edge_in.at[1 - way],
            send_sem=edge_send.at[way],
            recv_sem=edge_recv.at[1 - way],
            device_id=(me, below if way == 0 else above),
            device_id_type=MESH,
        )

    def near_copy(side, j):
        return pltpu.make_async_remote_copy(
            src_ref=iq_any.at[:, frame_at(side, j), :, cut(side)],
            dst_ref=near16.at[1 - side, j],
            send_sem=near_send.at[side],
            recv_sem=near_recv.at[1 - side, j],
            device_id=(next_to(side), level),
            device_id_type=MESH,
        )

    def part_of(side, part):
        return pl.ds((side + part - 2 * side * part) * SHARED, SHARED)

    def far_copy(way, part):
        return pltpu.make_async_remote_copy(
            src_ref=edge_out.at[way, part_of(slow, part), :, cut(slow)],
            dst_ref=near_edge.at[1 - slow, 1 - way, part_of(slow, part)],
            send_sem=far_send.at[part, way],
            recv_sem=far_recv.at[part, 1 - way],
            device_id=(next_to(slow), below if way == 0 else above),
            device_id_type=MESH,
        )

    def more_copy(j):
        return pltpu.make_async_remote_copy(
            src_ref=own16.at[:, frame_at(slow, j), :, cut(quick)],
            dst_ref=more16.at[j],
            send_sem=more_send,
            recv_sem=more_recv.at[j],
            device_id=(next_to(slow), level),
            device_id_type=MESH,
        )

    def rest_copy(way):
        return pltpu.make_async_remote_copy(
            src_ref=edge_out.at[way, pl.ds(slow * (frames - SHARED), SHARED), :, cut(quick)],
            dst_ref=more_edge.at[1 - way],
            send_sem=rest_send.at[way],
            recv_sem=rest_recv.at[1 - way],
            device_id=(next_to(slow), below if way == 0 else above),
            device_id_type=MESH,
        )

    def halo_copy():
        return pltpu.make_async_remote_copy(
            src_ref=edge_in.at[:, :, :, cut(quick)],
            dst_ref=near_edge.at[1 - quick],
            send_sem=halo_send,
            recv_sem=halo_recv,
            device_id=(next_to(quick), level),
            device_id_type=MESH,
        )

    def back_copy(side, count, part):
        first = 2 * frames + frames * side
        return pltpu.make_async_remote_copy(
            src_ref=total.at[pl.ds(first, count), part],
            dst_ref=back.at[1 - side, pl.ds(0, count), part],
            send_sem=back_send.at[side],
            recv_sem=back_recv.at[1 - side],
            device_id=(next_to(side), level),
            device_id_type=MESH,
        )

    def waiter(ref, send, recv):
        return pltpu.make_async_remote_copy(
            src_ref=ref, dst_ref=ref, send_sem=send, recv_sem=recv,
            device_id=(me, above), device_id_type=MESH,
        )

    def if_slow(act):
        pl.when(slow_here)(act)

    total[...] = jnp.zeros_like(total)
    columns = sum(here.astype(jnp.int32) for here in beside)
    others = sum(here.astype(jnp.int32) for here in slab_at)
    pl.semaphore_wait(barrier, others + columns * (1 + others))

    @if_slow
    def _():
        for j in range(SHARED):
            near_copy(slow, j).start()

    load.wait()

    for f in range(frames):
        first, last = [], []
        for c in range(2):
            wide = own16[c, f].astype(jnp.float32)
            first.append(wide[:HMAX])
            last.append(wide[depth - HMAX :])
        edge_out[0, f] = jnp.concatenate(first, axis=0).astype(jnp.bfloat16)
        edge_out[1, f] = jnp.concatenate(last, axis=0).astype(jnp.bfloat16)


    for way in range(2):

        @pl.when(slow_here & slab_at[way])
        def _(way=way):
            far_copy(way, 0).start()


    for way in range(2):

        @pl.when(slab_at[way])
        def _(way=way):
            edge_copy(way).start()

        @pl.when(jnp.logical_not(slab_at[way]))
        def _(way=way):
            edge_in[way] = jnp.zeros(edge_in.shape[1:], jnp.bfloat16)
            near_edge[slow, way] = jnp.zeros(near_edge.shape[2:], jnp.bfloat16)
            more_edge[way] = jnp.zeros(more_edge.shape[1:], jnp.bfloat16)

    @if_slow
    def _():
        for j in range(SHARED, frames):
            near_copy(slow, j).start()

    for way in range(2):

        @pl.when(slow_here & slab_at[way])
        def _(way=way):
            far_copy(way, 1).start()
            rest_copy(way).start()

    @if_slow
    def _():
        for j in range(SHARED):
            more_copy(j).start()

    for j in range(frames):
        near_copy(quick, j).start()

    for copy in small:
        copy.wait()
    for lag in range(LAGS):
        value = weights[lag].astype(jnp.float32)
        scaled[lag] = value
        scaled[LAGS + lag] = value * jnp.where(slow_here, 1.0, 0.0)
    sub = lax.broadcasted_iota(jnp.int32, (8, 4 * (depth + EDGE)), 0)
    column = lax.broadcasted_iota(jnp.int32, (8, 4 * (depth + EDGE)), 1)
    halo = lax.rem(column, EDGE)
    halo = jnp.where(halo < HMAX, halo - HMAX, halo - HMAX + depth)
    inside = column < 4 * depth
    place = jnp.where(inside, lax.rem(column, depth), halo)
    upper = column < jnp.where(inside, 2 * depth, 4 * depth + 2 * EDGE)
    reach = []
    for g in range(0, depth, 8):
        value = jnp.full(sub.shape, half[g], jnp.int32)
        for r in range(1, 8):
            value = jnp.where(sub == r, half[g + r], value)
        reach.append(value)
        keep = jnp.abs(place - (sub + g)) <= value
        band[g : g + 8] = jnp.where(keep & upper, 1.0, 0.0)
        band[depth + g : depth + g + 8] = jnp.where(keep & jnp.logical_not(upper), 1.0, 0.0)
    which = column // (2 * EDGE)
    for block in range(16):
        g = 0 if block % 2 == 0 else depth - 8
        keep = jnp.abs(halo - (sub + g)) <= reach[g // 8]
        edge_band[block * 8 : block * 8 + 8] = jnp.where(keep & (which == block // 2), 1.0, 0.0)
    window = band[...].astype(jnp.bfloat16)

    def own_field(f, carry):
        for c in range(2):
            wide = own16[c, f].astype(jnp.float32) * 0.5
            for s in range(2):
                field[2 * f + s, c] = wide[:, s * strip : (s + 1) * strip]
        return carry

    lax.fori_loop(0, frames, own_field, 0)
    back[slow, SHARED:] = jnp.zeros((frames - SHARED,) + back.shape[2:], jnp.float32)

    @pl.when(jnp.logical_not(slow_here))
    def _():
        back[slow, :SHARED] = jnp.zeros((SHARED,) + back.shape[2:], jnp.float32)

    low_factor = jnp.where(level > 0, 0.5, 0.0)
    high_factor = jnp.where(level < slabs - 1, 0.5, 0.0)

    def put_edges(slot, low, high):
        low = low.astype(jnp.float32) * low_factor
        high = high.astype(jnp.float32) * high_factor
        for c in range(2):
            edges[slot, c, 0:HMAX] = low[c * HMAX : (c + 1) * HMAX]
            edges[slot, c, HMAX:EDGE] = high[c * HMAX : (c + 1) * HMAX]

    def take_near(side, j):
        waiter(near16.at[side, j], near_send.at[side], near_recv.at[side, j]).wait_recv()
        for c in range(2):
            wide = near16[side, j, c].astype(jnp.float32) * 0.5
            field[2 * frames + frames * side + j, c] = wide

    def wait_ways(refs, send, recv):
        for way in range(2):

            @pl.when(slab_at[way])
            def _(way=way):
                waiter(refs.at[way], send.at[way], recv.at[way]).wait_recv()

    def sent_ways(refs, send):
        for way in range(2):

            @pl.when(slab_at[way])
            def _(way=way):
                waiter(refs.at[way], send.at[way], send.at[way]).wait_send()

    def wait_far(part):
        for way in range(2):

            @pl.when(slab_at[way])
            def _(way=way):
                ref = near_edge.at[slow, way, part_of(quick, part)]
                waiter(ref, far_send.at[part, way], far_recv.at[part, way]).wait_recv()

    def take_far(side, first, count):
        for j in range(first, first + count):
            frame = frame_at(1 - side, j)
            slot = 2 * frames + frames * side + j
            put_edges(slot, near_edge[side, 0, frame], near_edge[side, 1, frame])

    def take_more(j):
        waiter(more16.at[j], more_send, more_recv.at[j]).wait_recv()
        for c in range(2):
            field[4 * frames + j, c] = more16[j, c].astype(jnp.float32) * 0.5

    def take_rest():
        wait_ways(more_edge, rest_send, rest_recv)
        for j in range(SHARED):
            k = SHARED - 1 - j + slow * (2 * j - SHARED + 1)
            put_edges(4 * frames + j, more_edge[0, k], more_edge[1, k])

    def finish(place, part, y, x, weight):
        phase = signed_phase(y, x, weight)
        early, late = place
        first, second = total[early, part] + phase, total[late, part] + phase
        total[early, part] = first
        total[late, part] = second

    def inner_unit(n, q):
        c, s = q // 2, q % 2
        rows = ((0, 1 + c), (1, 2 + c) if c < 4 else (4, 5), (2, 3 + c) if c < 3 else (3, 1 + c))
        first, last = (
            jnp.where(n == 0, rows[0][i], jnp.where(n == 1, rows[1][i], rows[2][i])) for i in range(2)
        )
        return 2 * first + s, 2 * last + s, scaled[last - first - 1]

    def outer_unit(side, v, weight_at):
        j = sum(at_least(v, bound) for bound in (6, 11, 15, 18, 20))
        e = v - (6 * j - (j * (j - 1)) // 2)
        mine = 2 * frame_at(side, e) + 1 - side
        theirs = 2 * frames + frames * side + j
        early = theirs + side * (mine - theirs)
        late = mine + side * (theirs - mine)
        return early, late, scaled[weight_at + j + e]

    def middles(units, base):
        results = []
        for q in range(len(units) + 2):
            if q < len(units):
                early, late, _ = units[q]
                parts = split_products(
                    (field[early, 0], field[early, 1]), (field[late, 0], field[late, 1])
                )
                results.append(
                    jnp.dot(
                        window[:, : 4 * depth],
                        jnp.concatenate(parts, axis=0),
                        preferred_element_type=jnp.float32,
                    )
                )
            if q >= 2:
                early, late, weight = units[q - 2]
                real, imag = results[q - 2][:depth], results[q - 2][depth:]
                for c, value in enumerate((real, imag)):
                    held[base + q - 2, c, 0:HMAX] = value[:HMAX]
                    held[base + q - 2, c, HMAX:EDGE] = value[depth - HMAX :]
                for g in range(HMAX, depth - HMAX, 16):
                    finish(
                        (early, late), pl.ds(g, 16), imag[g : g + 16], real[g : g + 16], weight
                    )

    def rims(units, base):
        results = []
        for start in range(0, len(units), 4):
            group = units[start : start + 4]
            parts = []
            for early, late, _ in group:
                parts += split_products(
                    (edges[early, 0], edges[early, 1]), (edges[late, 0], edges[late, 1])
                )
            rows, columns = 2 * EDGE * len(group), 4 * EDGE * len(group)
            result = jnp.dot(
                edge_window[:rows, :columns],
                jnp.concatenate(parts, axis=0),
                preferred_element_type=jnp.float32,
            )
            results += [result[2 * EDGE * k : 2 * EDGE * (k + 1)] for k in range(len(group))]
        for q, (early, late, weight) in enumerate(units):
            real = results[q][:EDGE] + held[base + q, 0]
            imag = results[q][EDGE:] + held[base + q, 1]
            finish((early, late), pl.ds(0, HMAX), imag[:HMAX], real[:HMAX], weight)
            finish((early, late), pl.ds(depth - HMAX, HMAX), imag[HMAX:], real[HMAX:], weight)

    def inner_middles(n, carry):
        middles([inner_unit(n, q) for q in range(INNER)], n * INNER)
        return carry

    def inner_rims(n, carry):
        rims([inner_unit(n, q) for q in range(INNER)], n * INNER)
        return carry

    def quick_middles(n, carry):
        for at, js in ((0, (0, 1)), (1, (2,)), (2, (3, 4, 5))):

            @pl.when(n == at)
            def _(js=js):
                for j in js:
                    take_near(quick, j)

        middles([outer_unit(quick, n * QUICK + q, 0) for q in range(QUICK)], 3 * INNER + n * QUICK)
        return carry

    def quick_rims(n, carry):
        rims([outer_unit(quick, n * QUICK + q, 0) for q in range(QUICK)], 3 * INNER + n * QUICK)
        return carry

    def slow_unit(j, e):
        mine = 2 * frame_at(slow, e) + 1 - slow
        theirs = 2 * frames + frames * slow + j
        early = theirs + slow * (mine - theirs)
        late = mine + slow * (theirs - mine)
        return early, late, scaled[LAGS + j + e]

    def last_unit(n, q):
        def pick(values):
            value = values[3]
            for k in (2, 1, 0):
                value = jnp.where(n == k, values[k], value)
            return value

        j = pick(((3, 4, 0, 1), (3, 4, 0, 1), (3, 5, 0, 2))[q])
        e = pick(((0, 0, 3, 3), (1, 1, 4, 4), (2, 0, 5, 3))[q])
        own = jnp.where(n < 2, 1 - slow, slow)
        mine = 2 * frame_at(slow, e) + own
        theirs = j + jnp.where(n < 2, 2 * frames + frames * slow, 4 * frames)
        early = theirs + slow * (mine - theirs)
        late = mine + slow * (theirs - mine)
        return early, late, scaled[LAGS + j + e]

    def wholes(units):
        results = []
        for q in range(len(units) + 2):
            if q < len(units):
                early, late, _ = units[q]
                parts = split_products(
                    (field[early, 0], field[early, 1]), (field[late, 0], field[late, 1])
                ) + split_products(
                    (edges[early, 0], edges[early, 1]), (edges[late, 0], edges[late, 1])
                )
                results.append(
                    jnp.dot(
                        window, jnp.concatenate(parts, axis=0), preferred_element_type=jnp.float32
                    )
                )
            if q >= 2:
                early, late, weight = units[q - 2]
                real, imag = results[q - 2][:depth], results[q - 2][depth:]
                for g in range(0, depth, 24):
                    finish(
                        (early, late), pl.ds(g, 24), imag[g : g + 24], real[g : g + 24], weight
                    )

    def last_step(n, carry):
        @pl.when((n == 0) & slow_here)
        def _():
            wait_far(1)
            take_far(slow, SHARED, SHARED)
            take_near(slow, 3)

        @pl.when((n == 1) & slow_here)
        def _():
            take_near(slow, 4)
            take_near(slow, 5)

        @pl.when((n == 2) & slow_here)
        def _():
            take_rest()
            take_more(0)

        @pl.when((n == 3) & slow_here)
        def _():
            take_more(1)
            take_more(2)

        wholes([last_unit(n, q) for q in range(UNITS)])
        return carry

    @pl.when(jnp.logical_not(slow_here))
    def _():
        def clear(j, carry):
            slot = 2 * frames + frames * slow + j
            field[slot] = jnp.zeros(field.shape[1:], jnp.float32)
            edges[slot] = jnp.zeros(edges.shape[1:], jnp.float32)
            return carry

        lax.fori_loop(0, frames, clear, 0)
        for j in range(SHARED):
            field[4 * frames + j] = jnp.zeros(field.shape[1:], jnp.float32)
            edges[4 * frames + j] = jnp.zeros(edges.shape[1:], jnp.float32)

    lax.fori_loop(0, 3, inner_middles, 0)
    lax.fori_loop(0, 3, quick_middles, 0)

    shared = [[slow_unit(j, e) for e in range(frames - j)] for j in range(SHARED)]
    bases = [3 * (INNER + QUICK) + sum(map(len, shared[:j])) for j in range(SHARED)]
    for j, base in enumerate(bases):

        @if_slow
        def _(j=j):
            take_near(slow, j)

        middles(shared[j], base)

    @if_slow
    def _():
        back_copy(slow, SHARED, pl.ds(HMAX, depth - EDGE)).start()

    wait_ways(edge_in, edge_send, edge_recv)
    halo_copy().start()
    for f in range(frames):
        for s in range(2):
            lanes = pl.ds(s * strip, strip)
            put_edges(2 * f + s, edge_in[0, f, :, lanes], edge_in[1, f, :, lanes])

    edge_window = edge_band[...].astype(jnp.bfloat16)

    @if_slow
    def _():
        wait_far(0)
        take_far(slow, 0, SHARED)

    for j, base in enumerate(bases):
        rims(shared[j], base)

    @if_slow
    def _():
        for at in (0, depth - HMAX):
            back_copy(slow, SHARED, pl.ds(at, HMAX)).start()

    waiter(near_edge.at[quick], halo_send, halo_recv).wait_recv()
    take_far(quick, 0, frames)
    lax.fori_loop(0, 3, quick_rims, 0)
    back_copy(quick, frames, pl.ds(0, depth)).start()
    lax.fori_loop(0, 3, inner_rims, 0)

    frame_total = frames * blocks

    def write(side):
        lanes = cut(side)

        def write_frame(f, carry):
            now = me * frames + f
            norm = jnp.float32(0.0)
            for lag in range(1, LAGS + 1):
                count = at_least(frame_total - 1, now + lag) + at_least(now, lag)
                norm = norm + scaled[lag - 1] * count.astype(jnp.float32)
            inverse = 1.0 / jnp.full((8, strip), norm, jnp.float32)
            j = frame_at(side, f)
            slot = 2 * f + side
            for g in range(0, depth, 8):
                part = pl.ds(g, 8)
                out[f, part, lanes] = (total[slot, part] + back[side, j, part]) * inverse
            return carry

        for f in range(frames):
            write_frame(f, 0)

    lax.fori_loop(0, 2, last_step, 0)
    waiter(back.at[quick], back_send.at[quick], back_recv.at[quick]).wait()
    write(quick)
    lax.fori_loop(2, 4, last_step, 0)

    @if_slow
    def _():
        waiter(back.at[slow, pl.ds(0, SHARED)], back_send.at[slow], back_recv.at[slow]).wait()

    write(slow)

    @if_slow
    def _():
        sent_ways(more_edge, rest_send)
        for part in range(2):
            sent_ways(near_edge.at[slow, :, part_of(slow, part)], far_send.at[part])
        waiter(more16, more_send, more_send).wait_send()
        waiter(near16.at[slow], near_send.at[slow], near_send.at[slow]).wait_send()

    sent_ways(edge_out, edge_send)
    waiter(near_edge.at[quick], halo_send, halo_send).wait_send()
    waiter(near16.at[quick], near_send.at[quick], near_send.at[quick]).wait_send()


def shards(iq, half, weights):
    _, frames, depth, lines = iq.shape
    strip = lines // 2
    slots = 4 * frames + SHARED
    wide, thin = jnp.float32, jnp.bfloat16
    dma = pltpu.SemaphoreType.DMA
    return pl.pallas_call(
        kernel,
        out_shape=pltpu.VMEM((frames, depth, lines), wide),
        in_specs=[pl.BlockSpec(memory_space=pltpu.HBM)] * 3,
        out_specs=pl.BlockSpec(memory_space=pltpu.VMEM),
        scratch_shapes=[
            pltpu.SMEM(half.shape, jnp.int32),
            pltpu.SMEM(weights.shape, jnp.int32),
            pltpu.SMEM((2 * LAGS,), wide),
            pltpu.VMEM((2, frames, depth, lines), thin),
            pltpu.VMEM((2, frames, EDGE, lines), thin),
            pltpu.VMEM((2, frames, EDGE, lines), thin),
            pltpu.VMEM((2, frames, 2, depth, strip), thin),
            pltpu.VMEM((2, 2, frames, EDGE, strip), thin),
            pltpu.VMEM((SHARED, 2, depth, strip), thin),
            pltpu.VMEM((2, SHARED, EDGE, strip), thin),
            pltpu.VMEM((slots, 2, depth, strip), wide),
            pltpu.VMEM((slots, 2, EDGE, strip), wide),
            pltpu.VMEM((slots, depth, strip), wide),
            pltpu.VMEM((3 * (INNER + QUICK) + SHARED_STRIPS, 2, EDGE, strip), wide),
            pltpu.VMEM((2 * depth, 4 * (depth + EDGE)), wide),
            pltpu.VMEM((8 * EDGE, 16 * EDGE), wide),
            pltpu.VMEM((2, frames, depth, strip), wide),
            dma(()),
            dma((2,)),
            dma((2,)),
            dma((2,)),
            dma((2,)),
            dma((2, frames)),
            dma((2, 2)),
            dma((2, 2)),
            dma(()),
            dma(()),
            dma(()),
            dma((SHARED,)),
            dma((2,)),
            dma((2,)),
            dma((2,)),
            dma((2,)),
        ],
        compiler_params=pltpu.CompilerParams(
            collective_id=0, has_side_effects=True, vmem_limit_bytes=48 * 1024 * 1024
        ),
        name="pair_phases",
    )(*(pltpu.with_memory_space_constraint(x, pltpu.HBM) for x in (iq, half, weights)))


def solution(mesh):
    placed = (P(None, "tm", "depth", None), P("depth"), P())
    return jax.shard_map(
        shards, mesh=mesh, in_specs=placed, out_specs=P("tm", "depth", None), check_vma=False
    )
```
